32 devices in a mesh: dp: 4 (over z), fsdp: 8 (over y, x, core).
Axes of the slice: x: 2, y: 2, z: 4, core: 2. Of those that a mesh axis runs over, the one named last changes fastest.
Arguments:
- words_in: bfloat16 [384, 20, 768], P(('dp', 'fsdp')), may hold values from -6 to 6
- regions_in: bfloat16 [384, 36, 768], P(('dp', 'fsdp')), may hold values from -6 to 6
- word_mask: int32 [384, 20], P(('dp', 'fsdp')), may hold values from 0 to 1, as said below
- region_count: int32 [384], P(('dp', 'fsdp')), may hold values from 10 to 36, as said below
- cross_matrices: bfloat16 [4, 768, 768], P(None, 'fsdp'), may hold values from -0.3125 to 0.3125
- cross_vectors: bfloat16 [5, 768], P(None, 'fsdp'), may hold values from -1.5 to 1.5
- word_self_matrices: bfloat16 [4, 768, 768], P(None, 'fsdp'), may hold values from -0.3125 to 0.3125
- word_self_vectors: bfloat16 [5, 768], P(None, 'fsdp'), may hold values from -1.5 to 1.5
- region_self_matrices: bfloat16 [4, 768, 768], P(None, 'fsdp'), may hold values from -0.3125 to 0.3125
- region_self_vectors: bfloat16 [5, 768], P(None, 'fsdp'), may hold values from -1.5 to 1.5
- word_feed_matrices: bfloat16 [2, 768, 3072], P(None, 'fsdp'), may hold values from -0.21875 to 0.21875
- word_feed_vectors: bfloat16 [7, 768], P(None, 'fsdp'), may hold values from -1.5 to 1.5
- region_feed_matrices: bfloat16 [2, 768, 3072], P(None, 'fsdp'), may hold values from -0.21875 to 0.21875
- region_feed_vectors: bfloat16 [7, 768], P(None, 'fsdp'), may hold values from -1.5 to 1.5
- words_cotangent: bfloat16 [384, 20, 768], P(('dp', 'fsdp')), may hold values from -6 to 6
- regions_cotangent: bfloat16 [384, 36, 768], P(('dp', 'fsdp')), may hold values from -6 to 6
Outputs:
- words_out: bfloat16 [384, 20, 768], P(('dp', 'fsdp'))
- regions_out: bfloat16 [384, 36, 768], P(('dp', 'fsdp'))
- words_grad: bfloat16 [384, 20, 768], P(('dp', 'fsdp'))
- regions_grad: bfloat16 [384, 36, 768], P(('dp', 'fsdp'))
- grad_cross_matrices: float32 [4, 768, 768], P(None, 'fsdp')
- grad_cross_vectors: float32 [5, 768], P(None, 'fsdp')
- grad_word_self_matrices: float32 [4, 768, 768], P(None, 'fsdp')
- grad_word_self_vectors: float32 [5, 768], P(None, 'fsdp')
- grad_region_self_matrices: float32 [4, 768, 768], P(None, 'fsdp')
- grad_region_self_vectors: float32 [5, 768], P(None, 'fsdp')
- grad_word_feed_matrices: float32 [2, 768, 3072], P(None, 'fsdp')
- grad_word_feed_vectors: float32 [7, 768], P(None, 'fsdp')
- grad_region_feed_matrices: float32 [2, 768, 3072], P(None, 'fsdp')
- grad_region_feed_vectors: float32 [7, 768], P(None, 'fsdp')
The draws below stay inside these ranges and needn't reach their ends.
Inputs may be any that keep to these rules, and one draw needn't show every extreme that they name: `word_mask`: position 0 of every item is 1. `region_count`: some item has exactly 36 regions.
All inputs are finite; a program needn't handle non-finite values.
Results may differ from the reference program's by a relative error of at most 0.024.
Values may be sent and summed in bfloat16 or wider, within the bound.
No kernel may reach another device: no remote copies, remote signals or barrier semaphores. Data moves between devices by JAX's collectives and lax.ppermute only.
A program may use at most 320 MiB of HBM per device.

```python
import math
import jax
import jax.numpy as jnp
from jax import lax

D = 768
FF = 3072
HEADS = 12
WORDS = 20
REGIONS = 36
REGIONS_MIN = 10
ITEMS = 384


def vector_rows(key, count, gain_row):
    values = jnp.clip(0.3 * jax.random.normal(key, (count, D), jnp.float32), -1.5, 1.5)
    gains = jax.random.uniform(jax.random.fold_in(key, 1), (count, D), jnp.float32, 0.6, 1.4)
    is_gain = (jnp.arange(count) == gain_row)[:, None]
    return jnp.where(is_gain, gains, values).astype(jnp.bfloat16)


def draw_word_mask(key, part):
    key = jax.random.fold_in(key, 5)
    picks = jax.random.randint(key, (ITEMS, WORDS), 0, 4)
    first = (jnp.arange(WORDS) == 0)[None, :]
    return jnp.where(first | (picks != 0), 1, 0).astype(jnp.int32)


def draw_region_count(key, part):
    key = jax.random.fold_in(key, 7)
    first_key, second_key, chosen_key = jax.random.split(key, 3)
    span = REGIONS - REGIONS_MIN + 1
    smaller = jnp.minimum(jax.random.randint(first_key, (ITEMS,), 0, span), jax.random.randint(second_key, (ITEMS,), 0, span))
    chosen = jax.random.randint(chosen_key, (), 0, ITEMS)
    return jnp.where(jnp.arange(ITEMS) == chosen, REGIONS, REGIONS_MIN + smaller).astype(jnp.int32)


def draw_cross_vectors(key, part):
    key = jax.random.fold_in(key, 11)
    return vector_rows(key, 5, 3)


def draw_word_self_vectors(key, part):
    key = jax.random.fold_in(key, 13)
    return vector_rows(key, 5, 3)


def draw_region_self_vectors(key, part):
    key = jax.random.fold_in(key, 17)
    return vector_rows(key, 5, 3)


def draw_word_feed_vectors(key, part):
    key = jax.random.fold_in(key, 19)
    return vector_rows(key, 7, 5)


def draw_region_feed_vectors(key, part):
    key = jax.random.fold_in(key, 23)
    return vector_rows(key, 7, 5)


def level_of(rng, shape, pieces, smallest, high):
    def one(dim, shards_of):
        steps = jax.random.uniform(jax.random.fold_in(jax.random.fold_in(rng, 6), dim), (shards_of,), jnp.float32, smallest / len(pieces), high / len(pieces))
        return jnp.repeat(jnp.exp(steps), shape[dim] // shards_of).reshape((-1,) + (1,) * (len(shape) - dim - 1))

    level = one(*pieces[0])
    for cut in pieces[1:]:
        level = level * one(*cut)
    return level


def normal_values(rng, dims, scale, reach, cuts=(), kind=jnp.bfloat16):
    array = jax.random.normal(rng, dims, jnp.float32) * scale
    if len(cuts) > 0:
        array = level_of(rng, dims, cuts, -0.22, 0.18) * array
    return jnp.clip(array, min=-reach, max=reach).astype(kind)


def setup_inputs(seed: int = 0) -> dict:
    splits = jax.random.split(jax.random.key(seed), 17)
    words_in = normal_values(splits[0], (ITEMS, WORDS, D), 1.0, 6.0, ((0, 32),))
    regions_in = normal_values(splits[1], (ITEMS, REGIONS, D), 1.0, 6.0, ((0, 32),))
    word_mask = draw_word_mask(jax.random.fold_in(splits[16], 71), 0)
    region_count = draw_region_count(jax.random.fold_in(splits[16], 71), 0)
    cross_matrices = normal_values(splits[4], (4, D, D), (D // 2) ** -0.5, 0.3125, ((1, 8),))
    cross_vectors = draw_cross_vectors(jax.random.fold_in(splits[16], 71), 0)
    word_self_matrices = normal_values(splits[6], (4, D, D), (D // 2) ** -0.5, 0.3125, ((1, 8),))
    word_self_vectors = draw_word_self_vectors(jax.random.fold_in(splits[16], 71), 0)
    region_self_matrices = normal_values(splits[8], (4, D, D), (D // 2) ** -0.5, 0.3125, ((1, 8),))
    region_self_vectors = draw_region_self_vectors(jax.random.fold_in(splits[16], 71), 0)
    word_feed_matrices = normal_values(splits[10], (2, D, FF), D ** -0.5, 0.21875, ((1, 8),))
    word_feed_vectors = draw_word_feed_vectors(jax.random.fold_in(splits[16], 71), 0)
    region_feed_matrices = normal_values(splits[12], (2, D, FF), D ** -0.5, 0.21875, ((1, 8),))
    region_feed_vectors = draw_region_feed_vectors(jax.random.fold_in(splits[16], 71), 0)
    words_cotangent = normal_values(splits[14], (ITEMS, WORDS, D), 1.0, 6.0, ((0, 32),))
    regions_cotangent = normal_values(splits[15], (ITEMS, REGIONS, D), 1.0, 6.0, ((0, 32),))
    return {"words_in": words_in, "regions_in": regions_in, "word_mask": word_mask, "region_count": region_count, "cross_matrices": cross_matrices, "cross_vectors": cross_vectors, "word_self_matrices": word_self_matrices, "word_self_vectors": word_self_vectors, "region_self_matrices": region_self_matrices, "region_self_vectors": region_self_vectors, "word_feed_matrices": word_feed_matrices, "word_feed_vectors": word_feed_vectors, "region_feed_matrices": region_feed_matrices, "region_feed_vectors": region_feed_vectors, "words_cotangent": words_cotangent, "regions_cotangent": regions_cotangent}


highest = lax.Precision.HIGHEST
epsilon = 1e-12

@jax.custom_vjp
def low(v):
    return lax.optimization_barrier(v.astype(jnp.bfloat16)).astype(jnp.float32)

@jax.custom_vjp
def low_back(v):
    return v

def low_keep(v):
    return (low(v), None)

def low_pass(kept, grad):
    return (grad,)

def back_keep(v):
    return (v, None)

def back_low(kept, grad):
    return (low(grad),)
low.defvjp(low_keep, low_pass)
low_back.defvjp(back_keep, back_low)

def both_round(value):
    return low(low_back(value))

def normalize(total, gain, shift):
    centred = total - lax.optimization_barrier(jnp.mean(total, axis=-1, keepdims=True))
    spread = lax.optimization_barrier(jnp.mean(centred * centred, axis=-1, keepdims=True))
    return centred * lax.rsqrt(spread + epsilon) * gain + shift

def matmul(left, right):
    return jnp.einsum('gnd,de->gne', left, right, precision=highest)

def attend(query_side, context_side, key_bias, matrices, vectors):
    groups, query_len, width = query_side.shape
    size = width // HEADS
    queries = both_round(matmul(query_side, matrices[0]) + vectors[0])
    keys_all = both_round(matmul(context_side, matrices[1]))
    values_all = both_round(matmul(context_side, matrices[2]) + vectors[1])
    query_heads = queries.reshape(groups, query_len, HEADS, size)
    key_heads = keys_all.reshape(groups, -1, HEADS, size)
    value_heads = values_all.reshape(groups, -1, HEADS, size)
    scores = jnp.einsum('gqhe,gkhe->ghqk', query_heads, key_heads, precision=highest) / math.sqrt(size)
    scores = low_back(scores + key_bias[:, None, None, :])
    probs = low(jax.nn.softmax(scores, axis=-1))
    mixed = jnp.einsum('ghqk,gkhe->gqhe', probs, value_heads, precision=highest)
    context = both_round(mixed.reshape(groups, query_len, width))
    return low_back(matmul(context, matrices[3]) + vectors[2])

def feed(side, matrices, vectors):
    hidden_pre = low_back(matmul(side, matrices[0]) + vectors[0:4].reshape(-1))
    hidden = low(jax.nn.gelu(hidden_pre, approximate=False))
    return low_back(jnp.einsum('gnf,df->gnd', hidden, matrices[1], precision=highest) + vectors[4])

def layer(words, regions, word_bias, region_bias, params):
    cross_m, cross_v, wself_m, wself_v, rself_m, rself_v, wfeed_m, wfeed_v, rfeed_m, rfeed_v = params
    words_low = low(words)
    regions_low = low(regions)
    word_cross = normalize(words + attend(words_low, regions_low, region_bias, cross_m, cross_v), cross_v[3], cross_v[4])
    region_cross = normalize(regions + attend(regions_low, words_low, word_bias, cross_m, cross_v), cross_v[3], cross_v[4])
    word_cross_low = low(word_cross)
    region_cross_low = low(region_cross)
    word_self = normalize(word_cross + attend(word_cross_low, word_cross_low, word_bias, wself_m, wself_v), wself_v[3], wself_v[4])
    region_self = normalize(region_cross + attend(region_cross_low, region_cross_low, region_bias, rself_m, rself_v), rself_v[3], rself_v[4])
    word_out = normalize(word_self + feed(low(word_self), wfeed_m, wfeed_v), wfeed_v[5], wfeed_v[6])
    region_out = normalize(region_self + feed(low(region_self), rfeed_m, rfeed_v), rfeed_v[5], rfeed_v[6])
    return (word_out, region_out)

def reference(words_in, regions_in, word_mask, region_count, cross_matrices, cross_vectors, word_self_matrices, word_self_vectors, region_self_matrices, region_self_vectors, word_feed_matrices, word_feed_vectors, region_feed_matrices, region_feed_vectors, words_cotangent, regions_cotangent):
    group = math.gcd(ITEMS, 64)
    blocks = ITEMS // group
    word_bias = (word_mask.astype(jnp.float32) - 1.0) * 10000.0
    slots = jnp.arange(REGIONS, dtype=jnp.int32)
    region_bias = jnp.where(slots[None, :] < region_count[:, None], 0.0, -10000.0).astype(jnp.float32)
    params = tuple((weight.astype(jnp.float32) for weight in (cross_matrices, cross_vectors, word_self_matrices, word_self_vectors, region_self_matrices, region_self_vectors, word_feed_matrices, word_feed_vectors, region_feed_matrices, region_feed_vectors)))

    def whole(words, regions, weights):

        def one_group(block):
            return layer(block[0], block[1], block[2], block[3], weights)
        outputs = lax.map(jax.checkpoint(one_group), (words.reshape(blocks, group, WORDS, D), regions.reshape(blocks, group, REGIONS, D), word_bias.reshape(blocks, group, WORDS), region_bias.reshape(blocks, group, REGIONS)))
        return (outputs[0].reshape(ITEMS, WORDS, D), outputs[1].reshape(ITEMS, REGIONS, D))
    outputs, pull = jax.vjp(whole, words_in.astype(jnp.float32), regions_in.astype(jnp.float32), params)
    grad_words, grad_regions, grad_params = pull((words_cotangent.astype(jnp.float32), regions_cotangent.astype(jnp.float32)))
    return (outputs[0].astype(jnp.bfloat16), outputs[1].astype(jnp.bfloat16), grad_words.astype(jnp.bfloat16), grad_regions.astype(jnp.bfloat16), grad_params[0], grad_params[1], grad_params[2], grad_params[3], grad_params[4], grad_params[5], grad_params[6], grad_params[7], grad_params[8], grad_params[9])
```

```python
from functools import partial

import jax
import jax.numpy as jnp
from jax import lax
from jax.sharding import PartitionSpec as P
from jax.experimental import pallas as pl
from jax.experimental.pallas import tpu as pltpu

HEADS = 12
epsilon = 1e-12
negative = -10000.0
bf16 = jnp.bfloat16
f32 = jnp.float32

CROSS, WORD_SELF, REGION_SELF, WORD_FEED, REGION_FEED = 0, 5, 10, 15, 22
VECTOR_ROWS = 32


def nn(left, right):
    return jnp.dot(left, right, preferred_element_type=f32)


def nt(left, right):
    return lax.dot_general(left, right, (((1,), (1,)), ((), ())), preferred_element_type=f32)


def tn(left, right):
    return lax.dot_general(left, right, (((0,), (0,)), ((), ())), preferred_element_type=f32)


def norm_parts(total):
    centred = total - jnp.mean(total, axis=-1, keepdims=True)
    spread = jnp.mean(centred * centred, axis=-1, keepdims=True)
    rate = lax.rsqrt(spread + epsilon)
    return centred * rate, rate


def norm_back(grad, unit, rate, gain):
    scaled = grad * gain
    mean_one = jnp.mean(scaled, axis=-1, keepdims=True)
    mean_two = jnp.mean(scaled * unit, axis=-1, keepdims=True)
    return (
        rate * (scaled - mean_one - unit * mean_two),
        jnp.sum(grad * unit, axis=0, keepdims=True),
        jnp.sum(grad, axis=0, keepdims=True),
    )


def half_masks(rows):
    lane = lax.broadcasted_iota(jnp.int32, (rows, 128), 1)
    return (lane < 64, lane >= 64)


def heads_forward(q_ref, k_ref, v_ref, bias_ref, probs_ref, ctx_ref):
    blocks, qb, kb = bias_ref.shape
    pairs = q_ref.shape[1] // 128
    masks = half_masks(kb)
    zero = jnp.zeros((kb, 128), bf16)

    def block(b, carry):
        rq = pl.ds(pl.multiple_of(b * qb, 16), qb)
        rk = pl.ds(pl.multiple_of(b * kb, 16), kb)
        bias = bias_ref[b]
        for p in range(pairs):
            cols = pl.ds(p * 128, 128)
            qp = q_ref[rq, cols]
            kp = k_ref[rk, cols]
            vp = v_ref[rk, cols]
            mixed = None
            for half in range(2):
                s = nt(qp, jnp.where(masks[half], kp, zero)) * 0.125 + bias
                e = jnp.exp(s - jnp.max(s, axis=-1, keepdims=True))
                low = (e / jnp.sum(e, axis=-1, keepdims=True)).astype(bf16)
                probs_ref[b * (2 * pairs) + 2 * p + half] = low
                part = nn(low, jnp.where(masks[half], vp, zero))
                mixed = part if mixed is None else mixed + part
            ctx_ref[rq, cols] = mixed.astype(bf16)
        return carry

    lax.fori_loop(0, blocks, block, 0)


def heads_backward(q_ref, k_ref, v_ref, probs_ref, dctx_ref, dq_ref, dk_ref, dv_ref, blocks):
    qb = q_ref.shape[0] // blocks
    kb = k_ref.shape[0] // blocks
    pairs = q_ref.shape[1] // 128
    kmasks, qmasks = half_masks(kb), half_masks(qb)
    kzero, qzero = jnp.zeros((kb, 128), bf16), jnp.zeros((qb, 128), bf16)

    def block(b, carry):
        rq = pl.ds(pl.multiple_of(b * qb, 16), qb)
        rk = pl.ds(pl.multiple_of(b * kb, 16), kb)
        for p in range(pairs):
            cols = pl.ds(p * 128, 128)
            qp = q_ref[rq, cols]
            kp = k_ref[rk, cols]
            vp = v_ref[rk, cols]
            dc = dctx_ref[rq, cols]
            dq = dk = dv = 0.0
            for half in range(2):
                low = probs_ref[b * (2 * pairs) + 2 * p + half]
                probs = low.astype(f32)
                dp = nt(dc, jnp.where(kmasks[half], vp, kzero))
                dv = dv + tn(low, jnp.where(qmasks[half], dc, qzero))
                t = probs * dp
                ds = (t - probs * jnp.sum(t, axis=-1, keepdims=True)).astype(bf16)
                dq = dq + nn(ds, jnp.where(kmasks[half], kp, kzero))
                dk = dk + tn(ds, jnp.where(qmasks[half], qp, qzero))
            dq_ref[rq, cols] = (dq * 0.125).astype(bf16)
            dk_ref[rk, cols] = (dk * 0.125).astype(bf16)
            dv_ref[rk, cols] = dv.astype(bf16)
        return carry

    lax.fori_loop(0, blocks, block, 0)


def vec(vec_ref, row):
    return vec_ref[row : row + 1, :]


def attend(x_low, c_low, base, w_ref, vec_ref, row, bias_ref, q_ref, k_ref, v_ref, probs_ref, ctx_ref):
    q_ref[...] = (nn(x_low, w_ref[0]) + vec(vec_ref, row)).astype(bf16)
    k_ref[...] = nn(c_low, w_ref[1]).astype(bf16)
    v_ref[...] = (nn(c_low, w_ref[2]) + vec(vec_ref, row + 1)).astype(bf16)
    heads_forward(q_ref, k_ref, v_ref, bias_ref, probs_ref, ctx_ref)
    return base + nn(ctx_ref[...], w_ref[3]) + vec(vec_ref, row + 2)


def cross_forward_kernel(
    words_ref, regions_ref, w_ref, vec_ref, wr_ref, rw_ref,
    wtot_ref, rtot_ref, wq_ref, wk_ref, wv_ref, wp_ref, wc_ref, rq_ref, rk_ref, rv_ref, rp_ref, rc_ref,
):
    words, regions = words_ref[...], regions_ref[...]
    wtot_ref[...] = attend(words, regions, words.astype(f32), w_ref, vec_ref, CROSS, wr_ref, wq_ref, wk_ref, wv_ref, wp_ref, wc_ref)
    rtot_ref[...] = attend(regions, words, regions.astype(f32), w_ref, vec_ref, CROSS, rw_ref, rq_ref, rk_ref, rv_ref, rp_ref, rc_ref)


def self_forward_kernel(row, tot_ref, w_ref, vec_ref, bias_ref, out_ref, q_ref, k_ref, v_ref, p_ref, c_ref):
    unit, _ = norm_parts(tot_ref[...])
    y = unit * vec(vec_ref, CROSS + 3) + vec(vec_ref, CROSS + 4)
    low = y.astype(bf16)
    out_ref[...] = attend(low, low, y, w_ref, vec_ref, row, bias_ref, q_ref, k_ref, v_ref, p_ref, c_ref)


def gelu_parts(x):
    size = jnp.abs(x)
    e = jnp.exp(x * x * -0.5)
    t = 1.0 / (1.0 + (0.3275911 * 0.7071067811865476) * size)
    poly = t * (0.127414796 + t * (-0.142248368 + t * (0.7107068705 + t * (-0.7265760135 + t * 0.5307027145))))
    tail = poly * e
    phi = jnp.where(x >= 0, 1.0 - tail, tail)
    return x * phi, phi + x * e * 0.3989422804014327


def slot_of(s, me, order):
    k = s ^ me
    slot = 0
    for bit in order:
        slot = slot * 2 + ((k >> bit) & 1)
    return slot


def place(dest_ref, value, me, order):
    if order is None:
        dest_ref[...] = value
        return
    rows = value.shape[0] // SLOTS
    for s in range(SLOTS):
        slot = slot_of(s, me, order)
        dest_ref[pl.ds(pl.multiple_of(slot * rows, 16), rows), :] = value[s * rows : (s + 1) * rows, :]


SLOTS = 8


def put(keep_ref, send_ref, base, stride, cols, value):
    rows = value.shape[0] // SLOTS
    low = value.astype(bf16)
    for j in range(SLOTS):
        dest = keep_ref if j < SLOTS // 2 else send_ref
        start = base + (j % (SLOTS // 2)) * stride
        dest[start : start + rows, cols] = low[j * rows : (j + 1) * rows]


def feed_kernel(
    self_row, row, chunk, orders,
    me_ref, tot_ref, cot_ref, m_ref, vec_ref,
    out_ref, dtot_ref, keep_ref, send_ref, dvec_ref,
    x_ref, y_ref, h_ref, gp_ref, dpre_ref, dy_ref, xt_ref, dyt_ref, acc_ref, bup_ref, dbup_ref,
):
    me = me_ref[0]
    width = tot_ref.shape[1]
    hidden = m_ref.shape[2]
    parts = hidden // width
    block = width // SLOTS
    for i in range(parts):
        bup_ref[:, i * width : (i + 1) * width] = vec(vec_ref, row + i)
    unit2, rate2 = norm_parts(tot_ref[...])
    y = unit2 * vec(vec_ref, self_row + 3) + vec(vec_ref, self_row + 4)
    y_ref[...] = y
    x_ref[...] = y.astype(bf16)

    def up(i, carry):
        cols = pl.ds(pl.multiple_of(i * chunk, 128), chunk)
        pre = nn(x_ref[...], m_ref[0, :, cols]) + bup_ref[:, cols]
        value, slope = gelu_parts(pre)
        h_ref[:, cols] = value.astype(bf16)
        gp_ref[:, cols] = slope
        return carry

    lax.fori_loop(0, hidden // chunk, up, 0)

    def down(i, carry):
        cols = pl.ds(pl.multiple_of(i * 256, 128), 256)
        acc_ref[:, cols] = nt(h_ref[...], m_ref[1, pl.ds(pl.multiple_of(i * 256, 16), 256), :])
        return carry

    lax.fori_loop(0, width // 256, down, 0)
    gain = vec(vec_ref, row + 5)
    unit, rate = norm_parts(y_ref[...] + acc_ref[...] + vec(vec_ref, row + 4))
    out_ref[...] = (unit * gain + vec(vec_ref, row + 6)).astype(bf16)
    dtot, dgain, dshift = norm_back(cot_ref[...].astype(f32), unit, rate, gain)
    dy = dtot.astype(bf16)
    dy_ref[...] = dy
    dvec_ref[...] = jnp.zeros_like(dvec_ref)
    dvec_ref[row + 4 : row + 5, :] = jnp.sum(dy.astype(f32), axis=0, keepdims=True)
    dvec_ref[row + 5 : row + 6, :] = dgain
    dvec_ref[row + 6 : row + 7, :] = dshift
    y_ref[...] = dtot
    place(xt_ref, x_ref[...].T, me, orders[0])
    place(dyt_ref, dy.T, me, orders[1])

    def back(i, carry):
        cols = pl.ds(pl.multiple_of(i * chunk, 128), chunk)
        dpre = (nn(dy_ref[...], m_ref[1, :, cols]) * gp_ref[:, cols]).astype(bf16)
        dpre_ref[:, cols] = dpre
        dbup_ref[:, cols] = jnp.sum(dpre.astype(f32), axis=0, keepdims=True)
        put(keep_ref, send_ref, 0, block, cols, nn(xt_ref[...], dpre))
        put(keep_ref, send_ref, width // 2, block, cols, nn(dyt_ref[...], h_ref[:, cols]))
        return carry

    lax.fori_loop(0, hidden // chunk, back, 0)
    for i in range(parts):
        dvec_ref[row + i : row + i + 1, :] = dbup_ref[:, i * width : (i + 1) * width]

    def rows(i, carry):
        cols = pl.ds(pl.multiple_of(i * 256, 128), 256)
        acc_ref[:, cols] = nt(dpre_ref[...], m_ref[0, pl.ds(pl.multiple_of(i * 256, 16), 256), :])
        return carry

    lax.fori_loop(0, width // 256, rows, 0)
    unit2, rate2 = norm_parts(tot_ref[...])
    dtot2, dgain2, dshift2 = norm_back(acc_ref[...] + y_ref[...], unit2, rate2, vec(vec_ref, self_row + 3))
    dtot_ref[...] = dtot2
    dvec_ref[self_row + 3 : self_row + 4, :] = dgain2
    dvec_ref[self_row + 4 : self_row + 5, :] = dshift2


def column_sum(low):
    return jnp.sum(low.astype(f32), axis=0, keepdims=True)


def self_backward_kernel(
    row, blocks, orders,
    me_ref, dtot_ref, tot_ref, w_ref, vec_ref, q_ref, k_ref, v_ref, p_ref, c_ref,
    out_ref, keep_ref, send_ref, dvec_ref,
    dq_ref, dk_ref, dv_ref, dc_ref, xp_ref, xq_ref, ct_ref,
):
    me = me_ref[0]
    da = dtot_ref[...].astype(bf16)
    dvec_ref[...] = jnp.zeros_like(dvec_ref)
    dvec_ref[row + 2 : row + 3, :] = column_sum(da)
    dc_ref[...] = nt(da, w_ref[3]).astype(bf16)
    place(ct_ref, c_ref[...].T, me, orders[0])
    width = w_ref.shape[2]
    every = pl.ds(0, width)
    block = width // SLOTS
    put(keep_ref, send_ref, block, 2 * block, every, nn(ct_ref[...], da))
    heads_backward(q_ref, k_ref, v_ref, p_ref, dc_ref, dq_ref, dk_ref, dv_ref, blocks)
    unit, rate = norm_parts(tot_ref[...])
    gain = vec(vec_ref, CROSS + 3)
    low = (unit * gain + vec(vec_ref, CROSS + 4)).astype(bf16)
    turned = low.T
    place(xp_ref, turned, me, orders[0])
    place(xq_ref, turned, me, orders[1])
    dq, dk, dv = dq_ref[...], dk_ref[...], dv_ref[...]
    put(keep_ref, send_ref, 0, 2 * block, every, nn(xp_ref[...], dq))
    put(keep_ref, send_ref, width, 2 * block, every, nn(xq_ref[...], dk))
    put(keep_ref, send_ref, width + block, 2 * block, every, nn(xq_ref[...], dv))
    dvec_ref[row : row + 1, :] = column_sum(dq)
    dvec_ref[row + 1 : row + 2, :] = column_sum(dv)
    dx = dtot_ref[...] + nt(dq, w_ref[0]) + nt(dk, w_ref[1]) + nt(dv, w_ref[2])
    dtot, dgain, dshift = norm_back(dx, unit, rate, gain)
    out_ref[...] = dtot
    dvec_ref[CROSS + 3 : CROSS + 4, :] = dgain
    dvec_ref[CROSS + 4 : CROSS + 5, :] = dshift


def cross_backward_kernel(
    blocks, orders,
    me_ref, dw_ref, dr_ref, words_ref, regions_ref, w_ref, va_ref, vb_ref, vc_ref, vd_ref,
    wq_ref, wk_ref, wv_ref, wp_ref, wc_ref, rq_ref, rk_ref, rv_ref, rp_ref, rc_ref,
    wout_ref, rout_ref, keep_ref, send_ref,
    wdq_ref, wdk_ref, wdv_ref, wdc_ref, rdq_ref, rdk_ref, rdv_ref, rdc_ref, wt_ref, rt_ref, wp2_ref, rp2_ref, wq2_ref, rq2_ref, dvec_ref, vt_ref,
):
    me = me_ref[0]
    width = w_ref.shape[2]
    every = pl.ds(0, width)
    block = width // SLOTS
    stride = 2 * block + VECTOR_ROWS
    second = stride * (SLOTS // 2)
    wda, rda = dw_ref[...].astype(bf16), dr_ref[...].astype(bf16)
    dvec_ref[...] = va_ref[...] + vb_ref[...] + vc_ref[...] + vd_ref[...]
    dvec_ref[CROSS + 2 : CROSS + 3, :] = column_sum(wda) + column_sum(rda)
    wdc_ref[...] = nt(wda, w_ref[3]).astype(bf16)
    rdc_ref[...] = nt(rda, w_ref[3]).astype(bf16)
    heads_backward(wq_ref, wk_ref, wv_ref, wp_ref, wdc_ref, wdq_ref, wdk_ref, wdv_ref, blocks)
    heads_backward(rq_ref, rk_ref, rv_ref, rp_ref, rdc_ref, rdq_ref, rdk_ref, rdv_ref, blocks)
    place(wt_ref, wc_ref[...].T, me, orders[0])
    place(rt_ref, rc_ref[...].T, me, orders[0])
    put(keep_ref, send_ref, block, stride, every, nn(wt_ref[...], wda) + nn(rt_ref[...], rda))
    words_t, regions_t = words_ref[...].T, regions_ref[...].T
    place(wp2_ref, words_t, me, orders[0])
    place(rp2_ref, regions_t, me, orders[0])
    wdq, wdk, wdv = wdq_ref[...], wdk_ref[...], wdv_ref[...]
    rdq, rdk, rdv = rdq_ref[...], rdk_ref[...], rdv_ref[...]
    put(keep_ref, send_ref, 0, stride, every, nn(wp2_ref[...], wdq) + nn(rp2_ref[...], rdq))
    place(wq2_ref, words_t, me, orders[1])
    place(rq2_ref, regions_t, me, orders[1])
    put(keep_ref, send_ref, second, 2 * block, every, nn(rq2_ref[...], wdk) + nn(wq2_ref[...], rdk))
    put(keep_ref, send_ref, second + block, 2 * block, every, nn(rq2_ref[...], wdv) + nn(wq2_ref[...], rdv))
    dvec_ref[CROSS : CROSS + 1, :] = column_sum(wdq) + column_sum(rdq)
    dvec_ref[CROSS + 1 : CROSS + 2, :] = column_sum(wdv) + column_sum(rdv)
    vt_ref[...] = jnp.zeros_like(vt_ref)
    for s in range(SLOTS):
        slot = s if orders[0] is None else slot_of(s, me, orders[0])
        vt_ref[pl.ds(pl.multiple_of(slot * VECTOR_ROWS, 16), VECTOR_ROWS), 0:block] = dvec_ref[:, s * block : (s + 1) * block].astype(bf16)
    for j in range(SLOTS):
        dest = keep_ref if j < SLOTS // 2 else send_ref
        start = (j % (SLOTS // 2)) * stride + 2 * block
        dest[start : start + VECTOR_ROWS, :] = vt_ref[j * VECTOR_ROWS : (j + 1) * VECTOR_ROWS, :]
    wout_ref[...] = (dw_ref[...] + nt(wdq, w_ref[0]) + nt(rdk, w_ref[1]) + nt(rdv, w_ref[2])).astype(bf16)
    rout_ref[...] = (dr_ref[...] + nt(rdq, w_ref[0]) + nt(wdk, w_ref[1]) + nt(wdv, w_ref[2])).astype(bf16)


VMEM_LIMIT = 60 * 1024 * 1024


def call(kernel, name, outs, scratch, flops, args, scalar=False):
    whole = pl.BlockSpec(memory_space=pltpu.VMEM)
    specs = [whole] * len(args)
    if scalar:
        specs[0] = pl.BlockSpec(memory_space=pltpu.SMEM)
    out_shape = tuple(jax.ShapeDtypeStruct(s, d) for s, d in outs)
    moved = sum(a.size * a.dtype.itemsize for a in args) + sum(o.size * o.dtype.itemsize for o in out_shape)
    return pl.pallas_call(
        kernel,
        out_shape=out_shape,
        in_specs=specs,
        out_specs=tuple([whole] * len(outs)),
        scratch_shapes=[pltpu.VMEM(s, d) for s, d in scratch],
        compiler_params=pltpu.CompilerParams(vmem_limit_bytes=VMEM_LIMIT),
        cost_estimate=pl.CostEstimate(flops=int(flops), bytes_accessed=int(moved), transcendentals=0),
        name=name,
    )(*args)


def kept_shapes(nq, nk, width, bias):
    blocks, qb, kb = bias.shape
    return [((nq, width), bf16), ((nk, width), bf16), ((nk, width), bf16), ((blocks * HEADS, qb, kb), bf16), ((nq, width), bf16)]


def cross_forward(words, regions, w, vectors, wr, rw):
    nw, nr, width = words.shape[0], regions.shape[0], words.shape[1]
    outs = [((nw, width), f32), ((nr, width), f32)] + kept_shapes(nw, nr, width, wr) + kept_shapes(nr, nw, width, rw)
    got = call(cross_forward_kernel, "cross_forward", outs, [], 8.0 * (nw + nr) * width * width, (words, regions, w, vectors, wr, rw))
    return got[0], got[1], got[2:7], got[7:12]


def self_forward(row, total, w, vectors, bias):
    n, width = total.shape
    outs = [((n, width), f32)] + kept_shapes(n, n, width, bias)
    got = call(partial(self_forward_kernel, row), "self_forward", outs, [], 8.0 * n * width * width, (total, w, vectors, bias))
    return got[0], got[1:]


def feed_both(self_row, row, orders, me, total, cot, m, vectors):
    n, width = total.shape
    hidden = m.shape[2]
    half = (width, hidden)
    outs = [((n, width), bf16), ((n, width), f32), (half, bf16), (half, bf16), ((VECTOR_ROWS, width), f32)]
    scratch = [
        ((n, width), bf16), ((n, width), f32), ((n, hidden), bf16), ((n, hidden), f32), ((n, hidden), bf16),
        ((n, width), bf16), ((width, n), bf16), ((width, n), bf16), ((n, width), f32), ((1, hidden), f32), ((1, hidden), f32),
    ]
    return call(partial(feed_kernel, self_row, row, 512, orders), "feed", outs, scratch, 12.0 * n * width * hidden, (me, total, cot, m, vectors), scalar=True)


def self_backward(row, blocks, orders, me, dtot, total, w, vectors, kept):
    n, width = total.shape
    half = (2 * width, width)
    outs = [((n, width), f32), (half, bf16), (half, bf16), ((VECTOR_ROWS, width), f32)]
    scratch = [((n, width), bf16)] * 4 + [((width, n), bf16)] * 3
    return call(partial(self_backward_kernel, row, blocks, orders), "self_backward", outs, scratch, 16.0 * n * width * width, (me, dtot, total, w, vectors, *kept), scalar=True)


def cross_backward(blocks, orders, me, dw, dr, words, regions, w, dvecs, word_kept, region_kept):
    nw, nr, width = words.shape[0], regions.shape[0], words.shape[1]
    half = (2 * width + VECTOR_ROWS * (SLOTS // 2), width)
    outs = [((nw, width), bf16), ((nr, width), bf16), (half, bf16), (half, bf16)]
    scratch = [((nw, width), bf16), ((nr, width), bf16), ((nr, width), bf16), ((nw, width), bf16)]
    scratch += [((nr, width), bf16), ((nw, width), bf16), ((nw, width), bf16), ((nr, width), bf16)]
    scratch += [((width, nw), bf16), ((width, nr), bf16)] * 3
    scratch += [((VECTOR_ROWS, width), f32), ((VECTOR_ROWS * SLOTS, width), bf16)]
    return call(partial(cross_backward_kernel, blocks, orders), "cross_backward", outs, scratch, 16.0 * (nw + nr) * width * width, (me, dw, dr, words, regions, w, *dvecs, *word_kept, *region_kept), scalar=True)


def block_bias(query_slots, key_slots, key_bias, blocks):
    items = key_bias.shape[0] // blocks
    rows = jnp.arange(items * query_slots) // query_slots
    cols = jnp.arange(items * key_slots) // key_slots
    same = rows[:, None] == cols[None, :]
    return jnp.where(same[None], key_bias.reshape(blocks, 1, items * key_slots), -1e30).astype(f32)


def reduce_pieces(keep, send, first):
    def exchange(value, bit):
        return lax.ppermute(value, "fsdp", [(i, i ^ (1 << bit)) for i in range(SLOTS)])

    def add(left, right):
        return (left.astype(f32) + right.astype(f32)).astype(bf16)

    got = exchange(send, 0)
    cut = first
    rest = keep.shape[0]
    done = []
    for (low, high), bits in zip(((0, cut), (cut, rest)), ((1, 2), (2, 1))):
        half = (high - low) // 2
        mid = low + half
        sent = add(keep[mid:high], got[mid:high])
        held = add(keep[low:mid], got[low:mid])
        back = exchange(sent, bits[0])
        quarter = half // 2
        sent = add(held[quarter:], back[quarter:])
        held = add(held[:quarter], back[:quarter])
        back = exchange(sent, bits[1])
        done.append(add(held, back))
    return done


def local(
    words_in, regions_in, word_mask, region_count,
    cross_matrices, cross_vectors, word_self_matrices, word_self_vectors,
    region_self_matrices, region_self_vectors, word_feed_matrices, word_feed_vectors,
    region_feed_matrices, region_feed_vectors, words_cotangent, regions_cotangent,
):
    items, words, width = words_in.shape
    regions = regions_in.shape[1]
    share = cross_matrices.shape[1]
    count = width // share
    blocks = 3 if items % 12 == 0 else 1
    swaps = count == SLOTS
    orders = ((0, 1, 2), (0, 2, 1)) if swaps else (None, None)
    me = lax.axis_index("fsdp").astype(jnp.int32).reshape(1)

    own = jnp.concatenate([cross_vectors, word_self_vectors, region_self_vectors, word_feed_vectors, region_feed_vectors], axis=0)
    own = jnp.pad(own, ((0, VECTOR_ROWS - own.shape[0]), (0, 0)))
    vectors = lax.all_gather(own, "fsdp", axis=1, tiled=True).astype(f32)

    def whole(shard):
        return lax.all_gather(shard, "fsdp", axis=1, tiled=True)

    cross = whole(cross_matrices)
    region_self = whole(region_self_matrices)
    word_self = whole(word_self_matrices)
    region_feed = whole(region_feed_matrices)
    word_feed = whole(word_feed_matrices)

    word_bias = (word_mask.astype(f32) - 1.0) * 10000.0
    region_bias = jnp.where(jnp.arange(regions)[None, :] < region_count[:, None], 0.0, negative).astype(f32)
    word_rows = words_in.reshape(-1, width)
    region_rows = regions_in.reshape(-1, width)
    wr = block_bias(words, regions, region_bias, blocks)
    rw = block_bias(regions, words, word_bias, blocks)
    ww = block_bias(words, words, word_bias, blocks)
    rr = block_bias(regions, regions, region_bias, blocks)

    word_one, region_one, word_kept, region_kept = cross_forward(word_rows, region_rows, cross, vectors, wr, rw)
    region_two, region_self_kept = self_forward(REGION_SELF, region_one, region_self, vectors, rr)
    word_two, word_self_kept = self_forward(WORD_SELF, word_one, word_self, vectors, ww)
    regions_out, region_dtwo, region_feed_keep, region_feed_send, dvec_a = feed_both(
        REGION_SELF, REGION_FEED, orders, me, region_two, regions_cotangent.reshape(-1, width), region_feed, vectors
    )
    region_done, region_self_keep, region_self_send, dvec_b = self_backward(
        REGION_SELF, blocks, orders, me, region_dtwo, region_one, region_self, vectors, region_self_kept
    )
    words_out, word_dtwo, word_feed_keep, word_feed_send, dvec_c = feed_both(
        WORD_SELF, WORD_FEED, orders, me, word_two, words_cotangent.reshape(-1, width), word_feed, vectors
    )
    word_done, word_self_keep, word_self_send, dvec_d = self_backward(
        WORD_SELF, blocks, orders, me, word_dtwo, word_one, word_self, vectors, word_self_kept
    )
    words_grad, regions_grad, cross_keep, cross_send = cross_backward(
        blocks, orders, me, word_done, region_done, word_rows, region_rows, cross,
        (dvec_a, dvec_b, dvec_c, dvec_d), word_kept, region_kept,
    )

    half = SLOTS // 2
    block = width // SLOTS
    names = ["region_feed", "region_self", "word_feed", "word_self", "cross"]
    pairs = [
        (region_feed_keep, region_feed_send), (region_self_keep, region_self_send), (word_feed_keep, word_feed_send),
        (word_self_keep, word_self_send), (cross_keep, cross_send),
    ]
    grads = {}
    for name, (keep, send) in zip(names, pairs):
        per = [block, block] if "feed" in name else [2 * block, 2 * block]
        if name == "cross":
            per[0] += VECTOR_ROWS
        if swaps:
            first, second = reduce_pieces(keep, send, half * per[0])
        else:
            whole_rows = jnp.concatenate([keep[: half * per[0]], send[: half * per[0]], keep[half * per[0] :], send[half * per[0] :]])
            cut = SLOTS * per[0]
            first = whole_rows[:cut].reshape(SLOTS, per[0], -1)
            second = whole_rows[cut:].reshape(SLOTS, per[1], -1)

            def scattered(rows):
                joined = rows.reshape(SLOTS, -1, block, rows.shape[-1]).transpose(1, 0, 2, 3)
                joined = joined.reshape(-1, width, rows.shape[-1])
                return lax.psum_scatter(joined, "fsdp", scatter_dimension=1, tiled=True).reshape(-1, rows.shape[-1])

            if name == "cross":
                tail = first[:, 2 * block :, :block].transpose(1, 0, 2).reshape(VECTOR_ROWS, width)
                vector_shard = lax.psum_scatter(tail, "fsdp", scatter_dimension=1, tiled=True)
                first = first[:, : 2 * block]
            first, second = scattered(first), scattered(second)
        grads[name] = (first, second)
    result = {}
    for name in names:
        first, second = grads[name]
        if name == "cross" and swaps:
            first, second, vector_shard = lax.psum((first[: 2 * share], second, first[2 * share :, :share]), "dp")
            vector_sum = vector_shard
        elif name == "cross":
            first, second, vector_sum = lax.psum((first, second, vector_shard), "dp")
        else:
            first, second = lax.psum((first, second), "dp")
        if "feed" in name:
            result[name] = jnp.stack([first, second]).astype(f32)
        else:
            result[name] = jnp.stack([first[:share], second[:share], second[share:], first[share:]]).astype(f32)
    vector_sum = vector_sum.astype(f32)

    def rows_of(start, number):
        return vector_sum[start : start + number]

    return (
        words_out.reshape(items, words, width),
        regions_out.reshape(items, regions, width),
        words_grad.reshape(items, words, width),
        regions_grad.reshape(items, regions, width),
        result["cross"],
        rows_of(CROSS, 5),
        result["word_self"],
        rows_of(WORD_SELF, 5),
        result["region_self"],
        rows_of(REGION_SELF, 5),
        result["word_feed"],
        rows_of(WORD_FEED, 7),
        result["region_feed"],
        rows_of(REGION_FEED, 7),
    )


def solution(mesh):
    items = P(("dp", "fsdp"), None, None)
    matrix = P(None, "fsdp", None)
    vector = P(None, "fsdp")
    weights = (matrix, vector) * 5
    return jax.shard_map(
        local,
        mesh=mesh,
        in_specs=(items, items, P(("dp", "fsdp"), None), P(("dp", "fsdp")), *weights, items, items),
        out_specs=(items,) * 4 + weights,
        check_vma=False,
    )
```

```python
from functools import partial

import jax
import jax.numpy as jnp
from jax import lax
from jax.sharding import PartitionSpec as P
from jax.experimental import pallas as pl
from jax.experimental.pallas import tpu as pltpu

HEADS = 12
epsilon = 1e-12
negative = -10000.0
bf16 = jnp.bfloat16
f32 = jnp.float32

CROSS, WORD_SELF, REGION_SELF, WORD_FEED, REGION_FEED = 0, 5, 10, 15, 22
VECTOR_ROWS = 32


def nn(left, right):
    return jnp.dot(left, right, preferred_element_type=f32)


def nt(left, right):
    return lax.dot_general(left, right, (((1,), (1,)), ((), ())), preferred_element_type=f32)


def tn(left, right):
    return lax.dot_general(left, right, (((0,), (0,)), ((), ())), preferred_element_type=f32)


def norm_parts(total):
    centred = total - jnp.mean(total, axis=-1, keepdims=True)
    spread = jnp.mean(centred * centred, axis=-1, keepdims=True)
    rate = lax.rsqrt(spread + epsilon)
    return centred * rate, rate


def norm_back(grad, unit, rate, gain):
    scaled = grad * gain
    mean_one = jnp.mean(scaled, axis=-1, keepdims=True)
    mean_two = jnp.mean(scaled * unit, axis=-1, keepdims=True)
    return (
        rate * (scaled - mean_one - unit * mean_two),
        jnp.sum(grad * unit, axis=0, keepdims=True),
        jnp.sum(grad, axis=0, keepdims=True),
    )


def half_masks(rows):
    lane = lax.broadcasted_iota(jnp.int32, (rows, 128), 1)
    return (lane < 64, lane >= 64)


def heads_forward(q_ref, k_ref, v_ref, bias_ref, probs_ref, ctx_ref):
    blocks, qb, kb = bias_ref.shape
    pairs = q_ref.shape[1] // 128
    masks = half_masks(kb)
    zero = jnp.zeros((kb, 128), bf16)

    def block(b, carry):
        rq = pl.ds(pl.multiple_of(b * qb, 16), qb)
        rk = pl.ds(pl.multiple_of(b * kb, 16), kb)
        bias = bias_ref[b]
        for p in range(pairs):
            cols = pl.ds(p * 128, 128)
            qp = q_ref[rq, cols]
            kp = k_ref[rk, cols]
            vp = v_ref[rk, cols]
            mixed = None
            for half in range(2):
                s = nt(qp, jnp.where(masks[half], kp, zero)) * 0.125 + bias
                e = jnp.exp(s - jnp.max(s, axis=-1, keepdims=True))
                low = (e / jnp.sum(e, axis=-1, keepdims=True)).astype(bf16)
                probs_ref[b * (2 * pairs) + 2 * p + half] = low
                part = nn(low, jnp.where(masks[half], vp, zero))
                mixed = part if mixed is None else mixed + part
            ctx_ref[rq, cols] = mixed.astype(bf16)
        return carry

    lax.fori_loop(0, blocks, block, 0)


def heads_backward(q_ref, k_ref, v_ref, probs_ref, dctx_ref, dq_ref, dk_ref, dv_ref, blocks):
    qb = q_ref.shape[0] // blocks
    kb = k_ref.shape[0] // blocks
    pairs = q_ref.shape[1] // 128
    kmasks, qmasks = half_masks(kb), half_masks(qb)
    kzero, qzero = jnp.zeros((kb, 128), bf16), jnp.zeros((qb, 128), bf16)

    def block(b, carry):
        rq = pl.ds(pl.multiple_of(b * qb, 16), qb)
        rk = pl.ds(pl.multiple_of(b * kb, 16), kb)
        for p in range(pairs):
            cols = pl.ds(p * 128, 128)
            qp = q_ref[rq, cols]
            kp = k_ref[rk, cols]
            vp = v_ref[rk, cols]
            dc = dctx_ref[rq, cols]
            dq = dk = dv = 0.0
            for half in range(2):
                low = probs_ref[b * (2 * pairs) + 2 * p + half]
                probs = low.astype(f32)
                dp = nt(dc, jnp.where(kmasks[half], vp, kzero))
                dv = dv + tn(low, jnp.where(qmasks[half], dc, qzero))
                t = probs * dp
                ds = (t - probs * jnp.sum(t, axis=-1, keepdims=True)).astype(bf16)
                dq = dq + nn(ds, jnp.where(kmasks[half], kp, kzero))
                dk = dk + tn(ds, jnp.where(qmasks[half], qp, qzero))
            dq_ref[rq, cols] = (dq * 0.125).astype(bf16)
            dk_ref[rk, cols] = (dk * 0.125).astype(bf16)
            dv_ref[rk, cols] = dv.astype(bf16)
        return carry

    lax.fori_loop(0, blocks, block, 0)


def vec(vec_ref, row):
    return vec_ref[row : row + 1, :]


def attend(x_low, c_low, base, w_ref, vec_ref, row, bias_ref, q_ref, k_ref, v_ref, probs_ref, ctx_ref):
    q_ref[...] = (nn(x_low, w_ref[0]) + vec(vec_ref, row)).astype(bf16)
    k_ref[...] = nn(c_low, w_ref[1]).astype(bf16)
    v_ref[...] = (nn(c_low, w_ref[2]) + vec(vec_ref, row + 1)).astype(bf16)
    heads_forward(q_ref, k_ref, v_ref, bias_ref, probs_ref, ctx_ref)
    return base + nn(ctx_ref[...], w_ref[3]) + vec(vec_ref, row + 2)


def cross_forward_kernel(count, me_ref, words_ref, regions_ref, known_ref, wr_ref, rw_ref, *refs):
    parts, refs = refs[:count], refs[count:]
    wtot_ref, rtot_ref, wq_ref, wk_ref, wv_ref, wp_ref, wc_ref, rq_ref, rk_ref, rv_ref, rp_ref, rc_ref = refs[:12]
    vec_ref, w_ref, vt_ref, sems = refs[12:]
    settle(fetch(parts, me_ref[0], w_ref, sems, vt_ref))
    if count == 1:
        vec_ref[...] = known_ref[...].astype(f32)
    else:
        block = w_ref.shape[1] // SLOTS
        for s in range(SLOTS):
            vec_ref[:, s * block : (s + 1) * block] = vt_ref[s ^ me_ref[0]][:, :block].astype(f32)
    words, regions = words_ref[...], regions_ref[...]
    wtot_ref[...] = attend(words, regions, words.astype(f32), w_ref, vec_ref, CROSS, wr_ref, wq_ref, wk_ref, wv_ref, wp_ref, wc_ref)
    rtot_ref[...] = attend(regions, words, regions.astype(f32), w_ref, vec_ref, CROSS, rw_ref, rq_ref, rk_ref, rv_ref, rp_ref, rc_ref)


def self_forward_kernel(row, count, me_ref, tot_ref, vec_ref, bias_ref, *refs):
    parts = refs[:count]
    out_ref, q_ref, k_ref, v_ref, p_ref, c_ref, w_ref, sems = refs[count:]
    copies = fetch(parts, me_ref[0], w_ref, sems)
    unit, _ = norm_parts(tot_ref[...])
    y = unit * vec(vec_ref, CROSS + 3) + vec(vec_ref, CROSS + 4)
    low = y.astype(bf16)
    settle(copies)
    out_ref[...] = attend(low, low, y, w_ref, vec_ref, row, bias_ref, q_ref, k_ref, v_ref, p_ref, c_ref)


def gelu_parts(x):
    size = jnp.abs(x)
    e = jnp.exp(x * x * -0.5)
    t = 1.0 / (1.0 + (0.3275911 * 0.7071067811865476) * size)
    poly = t * (0.127414796 + t * (-0.142248368 + t * (0.7107068705 + t * (-0.7265760135 + t * 0.5307027145))))
    tail = poly * e
    phi = jnp.where(x >= 0, 1.0 - tail, tail)
    return x * phi, phi + x * e * 0.3989422804014327


def slot_of(s, me):
    k = s ^ me
    core, x, y = k & 1, (k >> 1) & 1, (k >> 2) & 1
    flip = (me & 1) ^ core
    return core * 4 + jnp.where(flip == 0, x * 2 + y, y * 2 + x)


def place(dest_ref, value, me):
    if me is None:
        dest_ref[...] = value
        return
    rows = value.shape[0] // SLOTS
    for s in range(SLOTS):
        dest_ref[pl.ds(pl.multiple_of(slot_of(s, me) * rows, 16), rows), :] = value[s * rows : (s + 1) * rows, :]


SLOTS = 8


def put(keep_ref, send_ref, base, stride, cols, value):
    rows = value.shape[0] // SLOTS
    low = value.astype(bf16)
    for j in range(SLOTS):
        dest = keep_ref if j < SLOTS // 2 else send_ref
        start = base + (j % (SLOTS // 2)) * stride
        dest[start : start + rows, cols] = low[j * rows : (j + 1) * rows]


def feed_kernel(
    self_row, row, chunk, swaps,
    me_ref, tot_ref, cot_ref, far_ref, vec_ref,
    out_ref, dtot_ref, far_keep_ref, far_send_ref, dvec_ref,
    x_ref, y_ref, h_ref, gp_ref, dpre_ref, dy_ref, xt_ref, dyt_ref, acc_ref, bup_ref, dbup_ref,
    m_ref, keep_ref, send_ref, in_sems, out_sems,
):
    me = me_ref[0] if swaps else None
    copies = [pltpu.make_async_copy(far_ref.at[m], m_ref.at[m], in_sems.at[m]) for m in range(2)]
    for copy in copies:
        copy.start()
    width = tot_ref.shape[1]
    hidden = m_ref.shape[2]
    parts = hidden // width
    block = width // SLOTS
    for i in range(parts):
        bup_ref[:, i * width : (i + 1) * width] = vec(vec_ref, row + i)
    unit2, rate2 = norm_parts(tot_ref[...])
    y = unit2 * vec(vec_ref, self_row + 3) + vec(vec_ref, self_row + 4)
    y_ref[...] = y
    x_ref[...] = y.astype(bf16)
    copies[0].wait()

    def up(i, carry):
        cols = pl.ds(pl.multiple_of(i * chunk, 128), chunk)
        pre = nn(x_ref[...], m_ref[0, :, cols]) + bup_ref[:, cols]
        value, slope = gelu_parts(pre)
        h_ref[:, cols] = value.astype(bf16)
        gp_ref[:, cols] = slope
        return carry

    lax.fori_loop(0, hidden // chunk, up, 0)
    copies[1].wait()

    def down(i, carry):
        cols = pl.ds(pl.multiple_of(i * 256, 128), 256)
        acc_ref[:, cols] = nt(h_ref[...], m_ref[1, pl.ds(pl.multiple_of(i * 256, 16), 256), :])
        return carry

    lax.fori_loop(0, width // 256, down, 0)
    gain = vec(vec_ref, row + 5)
    unit, rate = norm_parts(y_ref[...] + acc_ref[...] + vec(vec_ref, row + 4))
    out_ref[...] = (unit * gain + vec(vec_ref, row + 6)).astype(bf16)
    dtot, dgain, dshift = norm_back(cot_ref[...].astype(f32), unit, rate, gain)
    dy = dtot.astype(bf16)
    dy_ref[...] = dy
    dvec_ref[...] = jnp.zeros_like(dvec_ref)
    dvec_ref[row + 4 : row + 5, :] = jnp.sum(dy.astype(f32), axis=0, keepdims=True)
    dvec_ref[row + 5 : row + 6, :] = dgain
    dvec_ref[row + 6 : row + 7, :] = dshift
    y_ref[...] = dtot
    place(xt_ref, x_ref[...].T, me)
    place(dyt_ref, dy.T, me)

    def leaving(i):
        cols = pl.ds(pl.multiple_of(i * chunk, 128), chunk)
        return (
            pltpu.make_async_copy(keep_ref.at[:, cols], far_keep_ref.at[:, cols], out_sems.at[i, 0]),
            pltpu.make_async_copy(send_ref.at[:, cols], far_send_ref.at[:, cols], out_sems.at[i, 1]),
        )

    def back(i, carry):
        cols = pl.ds(pl.multiple_of(i * chunk, 128), chunk)
        dpre = (nn(dy_ref[...], m_ref[1, :, cols]) * gp_ref[:, cols]).astype(bf16)
        dpre_ref[:, cols] = dpre
        dbup_ref[:, cols] = jnp.sum(dpre.astype(f32), axis=0, keepdims=True)
        put(keep_ref, send_ref, 0, 2 * block, cols, nn(xt_ref[...], dpre))
        put(keep_ref, send_ref, block, 2 * block, cols, nn(dyt_ref[...], h_ref[:, cols]))
        for copy in leaving(i):
            copy.start()
        return carry

    lax.fori_loop(0, hidden // chunk, back, 0)
    for i in range(parts):
        dvec_ref[row + i : row + i + 1, :] = dbup_ref[:, i * width : (i + 1) * width]

    def rows(i, carry):
        cols = pl.ds(pl.multiple_of(i * 256, 128), 256)
        acc_ref[:, cols] = nt(dpre_ref[...], m_ref[0, pl.ds(pl.multiple_of(i * 256, 16), 256), :])
        return carry

    lax.fori_loop(0, width // 256, rows, 0)
    unit2, rate2 = norm_parts(tot_ref[...])
    dtot2, dgain2, dshift2 = norm_back(acc_ref[...] + y_ref[...], unit2, rate2, vec(vec_ref, self_row + 3))
    dtot_ref[...] = dtot2
    dvec_ref[self_row + 3 : self_row + 4, :] = dgain2
    dvec_ref[self_row + 4 : self_row + 5, :] = dshift2
    for i in range(hidden // chunk):
        settle(leaving(i))


def column_sum(low):
    return jnp.sum(low.astype(f32), axis=0, keepdims=True)


def self_backward_kernel(
    row, blocks, swaps, count,
    me_ref, dtot_ref, tot_ref, vec_ref, q_ref, k_ref, v_ref, p_ref, c_ref, *refs,
):
    parts = refs[:count]
    out_ref, keep_ref, send_ref, dvec_ref, dq_ref, dk_ref, dv_ref, dc_ref, xt_ref, ct_ref, w_ref, sems = refs[count:]
    me = me_ref[0] if swaps else None
    copies = fetch(parts, me, w_ref, sems)
    da = dtot_ref[...].astype(bf16)
    dvec_ref[...] = jnp.zeros_like(dvec_ref)
    dvec_ref[row + 2 : row + 3, :] = column_sum(da)
    place(ct_ref, c_ref[...].T, me)
    width = w_ref.shape[2]
    every = pl.ds(0, width)
    block = width // SLOTS
    put(keep_ref, send_ref, 3 * block, 4 * block, every, nn(ct_ref[...], da))
    settle(copies)
    dc_ref[...] = nt(da, w_ref[3]).astype(bf16)
    heads_backward(q_ref, k_ref, v_ref, p_ref, dc_ref, dq_ref, dk_ref, dv_ref, blocks)
    unit, rate = norm_parts(tot_ref[...])
    gain = vec(vec_ref, CROSS + 3)
    low = (unit * gain + vec(vec_ref, CROSS + 4)).astype(bf16)
    place(xt_ref, low.T, me)
    dq, dk, dv = dq_ref[...], dk_ref[...], dv_ref[...]
    put(keep_ref, send_ref, 0, 4 * block, every, nn(xt_ref[...], dq))
    put(keep_ref, send_ref, block, 4 * block, every, nn(xt_ref[...], dk))
    put(keep_ref, send_ref, 2 * block, 4 * block, every, nn(xt_ref[...], dv))
    dvec_ref[row : row + 1, :] = column_sum(dq)
    dvec_ref[row + 1 : row + 2, :] = column_sum(dv)
    dx = dtot_ref[...] + nt(dq, w_ref[0]) + nt(dk, w_ref[1]) + nt(dv, w_ref[2])
    dtot, dgain, dshift = norm_back(dx, unit, rate, gain)
    out_ref[...] = dtot
    dvec_ref[CROSS + 3 : CROSS + 4, :] = dgain
    dvec_ref[CROSS + 4 : CROSS + 5, :] = dshift


def region_side_kernel(
    blocks, count,
    me_ref, dr_ref, rq_ref, rk_ref, rv_ref, rp_ref, *refs,
):
    rdq_ref, rdk_ref, rdv_ref, rpart_ref, wpart_ref, rdc_ref, w_ref, sems = refs[count:]
    settle(fetch(refs[:count], me_ref[0], w_ref, sems))
    rdc_ref[...] = nt(dr_ref[...].astype(bf16), w_ref[3]).astype(bf16)
    heads_backward(rq_ref, rk_ref, rv_ref, rp_ref, rdc_ref, rdq_ref, rdk_ref, rdv_ref, blocks)
    rpart_ref[...] = dr_ref[...] + nt(rdq_ref[...], w_ref[0])
    wpart_ref[...] = nt(rdk_ref[...], w_ref[1]) + nt(rdv_ref[...], w_ref[2])


def cross_backward_kernel(
    blocks, swaps, count,
    me_ref, dw_ref, dr_ref, words_ref, regions_ref, va_ref, vb_ref, vc_ref, vd_ref,
    wq_ref, wk_ref, wv_ref, wp_ref, wc_ref, rc_ref, rdq_ref, rdk_ref, rdv_ref, rpart_ref, wpart_ref, *refs,
):
    parts, refs = refs[:count], refs[count:]
    wout_ref, rout_ref, keep_ref, send_ref, wdq_ref, wdk_ref, wdv_ref, wdc_ref, wct_ref, rct_ref = refs[:10]
    wt_ref, rt_ref, dvec_ref, vt_ref, w_ref, sems = refs[10:]
    me = me_ref[0] if swaps else None
    copies = fetch(parts, me, w_ref, sems)
    width = w_ref.shape[2]
    every = pl.ds(0, width)
    block = width // SLOTS
    stride = 4 * block + VECTOR_ROWS
    wda, rda = dw_ref[...].astype(bf16), dr_ref[...].astype(bf16)
    dvec_ref[...] = va_ref[...] + vb_ref[...] + vc_ref[...] + vd_ref[...]
    dvec_ref[CROSS + 2 : CROSS + 3, :] = column_sum(wda) + column_sum(rda)
    place(wct_ref, wc_ref[...].T, me)
    place(rct_ref, rc_ref[...].T, me)
    put(keep_ref, send_ref, 3 * block, stride, every, nn(wct_ref[...], wda) + nn(rct_ref[...], rda))
    settle(copies)
    wdc_ref[...] = nt(wda, w_ref[3]).astype(bf16)
    heads_backward(wq_ref, wk_ref, wv_ref, wp_ref, wdc_ref, wdq_ref, wdk_ref, wdv_ref, blocks)
    place(wt_ref, words_ref[...].T, me)
    place(rt_ref, regions_ref[...].T, me)
    wdq, wdk, wdv = wdq_ref[...], wdk_ref[...], wdv_ref[...]
    rdq, rdk, rdv = rdq_ref[...], rdk_ref[...], rdv_ref[...]
    put(keep_ref, send_ref, 0, stride, every, nn(wt_ref[...], wdq) + nn(rt_ref[...], rdq))
    put(keep_ref, send_ref, block, stride, every, nn(rt_ref[...], wdk) + nn(wt_ref[...], rdk))
    put(keep_ref, send_ref, 2 * block, stride, every, nn(rt_ref[...], wdv) + nn(wt_ref[...], rdv))
    dvec_ref[CROSS : CROSS + 1, :] = column_sum(wdq) + column_sum(rdq)
    dvec_ref[CROSS + 1 : CROSS + 2, :] = column_sum(wdv) + column_sum(rdv)
    vt_ref[...] = jnp.zeros_like(vt_ref)
    for s in range(SLOTS):
        slot = slot_of(s, me) if swaps else s
        vt_ref[pl.ds(pl.multiple_of(slot * VECTOR_ROWS, 16), VECTOR_ROWS), 0:block] = dvec_ref[:, s * block : (s + 1) * block].astype(bf16)
    for j in range(SLOTS):
        dest = keep_ref if j < SLOTS // 2 else send_ref
        start = (j % (SLOTS // 2)) * stride + 4 * block
        dest[start : start + VECTOR_ROWS, :] = vt_ref[j * VECTOR_ROWS : (j + 1) * VECTOR_ROWS, :]
    wout_ref[...] = (dw_ref[...] + nt(wdq, w_ref[0]) + wpart_ref[...]).astype(bf16)
    rout_ref[...] = (rpart_ref[...] + nt(wdk, w_ref[1]) + nt(wdv, w_ref[2])).astype(bf16)


VMEM_LIMIT = 60 * 1024 * 1024


SCALE = 20


class Far:
    def __init__(self, array):
        self.array = array


class Scalar:
    def __init__(self, array):
        self.array = array


class Sequence:
    def __init__(self):
        self.token = self.more = ()
        self.free = False

    def after(self, *arrays):
        self.more += arrays

    def __call__(self, kernel, name, outs, scratch, us, args, far_outs=(), grid=None, in_specs=None, out_specs=None):
        here, far = pl.BlockSpec(memory_space=pltpu.VMEM), pl.BlockSpec(memory_space=pl.ANY)
        if in_specs is None:
            kinds = {Far: far, Scalar: pl.BlockSpec(memory_space=pltpu.SMEM)}
            in_specs = [kinds.get(type(a), here) for a in args]
            out_specs = [far if i in far_outs else here for i in range(len(outs))]
        arrays = [a.array if isinstance(a, (Far, Scalar)) else a for a in args]
        out_shape = tuple(jax.ShapeDtypeStruct(s, d) for s, d in outs)
        moved = sum(a.size * a.dtype.itemsize for a in arrays) + sum(o.size * o.dtype.itemsize for o in out_shape)
        token = self.token + self.more
        self.more = ()

        def body(*refs):
            kernel(*refs[: len(arrays)], *refs[len(arrays) + len(token) :])

        extra = {} if grid is None else {"grid": grid}
        got = pl.pallas_call(
            body,
            out_shape=out_shape,
            in_specs=list(in_specs) + [far] * len(token),
            out_specs=tuple(out_specs),
            scratch_shapes=[pltpu.VMEM(*s) if isinstance(s, tuple) else s for s in scratch],
            compiler_params=pltpu.CompilerParams(vmem_limit_bytes=VMEM_LIMIT),
            cost_estimate=pl.CostEstimate(flops=int(us * SCALE * 1.15e9), bytes_accessed=0, transcendentals=0),
            name=name,
            **extra,
        )(*arrays, *token)
        self.token = () if self.free else (min(got, key=lambda o: o.size * o.dtype.itemsize),)
        return got


def fetch(parts, me, w_ref, sems, vt_ref=None):
    copies = []

    def start(source, dest):
        copies.append(pltpu.make_async_copy(source, dest, sems.at[len(copies)]))
        copies[-1].start()

    if len(parts) == 1:
        for m in range(4):
            start(parts[0].at[m], w_ref.at[m])
        return copies
    block = w_ref.shape[1] // SLOTS
    for other in range(2):
        odd = ((me & 1) ^ other) == 1
        for i in range(4):
            k = jnp.where(odd, (i & 1) * 4 + (i >> 1) * 2, (i & 1) * 2 + (i >> 1) * 4) + other
            rows = pl.ds(pl.multiple_of((k ^ me) * block, 16), block)
            for m in range(4):
                start(parts[other].at[i, pl.ds(m * block, block)], w_ref.at[m, rows, :])
            if vt_ref is not None:
                start(parts[other].at[i, pl.ds(4 * block, VECTOR_ROWS)], vt_ref.at[k])
    return copies


def settle(copies):
    for copy in copies:
        copy.wait()


def kept_shapes(nq, nk, width, bias):
    blocks, qb, kb = bias.shape
    return [((nq, width), bf16), ((nk, width), bf16), ((nk, width), bf16), ((blocks * HEADS, qb, kb), bf16), ((nq, width), bf16)]


def attention_scratch(width):
    return [((4, width, width), bf16), pltpu.SemaphoreType.DMA((40,))]


def fars(parts):
    return [Far(p) for p in parts]


def cross_forward(run, me, words, regions, parts, vectors, wr, rw):
    nw, nr, width = words.shape[0], regions.shape[0], words.shape[1]
    outs = [((nw, width), f32), ((nr, width), f32)] + kept_shapes(nw, nr, width, wr) + kept_shapes(nr, nw, width, rw)
    outs += [((VECTOR_ROWS, width), f32)]
    scratch = attention_scratch(width)
    scratch.insert(1, ((SLOTS, VECTOR_ROWS, width), bf16))
    args = (Scalar(me), words, regions, vectors, wr, rw, *fars(parts))
    got = run(partial(cross_forward_kernel, len(parts)), "cross_forward", outs, scratch, 19, args)
    return got[0], got[1], got[2:7], got[7:12], got[12]


def self_forward(run, row, me, total, parts, vectors, bias):
    n, width = total.shape
    outs = [((n, width), f32)] + kept_shapes(n, n, width, bias)
    args = (Scalar(me), total, vectors, bias, *fars(parts))
    kernel = partial(self_forward_kernel, row, len(parts))
    got = run(kernel, "self_forward", outs, attention_scratch(width), n / 40, args)
    return got[0], got[1:]


def feed_both(run, self_row, row, swaps, me, total, cot, m, vectors):
    n, width = total.shape
    hidden = m.shape[2]
    chunk = 512
    half = (width, hidden)
    outs = [((n, width), bf16), ((n, width), f32), (half, bf16), (half, bf16), ((VECTOR_ROWS, width), f32)]
    scratch = [
        ((n, width), bf16), ((n, width), f32), ((n, hidden), bf16), ((n, hidden), f32), ((n, hidden), bf16),
        ((n, width), bf16), ((width, n), bf16), ((width, n), bf16), ((n, width), f32), ((1, hidden), f32), ((1, hidden), f32),
        ((2, width, hidden), bf16), (half, bf16), (half, bf16),
        pltpu.SemaphoreType.DMA((2,)), pltpu.SemaphoreType.DMA((hidden // chunk, 2)),
    ]
    args = (Scalar(me), total, cot, Far(m), vectors)
    return run(partial(feed_kernel, self_row, row, chunk, swaps), "feed", outs, scratch, 10 + n / 24, args, far_outs=(2, 3))


def self_backward(run, row, blocks, swaps, me, dtot, total, parts, vectors, kept):
    n, width = total.shape
    half = (2 * width, width)
    outs = [((n, width), f32), (half, bf16), (half, bf16), ((VECTOR_ROWS, width), f32)]
    scratch = [((n, width), bf16)] * 4 + [((width, n), bf16)] * 2 + attention_scratch(width)
    args = (Scalar(me), dtot, total, vectors, *kept, *fars(parts))
    kernel = partial(self_backward_kernel, row, blocks, swaps, len(parts))
    return run(kernel, "self_backward", outs, scratch, 8 + n / 40, args)


def region_side(run, blocks, me, dr, parts, kept):
    nr, width = dr.shape
    nw = kept[1].shape[0]
    outs = [((nr, width), bf16), ((nw, width), bf16), ((nw, width), bf16), ((nr, width), f32), ((nw, width), f32)]
    scratch = [((nr, width), bf16)] + attention_scratch(width)
    args = (Scalar(me), dr, *kept[:4], *fars(parts))
    return run(partial(region_side_kernel, blocks, len(parts)), "region_side", outs, scratch, 14, args)


def cross_backward(run, blocks, swaps, me, dw, dr, words, regions, parts, dvecs, word_kept, region_ctx, region_grads):
    nw, nr, width = words.shape[0], regions.shape[0], words.shape[1]
    half = (2 * width + VECTOR_ROWS * (SLOTS // 2), width)
    outs = [((nw, width), bf16), ((nr, width), bf16), (half, bf16), (half, bf16)]
    scratch = [((nw, width), bf16), ((nr, width), bf16), ((nr, width), bf16), ((nw, width), bf16)]
    scratch += [((width, nw), bf16), ((width, nr), bf16)] * 2
    scratch += [((VECTOR_ROWS, width), f32), ((VECTOR_ROWS * SLOTS, width), bf16)] + attention_scratch(width)
    args = (Scalar(me), dw, dr, words, regions, *dvecs, *word_kept, region_ctx, *region_grads, *fars(parts))
    return run(partial(cross_backward_kernel, blocks, swaps, len(parts)), "cross_backward", outs, scratch, 20, args)


def join_pieces(run, *arrays):
    outs = [((2 * a.shape[0], *a.shape[1:]), a.dtype) for a in arrays[::2]]

    def kernel(*refs):
        for i, a in enumerate(arrays):
            n = a.shape[0]
            refs[len(arrays) + i // 2][(i % 2) * n : (i % 2 + 1) * n] = refs[i][...]

    return run(kernel, "join_pieces", outs, [], 2, arrays)


def plus(left, right):
    return (left.astype(f32) + right.astype(f32)).astype(bf16)


def columns_of(width):
    return width // 4 if width % 512 == 0 else width // 3


def add_halves(run, keep, got):
    rows, width = keep.shape
    c = columns_of(width)
    half = rows // 2

    def kernel(keep_ref, got_ref, held_ref, sent_ref):
        held_ref[...] = plus(keep_ref[:half, :], got_ref[:half, :])
        sent_ref[...] = plus(keep_ref[half:, :], got_ref[half:, :])

    def block(n):
        return pl.BlockSpec((n, c), lambda i: (0, i))

    outs = [((half, width), bf16)] * 2
    return run(kernel, "add_halves", outs, [], 6, (keep, got), grid=(width // c,), in_specs=[block(rows)] * 2, out_specs=[block(half)] * 2)


def padded(rows):
    return -(-rows // 64) * 64


def add_last(run, z, held, back):
    n, width = held.shape
    rows = padded(n)

    def fill(held_ref, back_ref, ref):
        ref[:n, :] = plus(held_ref[...], back_ref[...])
        if rows > n:
            ref[n:, :] = jnp.zeros((rows - n, width), bf16)

    if z is None:
        return run(fill, "add_last", [((rows, width), bf16)], [], 2.5, (held, back))[0]

    def kernel(z_ref, held_ref, back_ref, keep_ref, send_ref, all_ref):
        fill(held_ref, back_ref, all_ref)
        split_rows(all_ref, z_ref[0] & 1, keep_ref, send_ref)

    outs = [((rows // 2, width), bf16)] * 2
    return run(kernel, "add_last", outs, [((rows, width), bf16)], 2.5, (Scalar(z), held, back))


def split_rows(all_ref, bit, keep_ref, send_ref):
    half = all_ref.shape[0] // 2
    keep_ref[...] = all_ref[pl.ds(pl.multiple_of(bit * half, 16), half), :]
    send_ref[...] = all_ref[pl.ds(pl.multiple_of((1 - bit) * half, 16), half), :]


def join_rows(own, other, bit, all_ref):
    half = own.shape[0]
    all_ref[pl.ds(pl.multiple_of(bit * half, 16), half), :] = own[...]
    all_ref[pl.ds(pl.multiple_of((1 - bit) * half, 16), half), :] = other[...]


def replicas_halve(run, z, held, back):
    rows, width = held.shape

    def kernel(z_ref, held_ref, back_ref, keep_ref, send_ref, all_ref):
        all_ref[...] = plus(held_ref[...], back_ref[...])
        split_rows(all_ref, (z_ref[0] >> 1) & 1, keep_ref, send_ref)

    outs = [((rows // 2, width), bf16)] * 2
    return run(kernel, "replicas_halve", outs, [((rows, width), bf16)], 2, (Scalar(z), held, back))


def replicas_sum(run, held, back):
    def kernel(held_ref, back_ref, out_ref):
        out_ref[...] = plus(held_ref[...], back_ref[...])

    return run(kernel, "replicas_sum", [(held.shape, bf16)], [], 1.7, (held, back))[0]


def replicas_join(run, z, own, other):
    rows, width = own.shape

    def kernel(z_ref, own_ref, other_ref, out_ref):
        join_rows(own_ref, other_ref, (z_ref[0] >> 1) & 1, out_ref)

    return run(kernel, "replicas_join", [((2 * rows, width), bf16)], [], 1.7, (Scalar(z), own, other))[0]


def shard_out(all_ref, share, refs):
    count = refs[0].shape[0]
    for m in range(count):
        refs[0][m] = all_ref[m * share : (m + 1) * share, :].astype(f32)
    if len(refs) == 2:
        refs[1][...] = all_ref[count * share : count * share + VECTOR_ROWS, :].astype(f32)


def shard_shapes(kind, share, width):
    if kind == "feed":
        return [((2, share, width), f32)]
    outs = [((4, share, width), f32)]
    return outs + [((VECTOR_ROWS, width), f32)] if kind == "cross" else outs


def shard_of_sum(run, kind, share, summed):
    def kernel(all_ref, *refs):
        shard_out(all_ref, share, refs)

    return run(kernel, "shard", shard_shapes(kind, share, summed.shape[1]), [], 2.5, (summed,))


def shard_of_halves(run, kind, share, z, own, other):
    rows, width = own.shape

    def kernel(z_ref, own_ref, other_ref, *refs):
        all_ref = refs[-1]
        join_rows(own_ref, other_ref, z_ref[0] & 1, all_ref)
        shard_out(all_ref, share, refs[:-1])

    return run(kernel, "shard", shard_shapes(kind, share, width), [((2 * rows, width), bf16)], 2.5, (Scalar(z), own, other))


def block_bias(query_slots, key_slots, key_bias, blocks):
    items = key_bias.shape[0] // blocks
    rows = jnp.arange(items * query_slots) // query_slots
    cols = jnp.arange(items * key_slots) // key_slots
    same = rows[:, None] == cols[None, :]
    return jnp.where(same[None], key_bias.reshape(blocks, 1, items * key_slots), -1e30).astype(f32)


def exchange(value, step):
    def partner(i):
        if step == 0:
            return i ^ 1
        return i ^ (2 if (step == 1) == (i % 2 == 0) else 4)

    return lax.ppermute(value, "fsdp", [(i, partner(i)) for i in range(SLOTS)])


def replica_exchange(value, bit):
    return lax.ppermute(value, "dp", [(i, i ^ (1 << bit)) for i in range(4)])


class Gather:
    def __init__(self, run, shard, below=None):
        self.run = run
        width = shard.shape[2]
        self.pieces = shard.reshape(1, -1, width)
        if below is not None:
            below = jnp.pad(below, ((0, VECTOR_ROWS - below.shape[0]), (0, width - below.shape[1])))
            self.pieces = jnp.concatenate([self.pieces, below[None]], axis=1)
        self.got = exchange(self.pieces, 1)

    def step(self):
        (self.pieces,) = join_pieces(self.run, self.pieces, self.got)
        self.got = exchange(self.pieces, 2)

    def finish(self):
        (self.pieces,) = join_pieces(self.run, self.pieces, self.got)
        return self.pieces, exchange(self.pieces, 0)


class Reduction:
    def __init__(self, run, kind, share, z, keep, send, by_exchange):
        self.run, self.kind, self.share, self.z, self.by_exchange = run, kind, share, z, by_exchange
        self.state = (keep, exchange(send, 0))

    def first(self):
        held, sent = add_halves(self.run, *self.state)
        self.state = (held, exchange(sent, 1))

    def second(self):
        held, sent = add_halves(self.run, *self.state)
        self.state = (held, exchange(sent, 2))

    def last(self):
        if not self.by_exchange:
            self.state = lax.psum(add_last(self.run, None, *self.state), "dp")
            return
        held, sent = add_last(self.run, self.z, *self.state)
        self.state = (held, replica_exchange(sent, 0))

    def halve(self):
        held, sent = replicas_halve(self.run, self.z, *self.state)
        self.state = (held, replica_exchange(sent, 1))

    def sum(self):
        own = replicas_sum(self.run, *self.state)
        self.state = (own, replica_exchange(own, 1))

    def join(self):
        own = replicas_join(self.run, self.z, *self.state)
        self.state = (own, replica_exchange(own, 0))

    def out(self):
        if self.by_exchange:
            return shard_of_halves(self.run, self.kind, self.share, self.z, *self.state)
        return shard_of_sum(self.run, self.kind, self.share, self.state)


def unswapped(keep, send, block, count):
    width, wide = block * SLOTS, keep.shape[1]
    rows = jnp.concatenate([keep, send]).reshape(SLOTS, -1, wide)
    matrices = rows[:, : count * block].reshape(SLOTS, count, block, wide).transpose(1, 0, 2, 3).reshape(count, width, wide)
    pieces = [lax.psum_scatter(matrices, "fsdp", scatter_dimension=1, tiled=True)]
    if rows.shape[1] > count * block:
        vectors = rows[:, count * block :, :block].transpose(1, 0, 2).reshape(VECTOR_ROWS, width)
        pieces.append(lax.psum_scatter(vectors, "fsdp", scatter_dimension=1, tiled=True))
    return [piece.astype(f32) for piece in lax.psum(pieces, "dp")]


def local(
    words_in, regions_in, word_mask, region_count,
    cross_matrices, cross_vectors, word_self_matrices, word_self_vectors,
    region_self_matrices, region_self_vectors, word_feed_matrices, word_feed_vectors,
    region_feed_matrices, region_feed_vectors, words_cotangent, regions_cotangent,
):
    items, words, width = words_in.shape
    regions = regions_in.shape[1]
    share = cross_matrices.shape[1]
    count = width // share
    blocks = 3 if items % 12 == 0 else 1
    swaps = count == SLOTS
    me = lax.axis_index("fsdp").astype(jnp.int32).reshape(1)
    z = lax.axis_index("dp").astype(jnp.int32).reshape(1)

    own = jnp.concatenate([cross_vectors, word_self_vectors, region_self_vectors, word_feed_vectors, region_feed_vectors], axis=0)
    def whole(shard):
        return lax.all_gather(shard, "fsdp", axis=1, tiled=True)

    run = Sequence()
    region_feed = whole(region_feed_matrices)
    word_feed = whole(word_feed_matrices)

    word_bias = (word_mask.astype(f32) - 1.0) * 10000.0
    region_bias = jnp.where(jnp.arange(regions)[None, :] < region_count[:, None], 0.0, negative).astype(f32)
    word_rows = words_in.reshape(-1, width)
    region_rows = regions_in.reshape(-1, width)
    wr = block_bias(words, regions, region_bias, blocks)
    rw = block_bias(regions, words, word_bias, blocks)
    ww = block_bias(words, words, word_bias, blocks)
    rr = block_bias(regions, regions, region_bias, blocks)

    block = width // SLOTS
    word_cot = words_cotangent.reshape(-1, width)
    region_cot = regions_cotangent.reshape(-1, width)
    if swaps:
        cross_gather, region_gather = Gather(run, cross_matrices, own), Gather(run, region_self_matrices)
        word_gather = Gather(run, word_self_matrices)
        cross_gather.step()
        region_gather.step()
        vectors = own
        run.after(wr, rw, ww, rr, word_rows, region_rows, word_cot, region_cot)
        cross = cross_gather.finish()
        region_self = region_gather.finish()
    else:
        own = jnp.pad(own, ((0, VECTOR_ROWS - own.shape[0]), (0, 0)))
        vectors = lax.all_gather(own, "fsdp", axis=1, tiled=True)
        cross, region_self, word_self = ((whole(w),) for w in (cross_matrices, region_self_matrices, word_self_matrices))

    def reduction(kind, keep, send, by_exchange):
        return Reduction(run, kind, share, z, keep, send, by_exchange and lax.axis_size("dp") == 4) if swaps else None

    def step(group, name):
        return getattr(group, name)() if swaps else None

    word_one, region_one, word_kept, region_kept, vectors = cross_forward(run, me, word_rows, region_rows, cross, vectors, wr, rw)
    if swaps:
        word_gather.step()
    region_two, region_self_kept = self_forward(run, REGION_SELF, me, region_one, region_self, vectors, rr)

    regions_out, region_dtwo, keep_rf, send_rf, dvec_a = feed_both(
        run, REGION_SELF, REGION_FEED, swaps, me, region_two, region_cot, region_feed, vectors
    )
    if swaps:
        word_self = word_gather.finish()
    rf = reduction("feed", keep_rf, send_rf, False)
    region_done, keep_rs, send_rs, dvec_b = self_backward(
        run, REGION_SELF, blocks, swaps, me, region_dtwo, region_one, region_self, vectors, region_self_kept
    )
    rs = reduction("self", keep_rs, send_rs, True)
    step(rf, "first")
    word_two, word_self_kept = self_forward(run, WORD_SELF, me, word_one, word_self, vectors, ww)
    region_grads = region_side(run, blocks, me, region_done, cross, region_kept)
    step(rs, "first")
    words_out, word_dtwo, keep_wf, send_wf, dvec_c = feed_both(
        run, WORD_SELF, WORD_FEED, swaps, me, word_two, word_cot, word_feed, vectors
    )
    wf = reduction("feed", keep_wf, send_wf, True)
    step(rf, "second")
    step(rs, "second")
    word_done, keep_ws, send_ws, dvec_d = self_backward(
        run, WORD_SELF, blocks, swaps, me, word_dtwo, word_one, word_self, vectors, word_self_kept
    )
    ws = reduction("self", keep_ws, send_ws, True)
    step(wf, "first")
    step(rf, "last")
    step(rs, "last")
    words_grad, regions_grad, keep_cr, send_cr = cross_backward(
        run, blocks, swaps, me, word_done, region_done, word_rows, region_rows, cross,
        (dvec_a, dvec_b, dvec_c, dvec_d), word_kept, region_kept[4], region_grads,
    )
    cr = reduction("cross", keep_cr, send_cr, True)

    if swaps:
        ws.first()
        wf.second()
        rs.halve()
        cr.first()
        ws.second()
        wf.last()
        rs.sum()
        cr.second()
        ws.last()
        wf.halve()
        rs.join()
        cr.last()
        ws.halve()
        wf.sum()
        (grad_rs,) = rs.out()
        cr.halve()
        ws.sum()
        wf.join()
        (grad_rf,) = rf.out()
        cr.sum()
        ws.join()
        (grad_wf,) = wf.out()
        cr.join()
        (grad_ws,) = ws.out()
        grad_cr, vector_sum = cr.out()
        vector_sum = vector_sum[:, :share]
    else:
        (grad_rf,), (grad_wf,) = unswapped(keep_rf, send_rf, block, 2), unswapped(keep_wf, send_wf, block, 2)
        (grad_rs,), (grad_ws,) = unswapped(keep_rs, send_rs, block, 4), unswapped(keep_ws, send_ws, block, 4)
        grad_cr, vector_sum = unswapped(keep_cr, send_cr, block, 4)

    def rows_of(start, number):
        return vector_sum[start : start + number]

    return (
        words_out.reshape(items, words, width),
        regions_out.reshape(items, regions, width),
        words_grad.reshape(items, words, width),
        regions_grad.reshape(items, regions, width),
        grad_cr,
        rows_of(CROSS, 5),
        grad_ws,
        rows_of(WORD_SELF, 5),
        grad_rs,
        rows_of(REGION_SELF, 5),
        grad_wf,
        rows_of(WORD_FEED, 7),
        grad_rf,
        rows_of(REGION_FEED, 7),
    )


def solution(mesh):
    items = P(("dp", "fsdp"), None, None)
    matrix = P(None, "fsdp", None)
    vector = P(None, "fsdp")
    weights = (matrix, vector) * 5
    return jax.shard_map(
        local,
        mesh=mesh,
        in_specs=(items, items, P(("dp", "fsdp"), None), P(("dp", "fsdp")), *weights, items, items),
        out_specs=(items,) * 4 + weights,
        check_vma=False,
    )
```

```python
from functools import partial
import math

import jax
import jax.numpy as jnp
from jax import lax
from jax.sharding import PartitionSpec as P
from jax.experimental import pallas as pl
from jax.experimental.pallas import tpu as pltpu

HEADS = 12
epsilon = 1e-12
negative = -10000.0
bf16 = jnp.bfloat16
f32 = jnp.float32

CROSS, WORD_SELF, REGION_SELF, WORD_FEED, REGION_FEED = 0, 5, 10, 15, 22
VECTOR_ROWS = 32


def nn(left, right):
    return jnp.dot(left, right, preferred_element_type=f32)


def nt(left, right):
    return lax.dot_general(left, right, (((1,), (1,)), ((), ())), preferred_element_type=f32)


def tn(left, right):
    return lax.dot_general(left, right, (((0,), (0,)), ((), ())), preferred_element_type=f32)


def norm_parts(total):
    centred = total - jnp.mean(total, axis=-1, keepdims=True)
    spread = jnp.mean(centred * centred, axis=-1, keepdims=True)
    rate = lax.rsqrt(spread + epsilon)
    return centred * rate, rate


def norm_back(grad, unit, rate, gain):
    scaled = grad * gain
    mean_one = jnp.mean(scaled, axis=-1, keepdims=True)
    mean_two = jnp.mean(scaled * unit, axis=-1, keepdims=True)
    return (
        rate * (scaled - mean_one - unit * mean_two),
        jnp.sum(grad * unit, axis=0, keepdims=True),
        jnp.sum(grad, axis=0, keepdims=True),
    )


def half_masks(rows):
    lane = lax.broadcasted_iota(jnp.int32, (rows, 128), 1)
    return (lane < 64, lane >= 64)


def heads_forward(q_ref, k_ref, v_ref, bias_ref, probs_ref, ctx_ref):
    blocks, qb, kb = bias_ref.shape
    pairs = q_ref.shape[1] // 128
    masks = half_masks(kb)
    zero = jnp.zeros((kb, 128), bf16)

    def block(b, carry):
        rq = pl.ds(pl.multiple_of(b * qb, 16), qb)
        rk = pl.ds(pl.multiple_of(b * kb, 16), kb)
        bias = bias_ref[b]
        for p in range(pairs):
            cols = pl.ds(p * 128, 128)
            qp = q_ref[rq, cols]
            kp = k_ref[rk, cols]
            vp = v_ref[rk, cols]
            mixed = None
            for half in range(2):
                s = nt(qp, jnp.where(masks[half], kp, zero)) * 0.125 + bias
                e = jnp.exp(s - jnp.max(s, axis=-1, keepdims=True))
                low = (e / jnp.sum(e, axis=-1, keepdims=True)).astype(bf16)
                probs_ref[b * (2 * pairs) + 2 * p + half] = low
                part = nn(low, jnp.where(masks[half], vp, zero))
                mixed = part if mixed is None else mixed + part
            ctx_ref[rq, cols] = mixed.astype(bf16)
        return carry

    lax.fori_loop(0, blocks, block, 0)


def heads_backward(q_ref, k_ref, v_ref, probs_ref, dctx_ref, dq_ref, dk_ref, dv_ref, blocks):
    qb = q_ref.shape[0] // blocks
    kb = k_ref.shape[0] // blocks
    pairs = q_ref.shape[1] // 128
    kmasks, qmasks = half_masks(kb), half_masks(qb)
    kzero, qzero = jnp.zeros((kb, 128), bf16), jnp.zeros((qb, 128), bf16)

    def block(b, carry):
        rq = pl.ds(pl.multiple_of(b * qb, 16), qb)
        rk = pl.ds(pl.multiple_of(b * kb, 16), kb)
        for p in range(pairs):
            cols = pl.ds(p * 128, 128)
            qp = q_ref[rq, cols]
            kp = k_ref[rk, cols]
            vp = v_ref[rk, cols]
            dc = dctx_ref[rq, cols]
            dq = dk = dv = 0.0
            for half in range(2):
                low = probs_ref[b * (2 * pairs) + 2 * p + half]
                probs = low.astype(f32)
                dp = nt(dc, jnp.where(kmasks[half], vp, kzero))
                dv = dv + tn(low, jnp.where(qmasks[half], dc, qzero))
                t = probs * dp
                ds = (t - probs * jnp.sum(t, axis=-1, keepdims=True)).astype(bf16)
                dq = dq + nn(ds, jnp.where(kmasks[half], kp, kzero))
                dk = dk + tn(ds, jnp.where(qmasks[half], qp, qzero))
            dq_ref[rq, cols] = (dq * 0.125).astype(bf16)
            dk_ref[rk, cols] = (dk * 0.125).astype(bf16)
            dv_ref[rk, cols] = dv.astype(bf16)
        return carry

    lax.fori_loop(0, blocks, block, 0)


def vec(vec_ref, row):
    return vec_ref[row : row + 1, :]


def attend(x_low, c_low, base, w_ref, vec_ref, row, bias_ref, q_ref, k_ref, v_ref, probs_ref, ctx_ref):
    q_ref[...] = (nn(x_low, w_ref[0]) + vec(vec_ref, row)).astype(bf16)
    k_ref[...] = nn(c_low, w_ref[1]).astype(bf16)
    v_ref[...] = (nn(c_low, w_ref[2]) + vec(vec_ref, row + 1)).astype(bf16)
    heads_forward(q_ref, k_ref, v_ref, bias_ref, probs_ref, ctx_ref)
    return base + nn(ctx_ref[...], w_ref[3]) + vec(vec_ref, row + 2)


def cross_forward_kernel(count, me_ref, words_ref, regions_ref, known_ref, wr_ref, rw_ref, *refs):
    vector_parts, refs = (refs[:2], refs[2:]) if count == 2 else ((), refs)
    parts, refs = refs[:count], refs[count:]
    wtot_ref, rtot_ref, wq_ref, wk_ref, wv_ref, wp_ref, wc_ref, rq_ref, rk_ref, rv_ref, rp_ref, rc_ref = refs[:12]
    vec_ref, w_ref, vt_ref, sems = refs[12:]
    settle(fetch(parts, me_ref[0], w_ref, sems, vector_parts, vt_ref))
    if count == 1:
        vec_ref[...] = known_ref[...].astype(f32)
    else:
        block = w_ref.shape[1] // SLOTS
        for s in range(SLOTS):
            vec_ref[:, s * block : (s + 1) * block] = vt_ref[s ^ me_ref[0]][:, :block].astype(f32)
    words, regions = words_ref[...], regions_ref[...]
    wtot_ref[...] = attend(words, regions, words.astype(f32), w_ref, vec_ref, CROSS, wr_ref, wq_ref, wk_ref, wv_ref, wp_ref, wc_ref)
    rtot_ref[...] = attend(regions, words, regions.astype(f32), w_ref, vec_ref, CROSS, rw_ref, rq_ref, rk_ref, rv_ref, rp_ref, rc_ref)


def self_forward_kernel(row, count, me_ref, tot_ref, vec_ref, bias_ref, *refs):
    parts = refs[:count]
    out_ref, q_ref, k_ref, v_ref, p_ref, c_ref, w_ref, sems = refs[count:]
    copies = fetch(parts, me_ref[0], w_ref, sems)
    unit, _ = norm_parts(tot_ref[...])
    y = unit * vec(vec_ref, CROSS + 3) + vec(vec_ref, CROSS + 4)
    low = y.astype(bf16)
    settle(copies)
    out_ref[...] = attend(low, low, y, w_ref, vec_ref, row, bias_ref, q_ref, k_ref, v_ref, p_ref, c_ref)


def gelu_parts(x):
    size = jnp.abs(x)
    e = jnp.exp(x * x * -0.5)
    t = 1.0 / (1.0 + (0.3275911 * 0.7071067811865476) * size)
    poly = t * (0.127414796 + t * (-0.142248368 + t * (0.7107068705 + t * (-0.7265760135 + t * 0.5307027145))))
    tail = poly * e
    phi = jnp.where(x >= 0, 1.0 - tail, tail)
    return x * phi, phi + x * e * 0.3989422804014327


def slot_of(s, me):
    k = s ^ me
    core, x, y = k & 1, (k >> 1) & 1, (k >> 2) & 1
    flip = (me & 1) ^ core
    return core * 4 + jnp.where(flip == 0, x * 2 + y, y * 2 + x)


def place(dest_ref, value, me):
    if me is None:
        dest_ref[...] = value
        return
    rows = value.shape[0] // SLOTS
    for s in range(SLOTS):
        dest_ref[pl.ds(pl.multiple_of(slot_of(s, me) * rows, 16), rows), :] = value[s * rows : (s + 1) * rows, :]


SLOTS = 8


def put(keep_ref, send_ref, base, stride, cols, value):
    rows = value.shape[0] // SLOTS
    low = value.astype(bf16)
    for j in range(SLOTS):
        dest = keep_ref if j < SLOTS // 2 else send_ref
        start = base + (j % (SLOTS // 2)) * stride
        dest[start : start + rows, cols] = low[j * rows : (j + 1) * rows]


def feed_kernel(
    self_row, row, chunk, swaps,
    me_ref, tot_ref, cot_ref, far_ref, vec_ref,
    out_ref, dtot_ref, far_keep_ref, far_send_ref, dvec_ref,
    x_ref, y_ref, h_ref, gp_ref, dpre_ref, dy_ref, xt_ref, dyt_ref, acc_ref, bup_ref, dbup_ref,
    m_ref, keep_ref, send_ref, in_sems, out_sems,
):
    me = me_ref[0] if swaps else None
    copies = [pltpu.make_async_copy(far_ref.at[m], m_ref.at[m], in_sems.at[m]) for m in range(2)]
    for copy in copies:
        copy.start()
    width = tot_ref.shape[1]
    hidden = m_ref.shape[2]
    parts = hidden // width
    block = width // SLOTS
    for i in range(parts):
        bup_ref[:, i * width : (i + 1) * width] = vec(vec_ref, row + i)
    unit2, rate2 = norm_parts(tot_ref[...])
    y = unit2 * vec(vec_ref, self_row + 3) + vec(vec_ref, self_row + 4)
    y_ref[...] = y
    x_ref[...] = y.astype(bf16)
    copies[0].wait()

    def up(i, carry):
        cols = pl.ds(pl.multiple_of(i * chunk, 128), chunk)
        pre = nn(x_ref[...], m_ref[0, :, cols]) + bup_ref[:, cols]
        value, slope = gelu_parts(pre)
        h_ref[:, cols] = value.astype(bf16)
        gp_ref[:, cols] = slope
        return carry

    lax.fori_loop(0, hidden // chunk, up, 0)
    copies[1].wait()

    def down(i, carry):
        cols = pl.ds(pl.multiple_of(i * 256, 128), 256)
        acc_ref[:, cols] = nt(h_ref[...], m_ref[1, pl.ds(pl.multiple_of(i * 256, 16), 256), :])
        return carry

    lax.fori_loop(0, width // 256, down, 0)
    gain = vec(vec_ref, row + 5)
    unit, rate = norm_parts(y_ref[...] + acc_ref[...] + vec(vec_ref, row + 4))
    out_ref[...] = (unit * gain + vec(vec_ref, row + 6)).astype(bf16)
    dtot, dgain, dshift = norm_back(cot_ref[...].astype(f32), unit, rate, gain)
    dy = dtot.astype(bf16)
    dy_ref[...] = dy
    dvec_ref[...] = jnp.zeros_like(dvec_ref)
    dvec_ref[row + 4 : row + 5, :] = jnp.sum(dy.astype(f32), axis=0, keepdims=True)
    dvec_ref[row + 5 : row + 6, :] = dgain
    dvec_ref[row + 6 : row + 7, :] = dshift
    y_ref[...] = dtot
    place(xt_ref, x_ref[...].T, me)
    place(dyt_ref, dy.T, me)

    def leaving(i):
        cols = pl.ds(pl.multiple_of(i * chunk, 128), chunk)
        return (
            pltpu.make_async_copy(keep_ref.at[:, cols], far_keep_ref.at[:, cols], out_sems.at[i, 0]),
            pltpu.make_async_copy(send_ref.at[:, cols], far_send_ref.at[:, cols], out_sems.at[i, 1]),
        )

    def back(i, carry):
        cols = pl.ds(pl.multiple_of(i * chunk, 128), chunk)
        dpre = (nn(dy_ref[...], m_ref[1, :, cols]) * gp_ref[:, cols]).astype(bf16)
        dpre_ref[:, cols] = dpre
        dbup_ref[:, cols] = jnp.sum(dpre.astype(f32), axis=0, keepdims=True)
        put(keep_ref, send_ref, 0, 2 * block, cols, nn(xt_ref[...], dpre))
        put(keep_ref, send_ref, block, 2 * block, cols, nn(dyt_ref[...], h_ref[:, cols]))
        for copy in leaving(i):
            copy.start()
        return carry

    lax.fori_loop(0, hidden // chunk, back, 0)
    for i in range(parts):
        dvec_ref[row + i : row + i + 1, :] = dbup_ref[:, i * width : (i + 1) * width]

    def rows(i, carry):
        cols = pl.ds(pl.multiple_of(i * 256, 128), 256)
        acc_ref[:, cols] = nt(dpre_ref[...], m_ref[0, pl.ds(pl.multiple_of(i * 256, 16), 256), :])
        return carry

    lax.fori_loop(0, width // 256, rows, 0)
    unit2, rate2 = norm_parts(tot_ref[...])
    dtot2, dgain2, dshift2 = norm_back(acc_ref[...] + y_ref[...], unit2, rate2, vec(vec_ref, self_row + 3))
    dtot_ref[...] = dtot2
    dvec_ref[self_row + 3 : self_row + 4, :] = dgain2
    dvec_ref[self_row + 4 : self_row + 5, :] = dshift2
    for i in range(hidden // chunk):
        settle(leaving(i))


def column_sum(low):
    return jnp.sum(low.astype(f32), axis=0, keepdims=True)


def self_backward_kernel(
    row, blocks, swaps, count,
    me_ref, dtot_ref, tot_ref, vec_ref, q_ref, k_ref, v_ref, p_ref, c_ref, *refs,
):
    parts = refs[:count]
    out_ref, keep_ref, send_ref, dvec_ref, dq_ref, dk_ref, dv_ref, dc_ref, xt_ref, ct_ref, w_ref, sems = refs[count:]
    me = me_ref[0] if swaps else None
    copies = fetch(parts, me, w_ref, sems)
    da = dtot_ref[...].astype(bf16)
    dvec_ref[...] = jnp.zeros_like(dvec_ref)
    dvec_ref[row + 2 : row + 3, :] = column_sum(da)
    place(ct_ref, c_ref[...].T, me)
    width = w_ref.shape[2]
    every = pl.ds(0, width)
    block = width // SLOTS
    put(keep_ref, send_ref, 3 * block, 4 * block, every, nn(ct_ref[...], da))
    settle(copies)
    dc_ref[...] = nt(da, w_ref[3]).astype(bf16)
    heads_backward(q_ref, k_ref, v_ref, p_ref, dc_ref, dq_ref, dk_ref, dv_ref, blocks)
    unit, rate = norm_parts(tot_ref[...])
    gain = vec(vec_ref, CROSS + 3)
    low = (unit * gain + vec(vec_ref, CROSS + 4)).astype(bf16)
    place(xt_ref, low.T, me)
    dq, dk, dv = dq_ref[...], dk_ref[...], dv_ref[...]
    put(keep_ref, send_ref, 0, 4 * block, every, nn(xt_ref[...], dq))
    put(keep_ref, send_ref, block, 4 * block, every, nn(xt_ref[...], dk))
    put(keep_ref, send_ref, 2 * block, 4 * block, every, nn(xt_ref[...], dv))
    dvec_ref[row : row + 1, :] = column_sum(dq)
    dvec_ref[row + 1 : row + 2, :] = column_sum(dv)
    dx = dtot_ref[...] + nt(dq, w_ref[0]) + nt(dk, w_ref[1]) + nt(dv, w_ref[2])
    dtot, dgain, dshift = norm_back(dx, unit, rate, gain)
    out_ref[...] = dtot
    dvec_ref[CROSS + 3 : CROSS + 4, :] = dgain
    dvec_ref[CROSS + 4 : CROSS + 5, :] = dshift


def region_side_kernel(
    blocks, count,
    me_ref, dr_ref, rq_ref, rk_ref, rv_ref, rp_ref, *refs,
):
    rdq_ref, rdk_ref, rdv_ref, rpart_ref, wpart_ref, rdc_ref, w_ref, sems = refs[count:]
    settle(fetch(refs[:count], me_ref[0], w_ref, sems))
    rdc_ref[...] = nt(dr_ref[...].astype(bf16), w_ref[3]).astype(bf16)
    heads_backward(rq_ref, rk_ref, rv_ref, rp_ref, rdc_ref, rdq_ref, rdk_ref, rdv_ref, blocks)
    rpart_ref[...] = dr_ref[...] + nt(rdq_ref[...], w_ref[0])
    wpart_ref[...] = nt(rdk_ref[...], w_ref[1]) + nt(rdv_ref[...], w_ref[2])


def cross_backward_kernel(
    blocks, swaps, count,
    me_ref, dw_ref, dr_ref, words_ref, regions_ref, va_ref, vb_ref, vc_ref, vd_ref,
    wq_ref, wk_ref, wv_ref, wp_ref, wc_ref, rc_ref, rdq_ref, rdk_ref, rdv_ref, rpart_ref, wpart_ref, *refs,
):
    parts, refs = refs[:count], refs[count:]
    wout_ref, rout_ref, keep_ref, send_ref, wdq_ref, wdk_ref, wdv_ref, wdc_ref, wct_ref, rct_ref = refs[:10]
    wt_ref, rt_ref, dvec_ref, vt_ref, w_ref, sems = refs[10:]
    me = me_ref[0] if swaps else None
    copies = fetch(parts, me, w_ref, sems)
    width = w_ref.shape[2]
    every = pl.ds(0, width)
    block = width // SLOTS
    stride = 4 * block + VECTOR_ROWS
    wda, rda = dw_ref[...].astype(bf16), dr_ref[...].astype(bf16)
    dvec_ref[...] = va_ref[...] + vb_ref[...] + vc_ref[...] + vd_ref[...]
    dvec_ref[CROSS + 2 : CROSS + 3, :] = column_sum(wda) + column_sum(rda)
    place(wct_ref, wc_ref[...].T, me)
    place(rct_ref, rc_ref[...].T, me)
    put(keep_ref, send_ref, 3 * block, stride, every, nn(wct_ref[...], wda) + nn(rct_ref[...], rda))
    settle(copies)
    wdc_ref[...] = nt(wda, w_ref[3]).astype(bf16)
    heads_backward(wq_ref, wk_ref, wv_ref, wp_ref, wdc_ref, wdq_ref, wdk_ref, wdv_ref, blocks)
    place(wt_ref, words_ref[...].T, me)
    place(rt_ref, regions_ref[...].T, me)
    wdq, wdk, wdv = wdq_ref[...], wdk_ref[...], wdv_ref[...]
    rdq, rdk, rdv = rdq_ref[...], rdk_ref[...], rdv_ref[...]
    put(keep_ref, send_ref, 0, stride, every, nn(wt_ref[...], wdq) + nn(rt_ref[...], rdq))
    put(keep_ref, send_ref, block, stride, every, nn(rt_ref[...], wdk) + nn(wt_ref[...], rdk))
    put(keep_ref, send_ref, 2 * block, stride, every, nn(rt_ref[...], wdv) + nn(wt_ref[...], rdv))
    dvec_ref[CROSS : CROSS + 1, :] = column_sum(wdq) + column_sum(rdq)
    dvec_ref[CROSS + 1 : CROSS + 2, :] = column_sum(wdv) + column_sum(rdv)
    vt_ref[...] = jnp.zeros_like(vt_ref)
    for s in range(SLOTS):
        slot = slot_of(s, me) if swaps else s
        vt_ref[pl.ds(pl.multiple_of(slot * VECTOR_ROWS, 16), VECTOR_ROWS), 0:block] = dvec_ref[:, s * block : (s + 1) * block].astype(bf16)
    for j in range(SLOTS):
        dest = keep_ref if j < SLOTS // 2 else send_ref
        start = (j % (SLOTS // 2)) * stride + 4 * block
        dest[start : start + VECTOR_ROWS, :] = vt_ref[j * VECTOR_ROWS : (j + 1) * VECTOR_ROWS, :]
    wout_ref[...] = (dw_ref[...] + nt(wdq, w_ref[0]) + wpart_ref[...]).astype(bf16)
    rout_ref[...] = (rpart_ref[...] + nt(wdk, w_ref[1]) + nt(wdv, w_ref[2])).astype(bf16)


MIB = 1024 * 1024


SCALE = 20


class Far:
    def __init__(self, array):
        self.array = array


class Scalar:
    def __init__(self, array):
        self.array = array


class Sequence:
    def __init__(self):
        self.token = self.more = ()
        self.free = False

    def after(self, *arrays):
        self.more += arrays

    def __call__(self, kernel, name, outs, scratch, us, args, far_outs=(), small=False, grid=None, in_specs=None, out_specs=None):
        here, far = pl.BlockSpec(memory_space=pltpu.VMEM), pl.BlockSpec(memory_space=pl.ANY)
        if in_specs is None:
            kinds = {Far: far, Scalar: pl.BlockSpec(memory_space=pltpu.SMEM)}
            in_specs = [kinds.get(type(a), here) for a in args]
            out_specs = [far if i in far_outs else here for i in range(len(outs))]
        arrays = [a.array if isinstance(a, (Far, Scalar)) else a for a in args]
        out_shape = tuple(jax.ShapeDtypeStruct(s, d) for s, d in outs)
        moved = sum(a.size * a.dtype.itemsize for a in arrays) + sum(o.size * o.dtype.itemsize for o in out_shape)
        if grid is None:
            held = [a for a in args if not isinstance(a, (Far, Scalar))] + [jax.ShapeDtypeStruct(*o) for i, o in enumerate(outs) if i not in far_outs]
            held += [jax.ShapeDtypeStruct(*s) for s in scratch if isinstance(s, tuple)]
            held = sum(math.prod(h.shape) * jnp.dtype(h.dtype).itemsize for h in held)
            limit = int(1.15 * held) + 2 * MIB if small else 60 * MIB
        else:
            limit = 16 * MIB if small else 60 * MIB
        token = self.token + self.more
        self.more = ()

        def body(*refs):
            kernel(*refs[: len(arrays)], *refs[len(arrays) + len(token) :])

        extra = {} if grid is None else {"grid": grid}
        got = pl.pallas_call(
            body,
            out_shape=out_shape,
            in_specs=list(in_specs) + [far] * len(token),
            out_specs=tuple(out_specs),
            scratch_shapes=[pltpu.VMEM(*s) if isinstance(s, tuple) else s for s in scratch],
            compiler_params=pltpu.CompilerParams(vmem_limit_bytes=limit),
            cost_estimate=pl.CostEstimate(flops=int(us * SCALE * 1.15e9), bytes_accessed=0, transcendentals=0),
            name=name,
            **extra,
        )(*arrays, *token)
        self.token = () if self.free else (min(got, key=lambda o: o.size * o.dtype.itemsize),)
        return got


def fetch(parts, me, w_ref, sems, vector_parts=(), vt_ref=None):
    copies = []

    def start(source, dest):
        copies.append(pltpu.make_async_copy(source, dest, sems.at[len(copies)]))
        copies[-1].start()

    if len(parts) == 1:
        for m in range(4):
            start(parts[0].at[m], w_ref.at[m])
        return copies
    block = w_ref.shape[1] // SLOTS
    for other in range(2):
        odd = ((me & 1) ^ other) == 1
        for i in range(4):
            k = jnp.where(odd, (i & 1) * 4 + (i >> 1) * 2, (i & 1) * 2 + (i >> 1) * 4) + other
            rows = pl.ds(pl.multiple_of((k ^ me) * block, 16), block)
            for m in range(4):
                start(parts[other].at[i, pl.ds(m * block, block)], w_ref.at[m, rows, :])
            if vt_ref is not None:
                start(vector_parts[other].at[i], vt_ref.at[k])
    return copies


def settle(copies):
    for copy in copies:
        copy.wait()


def kept_shapes(nq, nk, width, bias):
    blocks, qb, kb = bias.shape
    return [((nq, width), bf16), ((nk, width), bf16), ((nk, width), bf16), ((blocks * HEADS, qb, kb), bf16), ((nq, width), bf16)]


def attention_scratch(width):
    return [((4, width, width), bf16), pltpu.SemaphoreType.DMA((40,))]


def fars(parts):
    return [Far(p) for p in parts]


def cross_forward(run, me, words, regions, parts, vectors, vector_parts, wr, rw):
    nw, nr, width = words.shape[0], regions.shape[0], words.shape[1]
    outs = [((nw, width), f32), ((nr, width), f32)] + kept_shapes(nw, nr, width, wr) + kept_shapes(nr, nw, width, rw)
    outs += [((VECTOR_ROWS, width), f32)]
    scratch = attention_scratch(width)
    scratch.insert(1, ((SLOTS, VECTOR_ROWS, 128), bf16))
    args = (Scalar(me), words, regions, vectors, wr, rw, *fars(vector_parts), *fars(parts))
    got = run(partial(cross_forward_kernel, len(parts)), "cross_forward", outs, scratch, 0.05, args)
    return got[0], got[1], got[2:7], got[7:12], got[12]


def self_forward(run, row, me, total, parts, vectors, bias):
    n, width = total.shape
    outs = [((n, width), f32)] + kept_shapes(n, n, width, bias)
    args = (Scalar(me), total, vectors, bias, *fars(parts))
    kernel = partial(self_forward_kernel, row, len(parts))
    got = run(kernel, "self_forward", outs, attention_scratch(width), 0.05, args)
    return got[0], got[1:]


def feed_both(run, self_row, row, swaps, me, total, cot, m, vectors):
    n, width = total.shape
    hidden = m.shape[2]
    chunk = 512
    half = (width, hidden)
    outs = [((n, width), bf16), ((n, width), f32), (half, bf16), (half, bf16), ((VECTOR_ROWS, width), f32)]
    scratch = [
        ((n, width), bf16), ((n, width), f32), ((n, hidden), bf16), ((n, hidden), f32), ((n, hidden), bf16),
        ((n, width), bf16), ((width, n), bf16), ((width, n), bf16), ((n, width), f32), ((1, hidden), f32), ((1, hidden), f32),
        ((2, width, hidden), bf16), (half, bf16), (half, bf16),
        pltpu.SemaphoreType.DMA((2,)), pltpu.SemaphoreType.DMA((hidden // chunk, 2)),
    ]
    args = (Scalar(me), total, cot, Far(m), vectors)
    return run(partial(feed_kernel, self_row, row, chunk, swaps), "feed", outs, scratch, 10 + n / 24, args, far_outs=(2, 3))


def self_backward(run, row, blocks, swaps, me, dtot, total, parts, vectors, kept):
    n, width = total.shape
    half = (2 * width, width)
    outs = [((n, width), f32), (half, bf16), (half, bf16), ((VECTOR_ROWS, width), f32)]
    scratch = [((n, width), bf16)] * 4 + [((width, n), bf16)] * 2 + attention_scratch(width)
    args = (Scalar(me), dtot, total, vectors, *kept, *fars(parts))
    kernel = partial(self_backward_kernel, row, blocks, swaps, len(parts))
    return run(kernel, "self_backward", outs, scratch, 8 + n / 40, args)


def region_side(run, blocks, me, dr, parts, kept):
    nr, width = dr.shape
    nw = kept[1].shape[0]
    outs = [((nr, width), bf16), ((nw, width), bf16), ((nw, width), bf16), ((nr, width), f32), ((nw, width), f32)]
    scratch = [((nr, width), bf16)] + attention_scratch(width)
    args = (Scalar(me), dr, *kept[:4], *fars(parts))
    return run(partial(region_side_kernel, blocks, len(parts)), "region_side", outs, scratch, 14, args)


def cross_backward(run, blocks, swaps, me, dw, dr, words, regions, parts, dvecs, word_kept, region_ctx, region_grads):
    nw, nr, width = words.shape[0], regions.shape[0], words.shape[1]
    half = (2 * width + VECTOR_ROWS * (SLOTS // 2), width)
    outs = [((nw, width), bf16), ((nr, width), bf16), (half, bf16), (half, bf16)]
    scratch = [((nw, width), bf16), ((nr, width), bf16), ((nr, width), bf16), ((nw, width), bf16)]
    scratch += [((width, nw), bf16), ((width, nr), bf16)] * 2
    scratch += [((VECTOR_ROWS, width), f32), ((VECTOR_ROWS * SLOTS, width), bf16)] + attention_scratch(width)
    args = (Scalar(me), dw, dr, words, regions, *dvecs, *word_kept, region_ctx, *region_grads, *fars(parts))
    return run(partial(cross_backward_kernel, blocks, swaps, len(parts)), "cross_backward", outs, scratch, 20, args)


def join_pieces(run, pairs, along=()):
    outs = [((2 * p.shape[0], *p.shape[1:]), p.dtype) for p, _ in pairs] + [(a.shape, a.dtype) for a in along]
    arrays = [a for pair in pairs for a in pair] + list(along)

    def kernel(*refs):
        taken, given = refs[: len(arrays)], refs[len(arrays) :]
        for i, (p, _) in enumerate(pairs):
            n = p.shape[0]
            given[i][:n] = taken[2 * i][...]
            given[i][n:] = taken[2 * i + 1][...]
        for i in range(len(along)):
            given[len(pairs) + i][...] = taken[2 * len(pairs) + i][...]

    return run(kernel, "join_pieces", outs, [], 2, arrays, small=True)


def plus(left, right):
    return (left.astype(f32) + right.astype(f32)).astype(bf16)


def columns_of(width):
    return width // 4 if width % 512 == 0 else width // 3


def add_halves(run, keep, got):
    rows, width = keep.shape
    c = columns_of(width)
    half = rows // 2

    def kernel(keep_ref, got_ref, held_ref, sent_ref):
        held_ref[...] = plus(keep_ref[:half, :], got_ref[:half, :])
        sent_ref[...] = plus(keep_ref[half:, :], got_ref[half:, :])

    def block(n):
        return pl.BlockSpec((n, c), lambda i: (0, i))

    outs = [((half, width), bf16)] * 2
    return run(kernel, "add_halves", outs, [], 6, (keep, got), small=keep.size < MIB, grid=(width // c,), in_specs=[block(rows)] * 2, out_specs=[block(half)] * 2)


def padded(rows):
    return -(-rows // 64) * 64


def add_last(run, z, held, back):
    n, width = held.shape
    rows = padded(n)

    def fill(held_ref, back_ref, ref):
        ref[:n, :] = plus(held_ref[...], back_ref[...])
        if rows > n:
            ref[n:, :] = jnp.zeros((rows - n, width), bf16)

    if z is None:
        return run(fill, "add_last", [((rows, width), bf16)], [], 2.5, (held, back), small=True)[0]

    def kernel(z_ref, held_ref, back_ref, keep_ref, send_ref, all_ref):
        fill(held_ref, back_ref, all_ref)
        split_rows(all_ref, z_ref[0] & 1, keep_ref, send_ref)

    outs = [((rows // 2, width), bf16)] * 2
    return run(kernel, "add_last", outs, [((rows, width), bf16)], 2.5, (Scalar(z), held, back), small=True)


def split_rows(all_ref, bit, keep_ref, send_ref):
    half = all_ref.shape[0] // 2
    keep_ref[...] = all_ref[pl.ds(pl.multiple_of(bit * half, 16), half), :]
    send_ref[...] = all_ref[pl.ds(pl.multiple_of((1 - bit) * half, 16), half), :]


def join_rows(own, other, bit, all_ref):
    half = own.shape[0]
    all_ref[pl.ds(pl.multiple_of(bit * half, 16), half), :] = own[...]
    all_ref[pl.ds(pl.multiple_of((1 - bit) * half, 16), half), :] = other[...]


def replicas_halve(run, z, held, back):
    rows, width = held.shape

    def kernel(z_ref, held_ref, back_ref, keep_ref, send_ref, all_ref):
        all_ref[...] = plus(held_ref[...], back_ref[...])
        split_rows(all_ref, (z_ref[0] >> 1) & 1, keep_ref, send_ref)

    outs = [((rows // 2, width), bf16)] * 2
    return run(kernel, "replicas_halve", outs, [((rows, width), bf16)], 2, (Scalar(z), held, back), small=True)


def replicas_sum(run, held, back):
    def kernel(held_ref, back_ref, out_ref):
        out_ref[...] = plus(held_ref[...], back_ref[...])

    return run(kernel, "replicas_sum", [(held.shape, bf16)], [], 1.7, (held, back), small=True)[0]


def replicas_join(run, z, own, other):
    rows, width = own.shape

    def kernel(z_ref, own_ref, other_ref, out_ref):
        join_rows(own_ref, other_ref, (z_ref[0] >> 1) & 1, out_ref)

    return run(kernel, "replicas_join", [((2 * rows, width), bf16)], [], 1.7, (Scalar(z), own, other), small=True)[0]


def shard_out(all_ref, share, refs):
    count = refs[0].shape[0]
    for m in range(count):
        refs[0][m] = all_ref[m * share : (m + 1) * share, :].astype(f32)
    if len(refs) == 2:
        refs[1][...] = all_ref[count * share : count * share + VECTOR_ROWS, :].astype(f32)


def shard_shapes(kind, share, width):
    if kind == "feed":
        return [((2, share, width), f32)]
    outs = [((4, share, width), f32)]
    return outs + [((VECTOR_ROWS, width), f32)] if kind == "cross" else outs


def shard_of_sum(run, kind, share, summed):
    def kernel(all_ref, *refs):
        shard_out(all_ref, share, refs)

    return run(kernel, "shard", shard_shapes(kind, share, summed.shape[1]), [], 2.5, (summed,), small=True)


def shard_of_halves(run, kind, share, z, own, other):
    rows, width = own.shape

    def kernel(z_ref, own_ref, other_ref, *refs):
        all_ref = refs[-1]
        join_rows(own_ref, other_ref, z_ref[0] & 1, all_ref)
        shard_out(all_ref, share, refs[:-1])

    return run(kernel, "shard", shard_shapes(kind, share, width), [((2 * rows, width), bf16)], 2.5, (Scalar(z), own, other), small=True)


def block_bias(query_slots, key_slots, key_bias, blocks):
    items = key_bias.shape[0] // blocks
    rows = jnp.arange(items * query_slots) // query_slots
    cols = jnp.arange(items * key_slots) // key_slots
    same = rows[:, None] == cols[None, :]
    return jnp.where(same[None], key_bias.reshape(blocks, 1, items * key_slots), -1e30).astype(f32)


def exchange(value, step):
    def partner(i):
        if step == 0:
            return i ^ 1
        return i ^ (2 if (step == 1) == (i % 2 == 0) else 4)

    return lax.ppermute(value, "fsdp", [(i, partner(i)) for i in range(SLOTS)])


def replica_exchange(value, bit):
    return lax.ppermute(value, "dp", [(i, i ^ (1 << bit)) for i in range(4)])


class Gather:
    def __init__(self, run, *shards):
        self.run = run
        self.pieces = [shard.reshape(1, -1, shard.shape[-1]) for shard in shards]
        self.got = [exchange(p, 1) for p in self.pieces]

    def join(self, along):
        joined = join_pieces(self.run, list(zip(self.pieces, self.got)), along)
        self.pieces = joined[: len(self.pieces)]
        return joined[len(self.pieces) :]

    def step(self, *along):
        later = self.join(along)
        self.got = [exchange(p, 2) for p in self.pieces]
        return later

    def finish(self, *along):
        later = self.join(along)
        return [(p, exchange(p, 0)) for p in self.pieces], later


class Reduction:
    def __init__(self, run, kind, share, z, keep, send, by_exchange):
        self.run, self.kind, self.share, self.z, self.by_exchange = run, kind, share, z, by_exchange
        self.state = (keep, exchange(send, 0))

    def first(self):
        held, sent = add_halves(self.run, *self.state)
        self.state = (held, exchange(sent, 1))

    def second(self):
        held, sent = add_halves(self.run, *self.state)
        self.state = (held, exchange(sent, 2))

    def last(self):
        if not self.by_exchange:
            self.state = lax.psum(add_last(self.run, None, *self.state), "dp")
            return
        held, sent = add_last(self.run, self.z, *self.state)
        self.state = (held, replica_exchange(sent, 0))

    def halve(self):
        held, sent = replicas_halve(self.run, self.z, *self.state)
        self.state = (held, replica_exchange(sent, 1))

    def sum(self):
        own = replicas_sum(self.run, *self.state)
        self.state = (own, replica_exchange(own, 1))

    def join(self):
        own = replicas_join(self.run, self.z, *self.state)
        self.state = (own, replica_exchange(own, 0))

    def out(self):
        if self.by_exchange:
            return shard_of_halves(self.run, self.kind, self.share, self.z, *self.state)
        return shard_of_sum(self.run, self.kind, self.share, self.state)


def unswapped(keep, send, block, count):
    width, wide = block * SLOTS, keep.shape[1]
    rows = jnp.concatenate([keep, send]).reshape(SLOTS, -1, wide)
    matrices = rows[:, : count * block].reshape(SLOTS, count, block, wide).transpose(1, 0, 2, 3).reshape(count, width, wide)
    pieces = [lax.psum_scatter(matrices, "fsdp", scatter_dimension=1, tiled=True)]
    if rows.shape[1] > count * block:
        vectors = rows[:, count * block :, :block].transpose(1, 0, 2).reshape(VECTOR_ROWS, width)
        pieces.append(lax.psum_scatter(vectors, "fsdp", scatter_dimension=1, tiled=True))
    return [piece.astype(f32) for piece in lax.psum(pieces, "dp")]


def local(
    words_in, regions_in, word_mask, region_count,
    cross_matrices, cross_vectors, word_self_matrices, word_self_vectors,
    region_self_matrices, region_self_vectors, word_feed_matrices, word_feed_vectors,
    region_feed_matrices, region_feed_vectors, words_cotangent, regions_cotangent,
):
    items, words, width = words_in.shape
    regions = regions_in.shape[1]
    share = cross_matrices.shape[1]
    count = width // share
    blocks = 3 if items % 12 == 0 else 1
    swaps = count == SLOTS
    me = lax.axis_index("fsdp").astype(jnp.int32).reshape(1)
    z = lax.axis_index("dp").astype(jnp.int32).reshape(1)

    own = jnp.concatenate([cross_vectors, word_self_vectors, region_self_vectors, word_feed_vectors, region_feed_vectors], axis=0)
    def whole(shard):
        return lax.all_gather(shard, "fsdp", axis=1, tiled=True)

    run = Sequence()

    word_bias = (word_mask.astype(f32) - 1.0) * 10000.0
    region_bias = jnp.where(jnp.arange(regions)[None, :] < region_count[:, None], 0.0, negative).astype(f32)
    word_rows = words_in.reshape(-1, width)
    region_rows = regions_in.reshape(-1, width)
    wr = block_bias(words, regions, region_bias, blocks)
    rw = block_bias(regions, words, word_bias, blocks)
    ww = block_bias(words, words, word_bias, blocks)
    rr = block_bias(regions, regions, region_bias, blocks)

    block = width // SLOTS
    word_cot = words_cotangent.reshape(-1, width)
    region_cot = regions_cotangent.reshape(-1, width)
    if swaps:
        own = jnp.pad(own, ((0, VECTOR_ROWS - own.shape[0]), (0, 128 - share)))
        cross_gather = Gather(run, cross_matrices, own)
        region_gather = Gather(run, region_self_matrices)
        (region_feed_shard,) = cross_gather.step(region_feed_matrices)
        region_gather.step()
        run.after(wr, rw, ww, rr, word_rows, region_rows, word_cot, region_cot)
        (cross, vector_parts), (word_feed_shard,) = cross_gather.finish(word_feed_matrices)
        region_feed, word_feed = whole(region_feed_shard), whole(word_feed_shard)
        vectors = jnp.zeros((8, 128), bf16)
    else:
        own = jnp.pad(own, ((0, VECTOR_ROWS - own.shape[0]), (0, 0)))
        vectors, vector_parts = lax.all_gather(own, "fsdp", axis=1, tiled=True), ()
        cross, region_self, word_self = ((whole(w),) for w in (cross_matrices, region_self_matrices, word_self_matrices))
        region_feed, word_feed = whole(region_feed_matrices), whole(word_feed_matrices)

    def reduction(kind, keep, send, by_exchange):
        return Reduction(run, kind, share, z, keep, send, by_exchange and lax.axis_size("dp") == 4) if swaps else None

    def step(group, name):
        return getattr(group, name)() if swaps else None

    word_one, region_one, word_kept, region_kept, vectors = cross_forward(run, me, word_rows, region_rows, cross, vectors, vector_parts, wr, rw)
    if swaps:
        ((region_self,), (word_shard,)) = region_gather.finish(word_self_matrices)
        word_gather = Gather(run, word_shard)
    region_two, region_self_kept = self_forward(run, REGION_SELF, me, region_one, region_self, vectors, rr)

    if swaps:
        word_gather.step()
    regions_out, region_dtwo, keep_rf, send_rf, dvec_a = feed_both(
        run, REGION_SELF, REGION_FEED, swaps, me, region_two, region_cot, region_feed, vectors
    )
    if swaps:
        ((word_self,), _) = word_gather.finish()
    rf = reduction("feed", keep_rf, send_rf, False)
    region_done, keep_rs, send_rs, dvec_b = self_backward(
        run, REGION_SELF, blocks, swaps, me, region_dtwo, region_one, region_self, vectors, region_self_kept
    )
    rs = reduction("self", keep_rs, send_rs, True)
    step(rf, "first")
    word_two, word_self_kept = self_forward(run, WORD_SELF, me, word_one, word_self, vectors, ww)
    words_out, word_dtwo, keep_wf, send_wf, dvec_c = feed_both(
        run, WORD_SELF, WORD_FEED, swaps, me, word_two, word_cot, word_feed, vectors
    )
    wf = reduction("feed", keep_wf, send_wf, True)
    step(rs, "first")
    step(rf, "second")
    step(wf, "first")
    region_grads = region_side(run, blocks, me, region_done, cross, region_kept)
    step(rf, "last")
    step(rs, "second")
    word_done, keep_ws, send_ws, dvec_d = self_backward(
        run, WORD_SELF, blocks, swaps, me, word_dtwo, word_one, word_self, vectors, word_self_kept
    )
    ws = reduction("self", keep_ws, send_ws, True)
    step(wf, "second")
    step(rs, "last")
    words_grad, regions_grad, keep_cr, send_cr = cross_backward(
        run, blocks, swaps, me, word_done, region_done, word_rows, region_rows, cross,
        (dvec_a, dvec_b, dvec_c, dvec_d), word_kept, region_kept[4], region_grads,
    )
    cr = reduction("cross", keep_cr, send_cr, True)

    if swaps:
        ws.first()
        wf.last()
        rs.halve()
        cr.first()
        ws.second()
        wf.halve()
        rs.sum()
        (grad_rf,) = rf.out()
        cr.second()
        ws.last()
        wf.sum()
        rs.join()
        cr.last()
        ws.halve()
        wf.join()
        (grad_rs,) = rs.out()
        cr.halve()
        ws.sum()
        (grad_wf,) = wf.out()
        cr.sum()
        ws.join()
        cr.join()
        (grad_ws,) = ws.out()
        grad_cr, vector_sum = cr.out()
        vector_sum = vector_sum[:, :share]
    else:
        (grad_rf,), (grad_wf,) = unswapped(keep_rf, send_rf, block, 2), unswapped(keep_wf, send_wf, block, 2)
        (grad_rs,), (grad_ws,) = unswapped(keep_rs, send_rs, block, 4), unswapped(keep_ws, send_ws, block, 4)
        grad_cr, vector_sum = unswapped(keep_cr, send_cr, block, 4)

    def rows_of(start, number):
        return vector_sum[start : start + number]

    return (
        words_out.reshape(items, words, width),
        regions_out.reshape(items, regions, width),
        words_grad.reshape(items, words, width),
        regions_grad.reshape(items, regions, width),
        grad_cr,
        rows_of(CROSS, 5),
        grad_ws,
        rows_of(WORD_SELF, 5),
        grad_rs,
        rows_of(REGION_SELF, 5),
        grad_wf,
        rows_of(WORD_FEED, 7),
        grad_rf,
        rows_of(REGION_FEED, 7),
    )


def solution(mesh):
    items = P(("dp", "fsdp"), None, None)
    matrix = P(None, "fsdp", None)
    vector = P(None, "fsdp")
    weights = (matrix, vector) * 5
    return jax.shard_map(
        local,
        mesh=mesh,
        in_specs=(items, items, P(("dp", "fsdp"), None), P(("dp", "fsdp")), *weights, items, items),
        out_specs=(items,) * 4 + weights,
        check_vma=False,
    )
```

```python
from functools import partial
import math

import jax
import jax.numpy as jnp
from jax import lax
from jax.sharding import PartitionSpec as P
from jax.experimental import pallas as pl
from jax.experimental.pallas import tpu as pltpu

HEADS = 12
epsilon = 1e-12
negative = -10000.0
bf16 = jnp.bfloat16
f32 = jnp.float32

CROSS, WORD_SELF, REGION_SELF, WORD_FEED, REGION_FEED = 0, 5, 10, 15, 22
VECTOR_ROWS = 32


def nn(left, right):
    return jnp.dot(left, right, preferred_element_type=f32)


def nt(left, right):
    return lax.dot_general(left, right, (((1,), (1,)), ((), ())), preferred_element_type=f32)


def tn(left, right):
    return lax.dot_general(left, right, (((0,), (0,)), ((), ())), preferred_element_type=f32)


def norm_parts(total):
    centred = total - jnp.mean(total, axis=-1, keepdims=True)
    spread = jnp.mean(centred * centred, axis=-1, keepdims=True)
    rate = lax.rsqrt(spread + epsilon)
    return centred * rate, rate


def norm_back(grad, unit, rate, gain):
    scaled = grad * gain
    mean_one = jnp.mean(scaled, axis=-1, keepdims=True)
    mean_two = jnp.mean(scaled * unit, axis=-1, keepdims=True)
    return (
        rate * (scaled - mean_one - unit * mean_two),
        jnp.sum(grad * unit, axis=0, keepdims=True),
        jnp.sum(grad, axis=0, keepdims=True),
    )


def half_masks(rows):
    lane = lax.broadcasted_iota(jnp.int32, (rows, 128), 1)
    return (lane < 64, lane >= 64)


def heads_forward(q_ref, k_ref, v_ref, bias_ref, probs_ref, ctx_ref):
    blocks, qb, kb = bias_ref.shape
    pairs = q_ref.shape[1] // 128
    masks = half_masks(kb)
    zero = jnp.zeros((kb, 128), bf16)

    def block(b, carry):
        rq = pl.ds(pl.multiple_of(b * qb, 16), qb)
        rk = pl.ds(pl.multiple_of(b * kb, 16), kb)
        bias = bias_ref[b]
        for p in range(pairs):
            cols = pl.ds(p * 128, 128)
            qp = q_ref[rq, cols]
            kp = k_ref[rk, cols]
            vp = v_ref[rk, cols]
            mixed = None
            for half in range(2):
                s = nt(qp, jnp.where(masks[half], kp, zero)) * 0.125 + bias
                e = jnp.exp(s - jnp.max(s, axis=-1, keepdims=True))
                low = (e / jnp.sum(e, axis=-1, keepdims=True)).astype(bf16)
                probs_ref[b * (2 * pairs) + 2 * p + half] = low
                part = nn(low, jnp.where(masks[half], vp, zero))
                mixed = part if mixed is None else mixed + part
            ctx_ref[rq, cols] = mixed.astype(bf16)
        return carry

    lax.fori_loop(0, blocks, block, 0, unroll=True)


def heads_backward(q_ref, k_ref, v_ref, probs_ref, dctx_ref, dq_ref, dk_ref, dv_ref, blocks):
    qb = q_ref.shape[0] // blocks
    kb = k_ref.shape[0] // blocks
    pairs = q_ref.shape[1] // 128
    kmasks, qmasks = half_masks(kb), half_masks(qb)
    kzero, qzero = jnp.zeros((kb, 128), bf16), jnp.zeros((qb, 128), bf16)

    def block(b, carry):
        rq = pl.ds(pl.multiple_of(b * qb, 16), qb)
        rk = pl.ds(pl.multiple_of(b * kb, 16), kb)
        for p in range(pairs):
            cols = pl.ds(p * 128, 128)
            qp = q_ref[rq, cols]
            kp = k_ref[rk, cols]
            vp = v_ref[rk, cols]
            dc = dctx_ref[rq, cols]
            dq = dk = dv = 0.0
            for half in range(2):
                low = probs_ref[b * (2 * pairs) + 2 * p + half]
                probs = low.astype(f32)
                dp = nt(dc, jnp.where(kmasks[half], vp, kzero))
                dv = dv + tn(low, jnp.where(qmasks[half], dc, qzero))
                t = probs * dp
                ds = (t - probs * jnp.sum(t, axis=-1, keepdims=True)).astype(bf16)
                dq = dq + nn(ds, jnp.where(kmasks[half], kp, kzero))
                dk = dk + tn(ds, jnp.where(qmasks[half], qp, qzero))
            dq_ref[rq, cols] = (dq * 0.125).astype(bf16)
            dk_ref[rk, cols] = (dk * 0.125).astype(bf16)
            dv_ref[rk, cols] = dv.astype(bf16)
        return carry

    lax.fori_loop(0, blocks, block, 0, unroll=True)


def vec(vec_ref, row):
    return vec_ref[row : row + 1, :]


def attend(moves, x_low, c_low, base, w_ref, vec_ref, row, bias_ref, q_ref, k_ref, v_ref, probs_ref, ctx_ref):
    q_ref[...] = (nn(x_low, w_ref[0]) + vec(vec_ref, row)).astype(bf16)
    k_ref[...] = nn(c_low, w_ref[1]).astype(bf16)
    v_ref[...] = (nn(c_low, w_ref[2]) + vec(vec_ref, row + 1)).astype(bf16)
    moves.leave(q_ref, k_ref, v_ref)
    heads_forward(q_ref, k_ref, v_ref, bias_ref, probs_ref, ctx_ref)
    moves.leave(probs_ref, ctx_ref)
    return base + nn(ctx_ref[...], w_ref[3]) + vec(vec_ref, row + 2)


def cross_forward_kernel(count, moves, me_ref, words_ref, regions_ref, known_ref, wr_ref, rw_ref, *refs):
    vector_parts, refs = (refs[:2], refs[2:]) if count == 2 else ((), refs)
    parts, refs = refs[:count], refs[count:]
    wtot_ref, rtot_ref, wq_ref, wk_ref, wv_ref, wp_ref, wc_ref, rq_ref, rk_ref, rv_ref, rp_ref, rc_ref = refs[:12]
    vec_ref, w_ref, vt_ref, sems = refs[12:]
    copies = fetch(parts, me_ref[0], w_ref, sems, vector_parts, vt_ref)
    moves.arrive()
    settle(copies)
    if count == 1:
        vec_ref[...] = known_ref[...].astype(f32)
    else:
        block = w_ref.shape[1] // SLOTS
        for s in range(SLOTS):
            vec_ref[:, s * block : (s + 1) * block] = vt_ref[s ^ me_ref[0]][:, :block].astype(f32)
    words, regions = words_ref[...], regions_ref[...]
    wtot_ref[...] = attend(moves, words, regions, words.astype(f32), w_ref, vec_ref, CROSS, wr_ref, wq_ref, wk_ref, wv_ref, wp_ref, wc_ref)
    moves.leave(wtot_ref)
    rtot_ref[...] = attend(moves, regions, words, regions.astype(f32), w_ref, vec_ref, CROSS, rw_ref, rq_ref, rk_ref, rv_ref, rp_ref, rc_ref)


def self_forward_kernel(row, count, moves, me_ref, tot_ref, vec_ref, bias_ref, *refs):
    parts = refs[:count]
    out_ref, q_ref, k_ref, v_ref, p_ref, c_ref, w_ref, sems = refs[count:]
    copies = fetch(parts, me_ref[0], w_ref, sems)
    moves.arrive()
    unit, _ = norm_parts(tot_ref[...])
    y = unit * vec(vec_ref, CROSS + 3) + vec(vec_ref, CROSS + 4)
    low = y.astype(bf16)
    settle(copies)
    out_ref[...] = attend(moves, low, low, y, w_ref, vec_ref, row, bias_ref, q_ref, k_ref, v_ref, p_ref, c_ref)


def gelu_parts(x):
    size = jnp.abs(x)
    e = jnp.exp(x * x * -0.5)
    t = 1.0 / (1.0 + (0.3275911 * 0.7071067811865476) * size)
    poly = t * (0.127414796 + t * (-0.142248368 + t * (0.7107068705 + t * (-0.7265760135 + t * 0.5307027145))))
    tail = poly * e
    phi = jnp.where(x >= 0, 1.0 - tail, tail)
    return x * phi, phi + x * e * 0.3989422804014327


def slot_of(s, me):
    k = s ^ me
    core, x, y = k & 1, (k >> 1) & 1, (k >> 2) & 1
    flip = (me & 1) ^ core
    return core * 4 + jnp.where(flip == 0, x * 2 + y, y * 2 + x)


def place(dest_ref, value, me):
    if me is None:
        dest_ref[...] = value
        return
    rows = value.shape[0] // SLOTS
    for s in range(SLOTS):
        dest_ref[pl.ds(pl.multiple_of(slot_of(s, me) * rows, 16), rows), :] = value[s * rows : (s + 1) * rows, :]


SLOTS = 8


def put(keep_ref, send_ref, base, stride, cols, value):
    rows = value.shape[0] // SLOTS
    low = value.astype(bf16)
    for j in range(SLOTS):
        dest = keep_ref if j < SLOTS // 2 else send_ref
        start = base + (j % (SLOTS // 2)) * stride
        dest[start : start + rows, cols] = low[j * rows : (j + 1) * rows]


def feed_kernel(
    self_row, row, chunk, swaps,
    moves, me_ref, tot_ref, cot_ref, far_ref, vec_ref,
    out_ref, dtot_ref, far_keep_ref, far_send_ref, dvec_ref,
    x_ref, y_ref, h_ref, gp_ref, dpre_ref, dy_ref, xt_ref, dyt_ref, acc_ref, bup_ref, dbup_ref,
    m_ref, keep_ref, send_ref, in_sems, out_sems,
):
    me = me_ref[0] if swaps else None
    copies = [pltpu.make_async_copy(far_ref.at[m], m_ref.at[m], in_sems.at[m]) for m in range(2)]
    for copy in copies:
        copy.start()
    moves.arrive()
    width = tot_ref.shape[1]
    hidden = m_ref.shape[2]
    parts = hidden // width
    block = width // SLOTS
    for i in range(parts):
        bup_ref[:, i * width : (i + 1) * width] = vec(vec_ref, row + i)
    unit2, rate2 = norm_parts(tot_ref[...])
    y = unit2 * vec(vec_ref, self_row + 3) + vec(vec_ref, self_row + 4)
    y_ref[...] = y
    x_ref[...] = y.astype(bf16)
    copies[0].wait()

    def up(i, carry):
        cols = pl.ds(pl.multiple_of(i * chunk, 128), chunk)
        pre = nn(x_ref[...], m_ref[0, :, cols]) + bup_ref[:, cols]
        value, slope = gelu_parts(pre)
        h_ref[:, cols] = value.astype(bf16)
        gp_ref[:, cols] = slope
        return carry

    lax.fori_loop(0, hidden // chunk, up, 0)
    copies[1].wait()

    def down(i, carry):
        cols = pl.ds(0, width)
        acc_ref[:, cols] = nt(h_ref[...], m_ref[1, pl.ds(0, width), :])
        return carry

    lax.fori_loop(0, 1, down, 0, unroll=True)
    gain = vec(vec_ref, row + 5)
    unit, rate = norm_parts(y_ref[...] + acc_ref[...] + vec(vec_ref, row + 4))
    out_ref[...] = (unit * gain + vec(vec_ref, row + 6)).astype(bf16)
    moves.leave(out_ref)
    dtot, dgain, dshift = norm_back(cot_ref[...].astype(f32), unit, rate, gain)
    dy = dtot.astype(bf16)
    dy_ref[...] = dy
    dvec_ref[...] = jnp.zeros_like(dvec_ref)
    dvec_ref[row + 4 : row + 5, :] = jnp.sum(dy.astype(f32), axis=0, keepdims=True)
    dvec_ref[row + 5 : row + 6, :] = dgain
    dvec_ref[row + 6 : row + 7, :] = dshift
    y_ref[...] = dtot
    place(xt_ref, x_ref[...].T, me)
    place(dyt_ref, dy.T, me)

    def leaving(i):
        cols = pl.ds(pl.multiple_of(i * chunk, 128), chunk)
        return (
            pltpu.make_async_copy(keep_ref.at[:, cols], far_keep_ref.at[:, cols], out_sems.at[i, 0]),
            pltpu.make_async_copy(send_ref.at[:, cols], far_send_ref.at[:, cols], out_sems.at[i, 1]),
        )

    def back(i, carry):
        cols = pl.ds(pl.multiple_of(i * chunk, 128), chunk)
        dpre = (nn(dy_ref[...], m_ref[1, :, cols]) * gp_ref[:, cols]).astype(bf16)
        dpre_ref[:, cols] = dpre
        dbup_ref[:, cols] = jnp.sum(dpre.astype(f32), axis=0, keepdims=True)
        put(keep_ref, send_ref, 0, 2 * block, cols, nn(xt_ref[...], dpre))
        put(keep_ref, send_ref, block, 2 * block, cols, nn(dyt_ref[...], h_ref[:, cols]))
        for copy in leaving(i):
            copy.start()
        return carry

    lax.fori_loop(0, hidden // chunk, back, 0)
    for i in range(parts):
        dvec_ref[row + i : row + i + 1, :] = dbup_ref[:, i * width : (i + 1) * width]

    def rows(i, carry):
        cols = pl.ds(0, width)
        acc_ref[:, cols] = nt(dpre_ref[...], m_ref[0, pl.ds(0, width), :])
        return carry

    lax.fori_loop(0, 1, rows, 0, unroll=True)
    unit2, rate2 = norm_parts(tot_ref[...])
    dtot2, dgain2, dshift2 = norm_back(acc_ref[...] + y_ref[...], unit2, rate2, vec(vec_ref, self_row + 3))
    dtot_ref[...] = dtot2
    dvec_ref[self_row + 3 : self_row + 4, :] = dgain2
    dvec_ref[self_row + 4 : self_row + 5, :] = dshift2
    for i in range(hidden // chunk):
        settle(leaving(i))


def column_sum(low):
    return jnp.sum(low.astype(f32), axis=0, keepdims=True)


def self_backward_kernel(
    row, blocks, swaps, count,
    moves, me_ref, dtot_ref, tot_ref, vec_ref, q_ref, k_ref, v_ref, p_ref, c_ref, *refs,
):
    parts = refs[:count]
    out_ref, keep_ref, send_ref, dvec_ref, dq_ref, dk_ref, dv_ref, dc_ref, xt_ref, ct_ref, w_ref, sems = refs[count:]
    me = me_ref[0] if swaps else None
    copies = fetch(parts, me, w_ref, sems)
    moves.arrive()
    da = dtot_ref[...].astype(bf16)
    dvec_ref[...] = jnp.zeros_like(dvec_ref)
    dvec_ref[row + 2 : row + 3, :] = column_sum(da)
    place(ct_ref, c_ref[...].T, me)
    width = w_ref.shape[2]
    every = pl.ds(0, width)
    block = width // SLOTS
    put(keep_ref, send_ref, 3 * block, 4 * block, every, nn(ct_ref[...], da))
    settle(copies)
    dc_ref[...] = nt(da, w_ref[3]).astype(bf16)
    heads_backward(q_ref, k_ref, v_ref, p_ref, dc_ref, dq_ref, dk_ref, dv_ref, blocks)
    unit, rate = norm_parts(tot_ref[...])
    gain = vec(vec_ref, CROSS + 3)
    low = (unit * gain + vec(vec_ref, CROSS + 4)).astype(bf16)
    place(xt_ref, low.T, me)
    dq, dk, dv = dq_ref[...], dk_ref[...], dv_ref[...]
    put(keep_ref, send_ref, 0, 4 * block, every, nn(xt_ref[...], dq))
    put(keep_ref, send_ref, block, 4 * block, every, nn(xt_ref[...], dk))
    put(keep_ref, send_ref, 2 * block, 4 * block, every, nn(xt_ref[...], dv))
    moves.leave(keep_ref, send_ref)
    dvec_ref[row : row + 1, :] = column_sum(dq)
    dvec_ref[row + 1 : row + 2, :] = column_sum(dv)
    dx = dtot_ref[...] + nt(dq, w_ref[0]) + nt(dk, w_ref[1]) + nt(dv, w_ref[2])
    dtot, dgain, dshift = norm_back(dx, unit, rate, gain)
    out_ref[...] = dtot
    dvec_ref[CROSS + 3 : CROSS + 4, :] = dgain
    dvec_ref[CROSS + 4 : CROSS + 5, :] = dshift


def region_side_kernel(
    blocks, count,
    moves, me_ref, dr_ref, rq_ref, rk_ref, rv_ref, rp_ref, *refs,
):
    rdq_ref, rdk_ref, rdv_ref, rpart_ref, wpart_ref, rdc_ref, w_ref, sems = refs[count:]
    copies = fetch(refs[:count], me_ref[0], w_ref, sems)
    moves.arrive()
    settle(copies)
    rdc_ref[...] = nt(dr_ref[...].astype(bf16), w_ref[3]).astype(bf16)
    heads_backward(rq_ref, rk_ref, rv_ref, rp_ref, rdc_ref, rdq_ref, rdk_ref, rdv_ref, blocks)
    moves.leave(rdq_ref, rdk_ref, rdv_ref)
    rpart_ref[...] = dr_ref[...] + nt(rdq_ref[...], w_ref[0])
    wpart_ref[...] = nt(rdk_ref[...], w_ref[1]) + nt(rdv_ref[...], w_ref[2])


def cross_backward_kernel(
    blocks, swaps, count,
    moves, me_ref, dw_ref, dr_ref, words_ref, regions_ref, va_ref, vb_ref, vc_ref, vd_ref,
    wq_ref, wk_ref, wv_ref, wp_ref, wc_ref, rc_ref, rdq_ref, rdk_ref, rdv_ref, rpart_ref, wpart_ref, *refs,
):
    parts, refs = refs[:count], refs[count:]
    wout_ref, rout_ref, keep_ref, send_ref, wdq_ref, wdk_ref, wdv_ref, wdc_ref, wct_ref, rct_ref = refs[:10]
    wt_ref, rt_ref, dvec_ref, vt_ref, w_ref, sems = refs[10:]
    me = me_ref[0] if swaps else None
    copies = fetch(parts, me, w_ref, sems)
    moves.arrive()
    width = w_ref.shape[2]
    every = pl.ds(0, width)
    block = width // SLOTS
    stride = 4 * block + VECTOR_ROWS
    wda, rda = dw_ref[...].astype(bf16), dr_ref[...].astype(bf16)
    dvec_ref[...] = va_ref[...] + vb_ref[...] + vc_ref[...] + vd_ref[...]
    dvec_ref[CROSS + 2 : CROSS + 3, :] = column_sum(wda) + column_sum(rda)
    place(wct_ref, wc_ref[...].T, me)
    place(rct_ref, rc_ref[...].T, me)
    put(keep_ref, send_ref, 3 * block, stride, every, nn(wct_ref[...], wda) + nn(rct_ref[...], rda))
    settle(copies)
    wdc_ref[...] = nt(wda, w_ref[3]).astype(bf16)
    heads_backward(wq_ref, wk_ref, wv_ref, wp_ref, wdc_ref, wdq_ref, wdk_ref, wdv_ref, blocks)
    place(wt_ref, words_ref[...].T, me)
    place(rt_ref, regions_ref[...].T, me)
    wdq, wdk, wdv = wdq_ref[...], wdk_ref[...], wdv_ref[...]
    rdq, rdk, rdv = rdq_ref[...], rdk_ref[...], rdv_ref[...]
    put(keep_ref, send_ref, 0, stride, every, nn(wt_ref[...], wdq) + nn(rt_ref[...], rdq))
    put(keep_ref, send_ref, block, stride, every, nn(rt_ref[...], wdk) + nn(wt_ref[...], rdk))
    put(keep_ref, send_ref, 2 * block, stride, every, nn(rt_ref[...], wdv) + nn(wt_ref[...], rdv))
    dvec_ref[CROSS : CROSS + 1, :] = column_sum(wdq) + column_sum(rdq)
    dvec_ref[CROSS + 1 : CROSS + 2, :] = column_sum(wdv) + column_sum(rdv)
    vt_ref[...] = jnp.zeros_like(vt_ref)
    for s in range(SLOTS):
        slot = slot_of(s, me) if swaps else s
        vt_ref[pl.ds(pl.multiple_of(slot * VECTOR_ROWS, 16), VECTOR_ROWS), 0:block] = dvec_ref[:, s * block : (s + 1) * block].astype(bf16)
    for j in range(SLOTS):
        dest = keep_ref if j < SLOTS // 2 else send_ref
        start = (j % (SLOTS // 2)) * stride + 4 * block
        dest[start : start + VECTOR_ROWS, :] = vt_ref[j * VECTOR_ROWS : (j + 1) * VECTOR_ROWS, :]
    moves.leave(keep_ref, send_ref)
    wout_ref[...] = (dw_ref[...] + nt(wdq, w_ref[0]) + wpart_ref[...]).astype(bf16)
    rout_ref[...] = (rpart_ref[...] + nt(wdk, w_ref[1]) + nt(wdv, w_ref[2])).astype(bf16)


MIB = 1024 * 1024


SCALE = 20


class Moves:
    def __init__(self, ins, outs, sems):
        self.ins = [pltpu.make_async_copy(source, dest, sems.at[i]) for i, (source, dest) in enumerate(ins)]
        self.outs = [(ref, pltpu.make_async_copy(ref, dest, sems.at[len(ins) + i])) for i, (ref, dest) in enumerate(outs)]
        self.left = set()
        for copy in self.ins:
            copy.start()

    def arrive(self):
        for copy in self.ins:
            copy.wait()

    def leave(self, *refs):
        for i, (ref, copy) in enumerate(self.outs):
            if any(ref is r for r in refs):
                copy.start()
                self.left.add(i)

    def finish(self):
        for i, (_, copy) in enumerate(self.outs):
            if i not in self.left:
                copy.start()
        for _, copy in self.outs:
            copy.wait()


class Far:
    def __init__(self, array):
        self.array = array


class Scalar:
    def __init__(self, array):
        self.array = array


class Sequence:
    def __init__(self):
        self.token = self.more = ()
        self.free = False
        self.between = True

    def after(self, *arrays):
        self.more += arrays

    def __call__(self, kernel, name, outs, scratch, us, args, far_outs=(), small=False, manual=False, grid=None, in_specs=None, out_specs=None):
        here, far = pl.BlockSpec(memory_space=pltpu.VMEM), pl.BlockSpec(memory_space=pl.ANY)
        moved_in = [i for i, a in enumerate(args) if manual and not isinstance(a, (Far, Scalar))]
        moved_out = [i for i in range(len(outs)) if manual and i not in far_outs]
        if in_specs is None:
            kinds = {Far: far, Scalar: pl.BlockSpec(memory_space=pltpu.SMEM)}
            in_specs = [kinds.get(type(a), here) for a in args]
            out_specs = [far if manual or i in far_outs else here for i in range(len(outs))]
            in_specs = [far if i in moved_in else spec for i, spec in enumerate(in_specs)]
        arrays = [a.array if isinstance(a, (Far, Scalar)) else a for a in args]
        out_shape = tuple(jax.ShapeDtypeStruct(s, d) for s, d in outs)
        moved = sum(a.size * a.dtype.itemsize for a in arrays) + sum(o.size * o.dtype.itemsize for o in out_shape)
        small = small and self.between
        if grid is None:
            held = [a for a in args if not isinstance(a, (Far, Scalar))] + [jax.ShapeDtypeStruct(*o) for i, o in enumerate(outs) if i not in far_outs]
            held += [jax.ShapeDtypeStruct(*s) for s in scratch if isinstance(s, tuple)]
            held = sum(math.prod(h.shape) * jnp.dtype(h.dtype).itemsize for h in held)
            limit = int(1.15 * held) + 2 * MIB if small else 60 * MIB
        else:
            limit = 16 * MIB if small else 60 * MIB
        token = self.token + self.more
        self.more = ()

        scratch = list(scratch)
        own = len(scratch)
        if manual:
            scratch += [(arrays[i].shape, arrays[i].dtype) for i in moved_in] + [outs[i] for i in moved_out]
            scratch.append(pltpu.SemaphoreType.DMA((len(moved_in) + len(moved_out),)))

        def body(*refs):
            taken, rest = list(refs[: len(arrays)]), refs[len(arrays) + len(token) :]
            given, rest = list(rest[: len(outs)]), rest[len(outs) :]
            if not manual:
                kernel(*taken, *given, *rest)
                return
            buffers = rest[own:]
            ins = [(taken[i], buffers[j]) for j, i in enumerate(moved_in)]
            leaving = [(buffers[len(moved_in) + j], given[i]) for j, i in enumerate(moved_out)]
            for j, i in enumerate(moved_in):
                taken[i] = buffers[j]
            for j, i in enumerate(moved_out):
                given[i] = buffers[len(moved_in) + j]
            moves = Moves(ins, leaving, buffers[-1])
            kernel(moves, *taken, *given, *rest[:own])
            moves.finish()

        extra = {} if grid is None else {"grid": grid}
        got = pl.pallas_call(
            body,
            out_shape=out_shape,
            in_specs=list(in_specs) + [far] * len(token),
            out_specs=tuple(out_specs),
            scratch_shapes=[pltpu.VMEM(*s) if isinstance(s, tuple) else s for s in scratch],
            compiler_params=pltpu.CompilerParams(vmem_limit_bytes=limit),
            cost_estimate=pl.CostEstimate(flops=int(us * SCALE * 1.15e9), bytes_accessed=0, transcendentals=0),
            name=name,
            **extra,
        )(*arrays, *token)
        self.token = () if self.free else (min(got, key=lambda o: o.size * o.dtype.itemsize),)
        return got


def fetch(parts, me, w_ref, sems, vector_parts=(), vt_ref=None):
    copies = []

    def start(source, dest):
        copies.append(pltpu.make_async_copy(source, dest, sems.at[len(copies)]))
        copies[-1].start()

    if len(parts) == 1:
        for m in range(4):
            start(parts[0].at[m], w_ref.at[m])
        return copies
    block = w_ref.shape[1] // SLOTS
    for other in range(2):
        odd = ((me & 1) ^ other) == 1
        for i in range(4):
            k = jnp.where(odd, (i & 1) * 4 + (i >> 1) * 2, (i & 1) * 2 + (i >> 1) * 4) + other
            rows = pl.ds(pl.multiple_of((k ^ me) * block, 16), block)
            for m in range(4):
                start(parts[other].at[i, pl.ds(m * block, block)], w_ref.at[m, rows, :])
            if vt_ref is not None:
                start(vector_parts[other].at[i], vt_ref.at[k])
    return copies


def settle(copies):
    for copy in copies:
        copy.wait()


def kept_shapes(nq, nk, width, bias):
    blocks, qb, kb = bias.shape
    return [((nq, width), bf16), ((nk, width), bf16), ((nk, width), bf16), ((blocks * HEADS, qb, kb), bf16), ((nq, width), bf16)]


def attention_scratch(width):
    return [((4, width, width), bf16), pltpu.SemaphoreType.DMA((40,))]


def fars(parts):
    return [Far(p) for p in parts]


def cross_forward(run, me, words, regions, parts, vectors, vector_parts, wr, rw):
    nw, nr, width = words.shape[0], regions.shape[0], words.shape[1]
    outs = [((nw, width), f32), ((nr, width), f32)] + kept_shapes(nw, nr, width, wr) + kept_shapes(nr, nw, width, rw)
    outs += [((VECTOR_ROWS, width), f32)]
    scratch = attention_scratch(width)
    scratch.insert(1, ((SLOTS, VECTOR_ROWS, 128), bf16))
    args = (Scalar(me), words, regions, vectors, wr, rw, *fars(vector_parts), *fars(parts))
    got = run(partial(cross_forward_kernel, len(parts)), "cross_forward", outs, scratch, 0.05, args, manual=True)
    return got[0], got[1], got[2:7], got[7:12], got[12]


def self_forward(run, row, me, total, parts, vectors, bias):
    n, width = total.shape
    outs = [((n, width), f32)] + kept_shapes(n, n, width, bias)
    args = (Scalar(me), total, vectors, bias, *fars(parts))
    kernel = partial(self_forward_kernel, row, len(parts))
    got = run(kernel, "self_forward", outs, attention_scratch(width), 0.05, args, manual=True)
    return got[0], got[1:]


def feed_both(run, self_row, row, swaps, me, total, cot, m, vectors):
    n, width = total.shape
    hidden = m.shape[2]
    chunk = 1536
    half = (width, hidden)
    outs = [((n, width), bf16), ((n, width), f32), (half, bf16), (half, bf16), ((VECTOR_ROWS, width), f32)]
    scratch = [
        ((n, width), bf16), ((n, width), f32), ((n, hidden), bf16), ((n, hidden), f32), ((n, hidden), bf16),
        ((n, width), bf16), ((width, n), bf16), ((width, n), bf16), ((n, width), f32), ((1, hidden), f32), ((1, hidden), f32),
        ((2, width, hidden), bf16), (half, bf16), (half, bf16),
        pltpu.SemaphoreType.DMA((2,)), pltpu.SemaphoreType.DMA((hidden // chunk, 2)),
    ]
    args = (Scalar(me), total, cot, Far(m), vectors)
    return run(partial(feed_kernel, self_row, row, chunk, swaps), "feed", outs, scratch, 10 + n / 24, args, far_outs=(2, 3), manual=True)


def self_backward(run, row, blocks, swaps, me, dtot, total, parts, vectors, kept):
    n, width = total.shape
    half = (2 * width, width)
    outs = [((n, width), f32), (half, bf16), (half, bf16), ((VECTOR_ROWS, width), f32)]
    scratch = [((n, width), bf16)] * 4 + [((width, n), bf16)] * 2 + attention_scratch(width)
    args = (Scalar(me), dtot, total, vectors, *kept, *fars(parts))
    kernel = partial(self_backward_kernel, row, blocks, swaps, len(parts))
    return run(kernel, "self_backward", outs, scratch, 8 + n / 40, args, manual=True)


def region_side(run, blocks, me, dr, parts, kept):
    nr, width = dr.shape
    nw = kept[1].shape[0]
    outs = [((nr, width), bf16), ((nw, width), bf16), ((nw, width), bf16), ((nr, width), f32), ((nw, width), f32)]
    scratch = [((nr, width), bf16)] + attention_scratch(width)
    args = (Scalar(me), dr, *kept[:4], *fars(parts))
    return run(partial(region_side_kernel, blocks, len(parts)), "region_side", outs, scratch, 14, args, manual=True)


def cross_backward(run, blocks, swaps, me, dw, dr, words, regions, parts, dvecs, word_kept, region_ctx, region_grads):
    nw, nr, width = words.shape[0], regions.shape[0], words.shape[1]
    half = (2 * width + VECTOR_ROWS * (SLOTS // 2), width)
    outs = [((nw, width), bf16), ((nr, width), bf16), (half, bf16), (half, bf16)]
    scratch = [((nw, width), bf16), ((nr, width), bf16), ((nr, width), bf16), ((nw, width), bf16)]
    scratch += [((width, nw), bf16), ((width, nr), bf16)] * 2
    scratch += [((VECTOR_ROWS, width), f32), ((VECTOR_ROWS * SLOTS, width), bf16)] + attention_scratch(width)
    args = (Scalar(me), dw, dr, words, regions, *dvecs, *word_kept, region_ctx, *region_grads, *fars(parts))
    return run(partial(cross_backward_kernel, blocks, swaps, len(parts)), "cross_backward", outs, scratch, 20, args, manual=True)


def join_pieces(run, pairs, along=()):
    outs = [((2 * p.shape[0], *p.shape[1:]), p.dtype) for p, _ in pairs] + [(a.shape, a.dtype) for a in along]
    arrays = [a for pair in pairs for a in pair] + list(along)

    def kernel(*refs):
        taken, given = refs[: len(arrays)], refs[len(arrays) :]
        for i, (p, _) in enumerate(pairs):
            n = p.shape[0]
            given[i][:n] = taken[2 * i][...]
            given[i][n:] = taken[2 * i + 1][...]
        for i in range(len(along)):
            given[len(pairs) + i][...] = taken[2 * len(pairs) + i][...]

    return run(kernel, "join_pieces", outs, [], 2, arrays, small=True)


def plus(left, right):
    return (left.astype(f32) + right.astype(f32)).astype(bf16)


def columns_of(width):
    return width // 4 if width % 512 == 0 else width // 3


def add_halves(run, keep, got):
    rows, width = keep.shape
    c = columns_of(width)
    half = rows // 2

    def kernel(keep_ref, got_ref, held_ref, sent_ref):
        held_ref[...] = plus(keep_ref[:half, :], got_ref[:half, :])
        sent_ref[...] = plus(keep_ref[half:, :], got_ref[half:, :])

    def block(n):
        return pl.BlockSpec((n, c), lambda i: (0, i))

    outs = [((half, width), bf16)] * 2
    return run(kernel, "add_halves", outs, [], 6, (keep, got), small=keep.size < MIB, grid=(width // c,), in_specs=[block(rows)] * 2, out_specs=[block(half)] * 2)


def padded(rows):
    return -(-rows // 64) * 64


def add_last(run, z, held, back):
    n, width = held.shape
    rows = padded(n)

    def fill(held_ref, back_ref, ref):
        ref[:n, :] = plus(held_ref[...], back_ref[...])
        if rows > n:
            ref[n:, :] = jnp.zeros((rows - n, width), bf16)

    if z is None:
        return run(fill, "add_last", [((rows, width), bf16)], [], 2.5, (held, back), small=True)[0]

    def kernel(z_ref, held_ref, back_ref, keep_ref, send_ref, all_ref):
        fill(held_ref, back_ref, all_ref)
        split_rows(all_ref, z_ref[0] & 1, keep_ref, send_ref)

    outs = [((rows // 2, width), bf16)] * 2
    return run(kernel, "add_last", outs, [((rows, width), bf16)], 2.5, (Scalar(z), held, back), small=True)


def add_three(run, z, first, last, halve):
    def kernel(moves, z_ref, keep_ref, got_ref, held_ref, back_ref, own_ref, other_ref, *refs):
        fh_ref, fs_ref, lk_ref, ls_ref, hk_ref, hs_ref, last_ref, halve_ref = refs
        moves.arrive()
        half = keep_ref.shape[0] // 2
        fs_ref[...] = plus(keep_ref[half:, :], got_ref[half:, :])
        moves.leave(fs_ref)
        last_ref[...] = plus(held_ref[...], back_ref[...])
        split_rows(last_ref, z_ref[0] & 1, lk_ref, ls_ref)
        moves.leave(ls_ref, lk_ref)
        halve_ref[...] = plus(own_ref[...], other_ref[...])
        split_rows(halve_ref, (z_ref[0] >> 1) & 1, hk_ref, hs_ref)
        moves.leave(hs_ref, hk_ref)
        fh_ref[...] = plus(keep_ref[:half, :], got_ref[:half, :])

    args = (Scalar(z), *first, *last, *halve)
    outs = [((pair[0].shape[0] // 2, pair[0].shape[1]), bf16) for pair in (first, first, last, last, halve, halve)]
    scratch = [(last[0].shape, bf16), (halve[0].shape, bf16)]
    got = run(kernel, "add_three", outs, scratch, 8, args, manual=True)
    return got[0:2], got[2:4], got[4:6]


def split_rows(all_ref, bit, keep_ref, send_ref):
    half = all_ref.shape[0] // 2
    keep_ref[...] = all_ref[pl.ds(pl.multiple_of(bit * half, 16), half), :]
    send_ref[...] = all_ref[pl.ds(pl.multiple_of((1 - bit) * half, 16), half), :]


def join_rows(own, other, bit, all_ref):
    half = own.shape[0]
    all_ref[pl.ds(pl.multiple_of(bit * half, 16), half), :] = own[...]
    all_ref[pl.ds(pl.multiple_of((1 - bit) * half, 16), half), :] = other[...]


def replicas_halve(run, z, held, back):
    rows, width = held.shape

    def kernel(z_ref, held_ref, back_ref, keep_ref, send_ref, all_ref):
        all_ref[...] = plus(held_ref[...], back_ref[...])
        split_rows(all_ref, (z_ref[0] >> 1) & 1, keep_ref, send_ref)

    outs = [((rows // 2, width), bf16)] * 2
    return run(kernel, "replicas_halve", outs, [((rows, width), bf16)], 2, (Scalar(z), held, back), small=True)


def replicas_sum(run, held, back):
    def kernel(held_ref, back_ref, out_ref):
        out_ref[...] = plus(held_ref[...], back_ref[...])

    return run(kernel, "replicas_sum", [(held.shape, bf16)], [], 1.7, (held, back), small=True)[0]


def replicas_join(run, z, own, other):
    rows, width = own.shape

    def kernel(z_ref, own_ref, other_ref, out_ref):
        join_rows(own_ref, other_ref, (z_ref[0] >> 1) & 1, out_ref)

    return run(kernel, "replicas_join", [((2 * rows, width), bf16)], [], 1.7, (Scalar(z), own, other), small=True)[0]


VECTOR_PARTS = ((CROSS, 5), (WORD_SELF, 5), (REGION_SELF, 5), (WORD_FEED, 7), (REGION_FEED, 7))


def shard_out(all_ref, share, refs):
    count = refs[0].shape[0]
    for m in range(count):
        refs[0][m] = all_ref[m * share : (m + 1) * share, :].astype(f32)
    if len(refs) > 1:
        vectors = all_ref[count * share : count * share + VECTOR_ROWS, :share].astype(f32)
        for ref, (start, number) in zip(refs[1:], VECTOR_PARTS):
            ref[...] = vectors[start : start + number]


def shard_shapes(kind, share, width):
    if kind == "feed":
        return [((2, share, width), f32)]
    outs = [((4, share, width), f32)]
    return outs + [((number, share), f32) for _, number in VECTOR_PARTS] if kind == "cross" else outs


def shard_of_sum(run, kind, share, summed):
    def kernel(all_ref, *refs):
        shard_out(all_ref, share, refs)

    return run(kernel, "shard", shard_shapes(kind, share, summed.shape[1]), [], 2.5, (summed,), small=True)


def shard_of_halves(run, kind, share, z, own, other):
    rows, width = own.shape

    def kernel(z_ref, own_ref, other_ref, *refs):
        all_ref = refs[-1]
        join_rows(own_ref, other_ref, z_ref[0] & 1, all_ref)
        shard_out(all_ref, share, refs[:-1])

    return run(kernel, "shard", shard_shapes(kind, share, width), [((2 * rows, width), bf16)], 2.5, (Scalar(z), own, other), small=True)


def block_bias(query_slots, key_slots, key_bias, blocks):
    items = key_bias.shape[0] // blocks
    rows = jnp.arange(items * query_slots) // query_slots
    cols = jnp.arange(items * key_slots) // key_slots
    same = rows[:, None] == cols[None, :]
    return jnp.where(same[None], key_bias.reshape(blocks, 1, items * key_slots), -1e30).astype(f32)


def exchange(value, step):
    def partner(i):
        if step == 0:
            return i ^ 1
        return i ^ (2 if (step == 1) == (i % 2 == 0) else 4)

    return lax.ppermute(value, "fsdp", [(i, partner(i)) for i in range(SLOTS)])


def replica_exchange(value, bit):
    return lax.ppermute(value, "dp", [(i, i ^ (1 << bit)) for i in range(4)])


class Gather:
    def __init__(self, run, *shards):
        self.run = run
        self.pieces = [shard.reshape(1, -1, shard.shape[-1]) for shard in shards]
        self.got = [exchange(p, 1) for p in self.pieces]

    def join(self, along):
        joined = join_pieces(self.run, list(zip(self.pieces, self.got)), along)
        self.pieces = joined[: len(self.pieces)]
        return joined[len(self.pieces) :]

    def step(self, *along):
        later = self.join(along)
        self.got = [exchange(p, 2) for p in self.pieces]
        return later

    def finish(self, *along):
        later = self.join(along)
        return [(p, exchange(p, 0)) for p in self.pieces], later


class Reduction:
    def __init__(self, run, kind, share, z, keep, send, by_exchange):
        self.run, self.kind, self.share, self.z, self.by_exchange = run, kind, share, z, by_exchange
        self.state = (keep, exchange(send, 0))

    def first(self):
        held, sent = add_halves(self.run, *self.state)
        self.state = (held, exchange(sent, 1))

    def second(self):
        held, sent = add_halves(self.run, *self.state)
        self.state = (held, exchange(sent, 2))

    def last(self):
        if not self.by_exchange:
            self.state = lax.psum(add_last(self.run, None, *self.state), "dp")
            return
        held, sent = add_last(self.run, self.z, *self.state)
        self.state = (held, replica_exchange(sent, 0))

    def halve(self):
        held, sent = replicas_halve(self.run, self.z, *self.state)
        self.state = (held, replica_exchange(sent, 1))

    def sum(self):
        own = replicas_sum(self.run, *self.state)
        self.state = (own, replica_exchange(own, 1))

    def join(self):
        own = replicas_join(self.run, self.z, *self.state)
        self.state = (own, replica_exchange(own, 0))

    def out(self):
        if self.by_exchange:
            return shard_of_halves(self.run, self.kind, self.share, self.z, *self.state)
        return shard_of_sum(self.run, self.kind, self.share, self.state)


def unswapped(keep, send, block, count):
    width, wide = block * SLOTS, keep.shape[1]
    rows = jnp.concatenate([keep, send]).reshape(SLOTS, -1, wide)
    matrices = rows[:, : count * block].reshape(SLOTS, count, block, wide).transpose(1, 0, 2, 3).reshape(count, width, wide)
    pieces = [lax.psum_scatter(matrices, "fsdp", scatter_dimension=1, tiled=True)]
    if rows.shape[1] > count * block:
        vectors = rows[:, count * block :, :block].transpose(1, 0, 2).reshape(VECTOR_ROWS, width)
        pieces.append(lax.psum_scatter(vectors, "fsdp", scatter_dimension=1, tiled=True))
    return [piece.astype(f32) for piece in lax.psum(pieces, "dp")]


def local(
    words_in, regions_in, word_mask, region_count,
    cross_matrices, cross_vectors, word_self_matrices, word_self_vectors,
    region_self_matrices, region_self_vectors, word_feed_matrices, word_feed_vectors,
    region_feed_matrices, region_feed_vectors, words_cotangent, regions_cotangent,
):
    items, words, width = words_in.shape
    regions = regions_in.shape[1]
    share = cross_matrices.shape[1]
    count = width // share
    blocks = 3 if items % 12 == 0 else 1
    swaps = count == SLOTS
    me = lax.axis_index("fsdp").astype(jnp.int32).reshape(1)
    z = lax.axis_index("dp").astype(jnp.int32).reshape(1)

    own = jnp.concatenate([cross_vectors, word_self_vectors, region_self_vectors, word_feed_vectors, region_feed_vectors], axis=0)
    def whole(shard):
        return lax.all_gather(shard, "fsdp", axis=1, tiled=True)

    run = Sequence()

    word_bias = (word_mask.astype(f32) - 1.0) * 10000.0
    region_bias = jnp.where(jnp.arange(regions)[None, :] < region_count[:, None], 0.0, negative).astype(f32)
    word_rows = words_in.reshape(-1, width)
    region_rows = regions_in.reshape(-1, width)
    wr = block_bias(words, regions, region_bias, blocks)
    rw = block_bias(regions, words, word_bias, blocks)
    ww = block_bias(words, words, word_bias, blocks)
    rr = block_bias(regions, regions, region_bias, blocks)

    block = width // SLOTS
    word_cot = words_cotangent.reshape(-1, width)
    region_cot = regions_cotangent.reshape(-1, width)
    if swaps:
        own = jnp.pad(own, ((0, VECTOR_ROWS - own.shape[0]), (0, 128 - share)))
        cross_gather = Gather(run, cross_matrices, own)
        region_gather = Gather(run, region_self_matrices)
        (region_feed_shard,) = cross_gather.step(region_feed_matrices)
        region_gather.step()
        run.after(wr, rw, ww, rr, word_rows, region_rows, word_cot, region_cot)
        (cross, vector_parts), (word_feed_shard,) = cross_gather.finish(word_feed_matrices)
        region_feed, word_feed = whole(region_feed_shard), whole(word_feed_shard)
        vectors = jnp.zeros((8, 128), bf16)
    else:
        own = jnp.pad(own, ((0, VECTOR_ROWS - own.shape[0]), (0, 0)))
        vectors, vector_parts = lax.all_gather(own, "fsdp", axis=1, tiled=True), ()
        cross, region_self, word_self = ((whole(w),) for w in (cross_matrices, region_self_matrices, word_self_matrices))
        region_feed, word_feed = whole(region_feed_matrices), whole(word_feed_matrices)

    def reduction(kind, keep, send, by_exchange):
        return Reduction(run, kind, share, z, keep, send, by_exchange and lax.axis_size("dp") == 4) if swaps else None

    def step(group, name):
        return getattr(group, name)() if swaps else None

    word_one, region_one, word_kept, region_kept, vectors = cross_forward(run, me, word_rows, region_rows, cross, vectors, vector_parts, wr, rw)
    if swaps:
        ((region_self,), (word_shard,)) = region_gather.finish(word_self_matrices)
        word_gather = Gather(run, word_shard)
    region_two, region_self_kept = self_forward(run, REGION_SELF, me, region_one, region_self, vectors, rr)

    if swaps:
        word_gather.step()
    run.between = False
    regions_out, region_dtwo, keep_rf, send_rf, dvec_a = feed_both(
        run, REGION_SELF, REGION_FEED, swaps, me, region_two, region_cot, region_feed, vectors
    )
    if swaps:
        ((word_self,), _) = word_gather.finish()
    rf = reduction("feed", keep_rf, send_rf, False)
    region_done, keep_rs, send_rs, dvec_b = self_backward(
        run, REGION_SELF, blocks, swaps, me, region_dtwo, region_one, region_self, vectors, region_self_kept
    )
    rs = reduction("self", keep_rs, send_rs, True)
    step(rf, "first")
    word_two, word_self_kept = self_forward(run, WORD_SELF, me, word_one, word_self, vectors, ww)
    words_out, word_dtwo, keep_wf, send_wf, dvec_c = feed_both(
        run, WORD_SELF, WORD_FEED, swaps, me, word_two, word_cot, word_feed, vectors
    )
    wf = reduction("feed", keep_wf, send_wf, True)
    step(rs, "first")
    step(rf, "second")
    step(wf, "first")
    region_grads = region_side(run, blocks, me, region_done, cross, region_kept)
    step(rf, "last")
    step(rs, "second")
    word_done, keep_ws, send_ws, dvec_d = self_backward(
        run, WORD_SELF, blocks, swaps, me, word_dtwo, word_one, word_self, vectors, word_self_kept
    )
    ws = reduction("self", keep_ws, send_ws, True)
    step(wf, "second")
    step(rs, "last")
    words_grad, regions_grad, keep_cr, send_cr = cross_backward(
        run, blocks, swaps, me, word_done, region_done, word_rows, region_rows, cross,
        (dvec_a, dvec_b, dvec_c, dvec_d), word_kept, region_kept[4], region_grads,
    )
    run.between = True
    cr = reduction("cross", keep_cr, send_cr, True)

    if swaps:
        (held, sent), (own, other), (kept, far) = add_three(run, z, ws.state, wf.state, rs.state)
        ws.state = (held, exchange(sent, 1))
        wf.state = (own, replica_exchange(other, 0))
        rs.state = (kept, replica_exchange(far, 1))
        cr.first()
        ws.second()
        wf.halve()
        rs.sum()
        (grad_rf,) = rf.out()
        cr.second()
        words_grad, regions_grad, _ = lax.optimization_barrier((words_grad, regions_grad, run.token))
        ws.last()
        wf.sum()
        rs.join()
        cr.last()
        ws.halve()
        wf.join()
        (grad_rs,) = rs.out()
        cr.halve()
        ws.sum()
        (grad_wf,) = wf.out()
        cr.sum()
        ws.join()
        cr.join()
        (grad_ws,) = ws.out()
        grad_cr, *vector_grads = cr.out()
    else:
        (grad_rf,), (grad_wf,) = unswapped(keep_rf, send_rf, block, 2), unswapped(keep_wf, send_wf, block, 2)
        (grad_rs,), (grad_ws,) = unswapped(keep_rs, send_rs, block, 4), unswapped(keep_ws, send_ws, block, 4)
        grad_cr, vector_sum = unswapped(keep_cr, send_cr, block, 4)
        vector_grads = [vector_sum[start : start + number] for start, number in VECTOR_PARTS]

    return (
        words_out.reshape(items, words, width),
        regions_out.reshape(items, regions, width),
        words_grad.reshape(items, words, width),
        regions_grad.reshape(items, regions, width),
        grad_cr,
        vector_grads[0],
        grad_ws,
        vector_grads[1],
        grad_rs,
        vector_grads[2],
        grad_wf,
        vector_grads[3],
        grad_rf,
        vector_grads[4],
    )


def solution(mesh):
    items = P(("dp", "fsdp"), None, None)
    matrix = P(None, "fsdp", None)
    vector = P(None, "fsdp")
    weights = (matrix, vector) * 5
    return jax.shard_map(
        local,
        mesh=mesh,
        in_specs=(items, items, P(("dp", "fsdp"), None), P(("dp", "fsdp")), *weights, items, items),
        out_specs=(items,) * 4 + weights,
        check_vma=False,
    )
```

```python
from functools import partial
import math

import jax
import jax.numpy as jnp
from jax import lax
from jax.sharding import PartitionSpec as P
from jax.experimental import pallas as pl
from jax.experimental.pallas import tpu as pltpu

HEADS = 12
epsilon = 1e-12
negative = -10000.0
bf16 = jnp.bfloat16
f32 = jnp.float32

CROSS, WORD_SELF, REGION_SELF, WORD_FEED, REGION_FEED = 0, 5, 10, 15, 22
VECTOR_ROWS = 32


def nn(left, right):
    return jnp.dot(left, right, preferred_element_type=f32)


def nt(left, right):
    return lax.dot_general(left, right, (((1,), (1,)), ((), ())), preferred_element_type=f32)


def tn(left, right):
    return lax.dot_general(left, right, (((0,), (0,)), ((), ())), preferred_element_type=f32)


def norm_parts(total):
    centred = total - jnp.mean(total, axis=-1, keepdims=True)
    spread = jnp.mean(centred * centred, axis=-1, keepdims=True)
    rate = lax.rsqrt(spread + epsilon)
    return centred * rate, rate


def norm_back(grad, unit, rate, gain):
    scaled = grad * gain
    mean_one = jnp.mean(scaled, axis=-1, keepdims=True)
    mean_two = jnp.mean(scaled * unit, axis=-1, keepdims=True)
    return (
        rate * (scaled - mean_one - unit * mean_two),
        jnp.sum(grad * unit, axis=0, keepdims=True),
        jnp.sum(grad, axis=0, keepdims=True),
    )


def half_masks(rows):
    lane = lax.broadcasted_iota(jnp.int32, (rows, 128), 1)
    return (lane < 64, lane >= 64)


def heads_forward(q_ref, k_ref, v_ref, bias_ref, probs_ref, ctx_ref):
    blocks, qb, kb = bias_ref.shape
    pairs = q_ref.shape[1] // 128
    masks = half_masks(kb)
    zero = jnp.zeros((kb, 128), bf16)

    def block(b, carry):
        rq = pl.ds(pl.multiple_of(b * qb, 16), qb)
        rk = pl.ds(pl.multiple_of(b * kb, 16), kb)
        bias = bias_ref[b]
        for p in range(pairs):
            cols = pl.ds(p * 128, 128)
            qp = q_ref[rq, cols]
            kp = k_ref[rk, cols]
            vp = v_ref[rk, cols]
            mixed = None
            for half in range(2):
                s = nt(qp, jnp.where(masks[half], kp, zero)) * 0.125 + bias
                e = jnp.exp(s - jnp.max(s, axis=-1, keepdims=True))
                low = (e / jnp.sum(e, axis=-1, keepdims=True)).astype(bf16)
                probs_ref[b * (2 * pairs) + 2 * p + half] = low
                part = nn(low, jnp.where(masks[half], vp, zero))
                mixed = part if mixed is None else mixed + part
            ctx_ref[rq, cols] = mixed.astype(bf16)
        return carry

    lax.fori_loop(0, blocks, block, 0, unroll=True)


def heads_backward(q_ref, k_ref, v_ref, probs_ref, dctx_ref, dq_ref, dk_ref, dv_ref, blocks):
    qb = q_ref.shape[0] // blocks
    kb = k_ref.shape[0] // blocks
    pairs = q_ref.shape[1] // 128
    kmasks, qmasks = half_masks(kb), half_masks(qb)
    kzero, qzero = jnp.zeros((kb, 128), bf16), jnp.zeros((qb, 128), bf16)

    def block(b, carry):
        rq = pl.ds(pl.multiple_of(b * qb, 16), qb)
        rk = pl.ds(pl.multiple_of(b * kb, 16), kb)
        for p in range(pairs):
            cols = pl.ds(p * 128, 128)
            qp = q_ref[rq, cols]
            kp = k_ref[rk, cols]
            vp = v_ref[rk, cols]
            dc = dctx_ref[rq, cols]
            dq = dk = dv = 0.0
            for half in range(2):
                low = probs_ref[b * (2 * pairs) + 2 * p + half]
                probs = low.astype(f32)
                dp = nt(dc, jnp.where(kmasks[half], vp, kzero))
                dv = dv + tn(low, jnp.where(qmasks[half], dc, qzero))
                t = probs * dp
                ds = (t - probs * jnp.sum(t, axis=-1, keepdims=True)).astype(bf16)
                dq = dq + nn(ds, jnp.where(kmasks[half], kp, kzero))
                dk = dk + tn(ds, jnp.where(qmasks[half], qp, qzero))
            dq_ref[rq, cols] = (dq * 0.125).astype(bf16)
            dk_ref[rk, cols] = (dk * 0.125).astype(bf16)
            dv_ref[rk, cols] = dv.astype(bf16)
        return carry

    lax.fori_loop(0, blocks, block, 0, unroll=True)


def vec(vec_ref, row):
    return vec_ref[row : row + 1, :]


def attend(moves, x_low, c_low, base, w_ref, vec_ref, row, bias_ref, q_ref, k_ref, v_ref, probs_ref, ctx_ref):
    q_ref[...] = (nn(x_low, w_ref[0]) + vec(vec_ref, row)).astype(bf16)
    k_ref[...] = nn(c_low, w_ref[1]).astype(bf16)
    v_ref[...] = (nn(c_low, w_ref[2]) + vec(vec_ref, row + 1)).astype(bf16)
    moves.leave(q_ref, k_ref, v_ref)
    heads_forward(q_ref, k_ref, v_ref, bias_ref, probs_ref, ctx_ref)
    moves.leave(probs_ref, ctx_ref)
    return base + nn(ctx_ref[...], w_ref[3]) + vec(vec_ref, row + 2)


def cross_forward_kernel(count, moves, me_ref, words_ref, regions_ref, known_ref, wr_ref, rw_ref, *refs):
    vector_parts, refs = (refs[:2], refs[2:]) if count == 2 else ((), refs)
    parts, refs = refs[:count], refs[count:]
    wtot_ref, rtot_ref, wq_ref, wk_ref, wv_ref, wp_ref, wc_ref, rq_ref, rk_ref, rv_ref, rp_ref, rc_ref = refs[:12]
    vec_ref, w_ref, vt_ref, sems = refs[12:]
    copies = fetch(parts, me_ref[0], w_ref, sems, vector_parts, vt_ref)
    moves.arrive()
    settle(copies)
    if count == 1:
        vec_ref[...] = known_ref[...].astype(f32)
    else:
        block = w_ref.shape[1] // SLOTS
        for s in range(SLOTS):
            vec_ref[:, s * block : (s + 1) * block] = vt_ref[s ^ me_ref[0]][:, :block].astype(f32)
    words, regions = words_ref[...], regions_ref[...]
    wtot_ref[...] = attend(moves, words, regions, words.astype(f32), w_ref, vec_ref, CROSS, wr_ref, wq_ref, wk_ref, wv_ref, wp_ref, wc_ref)
    moves.leave(wtot_ref)
    rtot_ref[...] = attend(moves, regions, words, regions.astype(f32), w_ref, vec_ref, CROSS, rw_ref, rq_ref, rk_ref, rv_ref, rp_ref, rc_ref)


def self_forward_kernel(row, count, moves, me_ref, tot_ref, vec_ref, bias_ref, *refs):
    parts = refs[:count]
    out_ref, q_ref, k_ref, v_ref, p_ref, c_ref, w_ref, sems = refs[count:]
    copies = fetch(parts, me_ref[0], w_ref, sems)
    moves.arrive()
    unit, _ = norm_parts(tot_ref[...])
    y = unit * vec(vec_ref, CROSS + 3) + vec(vec_ref, CROSS + 4)
    low = y.astype(bf16)
    settle(copies)
    out_ref[...] = attend(moves, low, low, y, w_ref, vec_ref, row, bias_ref, q_ref, k_ref, v_ref, p_ref, c_ref)


def gelu_parts(x):
    size = jnp.abs(x)
    e = jnp.exp(x * x * -0.5)
    t = 1.0 / (1.0 + (0.3275911 * 0.7071067811865476) * size)
    poly = t * (0.127414796 + t * (-0.142248368 + t * (0.7107068705 + t * (-0.7265760135 + t * 0.5307027145))))
    tail = poly * e
    phi = jnp.where(x >= 0, 1.0 - tail, tail)
    return x * phi, phi + x * e * 0.3989422804014327


def slot_of(s, me):
    k = s ^ me
    core, x, y = k & 1, (k >> 1) & 1, (k >> 2) & 1
    flip = (me & 1) ^ core
    return core * 4 + jnp.where(flip == 0, x * 2 + y, y * 2 + x)


def place(dest_ref, value, me):
    if me is None:
        dest_ref[...] = value
        return
    rows = value.shape[0] // SLOTS
    for s in range(SLOTS):
        dest_ref[pl.ds(pl.multiple_of(slot_of(s, me) * rows, 16), rows), :] = value[s * rows : (s + 1) * rows, :]


SLOTS = 8


def put(keep_ref, send_ref, base, stride, cols, value):
    rows = value.shape[0] // SLOTS
    low = value.astype(bf16)
    for j in range(SLOTS):
        dest = keep_ref if j < SLOTS // 2 else send_ref
        start = base + (j % (SLOTS // 2)) * stride
        dest[start : start + rows, cols] = low[j * rows : (j + 1) * rows]


def feed_kernel(
    self_row, row, chunk, swaps,
    moves, me_ref, tot_ref, cot_ref, far_ref, vec_ref,
    out_ref, dtot_ref, far_keep_ref, far_send_ref, dvec_ref,
    x_ref, y_ref, h_ref, gp_ref, dpre_ref, dy_ref, xt_ref, dyt_ref, acc_ref, bup_ref, dbup_ref,
    m_ref, keep_ref, send_ref, in_sems, out_sems,
):
    me = me_ref[0] if swaps else None
    copies = [pltpu.make_async_copy(far_ref.at[m], m_ref.at[m], in_sems.at[m]) for m in range(2)]
    for copy in copies:
        copy.start()
    moves.arrive()
    width = tot_ref.shape[1]
    hidden = m_ref.shape[2]
    parts = hidden // width
    block = width // SLOTS
    for i in range(parts):
        bup_ref[:, i * width : (i + 1) * width] = vec(vec_ref, row + i)
    unit2, rate2 = norm_parts(tot_ref[...])
    y = unit2 * vec(vec_ref, self_row + 3) + vec(vec_ref, self_row + 4)
    y_ref[...] = y
    x_ref[...] = y.astype(bf16)
    copies[0].wait()

    def up(i, carry):
        cols = pl.ds(pl.multiple_of(i * chunk, 128), chunk)
        pre = nn(x_ref[...], m_ref[0, :, cols]) + bup_ref[:, cols]
        value, slope = gelu_parts(pre)
        h_ref[:, cols] = value.astype(bf16)
        gp_ref[:, cols] = slope
        return carry

    lax.fori_loop(0, hidden // chunk, up, 0)
    copies[1].wait()

    def down(i, carry):
        cols = pl.ds(0, width)
        acc_ref[:, cols] = nt(h_ref[...], m_ref[1, pl.ds(0, width), :])
        return carry

    lax.fori_loop(0, 1, down, 0, unroll=True)
    gain = vec(vec_ref, row + 5)
    unit, rate = norm_parts(y_ref[...] + acc_ref[...] + vec(vec_ref, row + 4))
    out_ref[...] = (unit * gain + vec(vec_ref, row + 6)).astype(bf16)
    moves.leave(out_ref)
    dtot, dgain, dshift = norm_back(cot_ref[...].astype(f32), unit, rate, gain)
    dy = dtot.astype(bf16)
    dy_ref[...] = dy
    dvec_ref[...] = jnp.zeros_like(dvec_ref)
    dvec_ref[row + 4 : row + 5, :] = jnp.sum(dy.astype(f32), axis=0, keepdims=True)
    dvec_ref[row + 5 : row + 6, :] = dgain
    dvec_ref[row + 6 : row + 7, :] = dshift
    y_ref[...] = dtot
    place(xt_ref, x_ref[...].T, me)
    place(dyt_ref, dy.T, me)

    def leaving(i):
        cols = pl.ds(pl.multiple_of(i * chunk, 128), chunk)
        return (
            pltpu.make_async_copy(keep_ref.at[:, cols], far_keep_ref.at[:, cols], out_sems.at[i, 0]),
            pltpu.make_async_copy(send_ref.at[:, cols], far_send_ref.at[:, cols], out_sems.at[i, 1]),
        )

    def back(i, carry):
        cols = pl.ds(pl.multiple_of(i * chunk, 128), chunk)
        dpre = (nn(dy_ref[...], m_ref[1, :, cols]) * gp_ref[:, cols]).astype(bf16)
        dpre_ref[:, cols] = dpre
        dbup_ref[:, cols] = jnp.sum(dpre.astype(f32), axis=0, keepdims=True)
        put(keep_ref, send_ref, 0, 2 * block, cols, nn(xt_ref[...], dpre))
        put(keep_ref, send_ref, block, 2 * block, cols, nn(dyt_ref[...], h_ref[:, cols]))
        for copy in leaving(i):
            copy.start()
        return carry

    lax.fori_loop(0, hidden // chunk, back, 0)
    for i in range(parts):
        dvec_ref[row + i : row + i + 1, :] = dbup_ref[:, i * width : (i + 1) * width]

    def rows(i, carry):
        cols = pl.ds(0, width)
        acc_ref[:, cols] = nt(dpre_ref[...], m_ref[0, pl.ds(0, width), :])
        return carry

    lax.fori_loop(0, 1, rows, 0, unroll=True)
    unit2, rate2 = norm_parts(tot_ref[...])
    dtot2, dgain2, dshift2 = norm_back(acc_ref[...] + y_ref[...], unit2, rate2, vec(vec_ref, self_row + 3))
    dtot_ref[...] = dtot2
    dvec_ref[self_row + 3 : self_row + 4, :] = dgain2
    dvec_ref[self_row + 4 : self_row + 5, :] = dshift2
    for i in range(hidden // chunk):
        settle(leaving(i))


def column_sum(low):
    return jnp.sum(low.astype(f32), axis=0, keepdims=True)


def self_backward_kernel(
    row, blocks, swaps, count,
    moves, me_ref, dtot_ref, tot_ref, vec_ref, q_ref, k_ref, v_ref, p_ref, c_ref, *refs,
):
    parts = refs[:count]
    out_ref, keep_ref, send_ref, dvec_ref, dq_ref, dk_ref, dv_ref, dc_ref, xt_ref, ct_ref, w_ref, sems = refs[count:]
    me = me_ref[0] if swaps else None
    copies = fetch(parts, me, w_ref, sems)
    moves.arrive()
    da = dtot_ref[...].astype(bf16)
    dvec_ref[...] = jnp.zeros_like(dvec_ref)
    dvec_ref[row + 2 : row + 3, :] = column_sum(da)
    place(ct_ref, c_ref[...].T, me)
    width = w_ref.shape[2]
    every = pl.ds(0, width)
    block = width // SLOTS
    put(keep_ref, send_ref, 3 * block, 4 * block, every, nn(ct_ref[...], da))
    settle(copies)
    dc_ref[...] = nt(da, w_ref[3]).astype(bf16)
    heads_backward(q_ref, k_ref, v_ref, p_ref, dc_ref, dq_ref, dk_ref, dv_ref, blocks)
    unit, rate = norm_parts(tot_ref[...])
    gain = vec(vec_ref, CROSS + 3)
    low = (unit * gain + vec(vec_ref, CROSS + 4)).astype(bf16)
    place(xt_ref, low.T, me)
    dq, dk, dv = dq_ref[...], dk_ref[...], dv_ref[...]
    put(keep_ref, send_ref, 0, 4 * block, every, nn(xt_ref[...], dq))
    put(keep_ref, send_ref, block, 4 * block, every, nn(xt_ref[...], dk))
    put(keep_ref, send_ref, 2 * block, 4 * block, every, nn(xt_ref[...], dv))
    moves.leave(keep_ref, send_ref)
    dvec_ref[row : row + 1, :] = column_sum(dq)
    dvec_ref[row + 1 : row + 2, :] = column_sum(dv)
    dx = dtot_ref[...] + nt(dq, w_ref[0]) + nt(dk, w_ref[1]) + nt(dv, w_ref[2])
    dtot, dgain, dshift = norm_back(dx, unit, rate, gain)
    out_ref[...] = dtot
    dvec_ref[CROSS + 3 : CROSS + 4, :] = dgain
    dvec_ref[CROSS + 4 : CROSS + 5, :] = dshift


def region_side_kernel(
    blocks, count,
    moves, me_ref, dr_ref, rq_ref, rk_ref, rv_ref, rp_ref, *refs,
):
    rdq_ref, rdk_ref, rdv_ref, rpart_ref, wpart_ref, rdc_ref, w_ref, sems = refs[count:]
    copies = fetch(refs[:count], me_ref[0], w_ref, sems)
    moves.arrive()
    settle(copies)
    rdc_ref[...] = nt(dr_ref[...].astype(bf16), w_ref[3]).astype(bf16)
    heads_backward(rq_ref, rk_ref, rv_ref, rp_ref, rdc_ref, rdq_ref, rdk_ref, rdv_ref, blocks)
    moves.leave(rdq_ref, rdk_ref, rdv_ref)
    rpart_ref[...] = dr_ref[...] + nt(rdq_ref[...], w_ref[0])
    wpart_ref[...] = nt(rdk_ref[...], w_ref[1]) + nt(rdv_ref[...], w_ref[2])


def cross_backward_kernel(
    blocks, swaps, count,
    moves, me_ref, dw_ref, dr_ref, words_ref, regions_ref, va_ref, vb_ref, vc_ref, vd_ref,
    wq_ref, wk_ref, wv_ref, wp_ref, wc_ref, rc_ref, rdq_ref, rdk_ref, rdv_ref, rpart_ref, wpart_ref, *refs,
):
    parts, refs = refs[:count], refs[count:]
    wout_ref, rout_ref, keep_ref, send_ref, wdq_ref, wdk_ref, wdv_ref, wdc_ref, wct_ref, rct_ref = refs[:10]
    wt_ref, rt_ref, dvec_ref, vt_ref, w_ref, sems = refs[10:]
    me = me_ref[0] if swaps else None
    copies = fetch(parts, me, w_ref, sems)
    moves.arrive()
    width = w_ref.shape[2]
    every = pl.ds(0, width)
    block = width // SLOTS
    stride = 4 * block + VECTOR_ROWS
    wda, rda = dw_ref[...].astype(bf16), dr_ref[...].astype(bf16)
    dvec_ref[...] = va_ref[...] + vb_ref[...] + vc_ref[...] + vd_ref[...]
    dvec_ref[CROSS + 2 : CROSS + 3, :] = column_sum(wda) + column_sum(rda)
    place(wct_ref, wc_ref[...].T, me)
    place(rct_ref, rc_ref[...].T, me)
    put(keep_ref, send_ref, 3 * block, stride, every, nn(wct_ref[...], wda) + nn(rct_ref[...], rda))
    settle(copies)
    wdc_ref[...] = nt(wda, w_ref[3]).astype(bf16)
    heads_backward(wq_ref, wk_ref, wv_ref, wp_ref, wdc_ref, wdq_ref, wdk_ref, wdv_ref, blocks)
    place(wt_ref, words_ref[...].T, me)
    place(rt_ref, regions_ref[...].T, me)
    wdq, wdk, wdv = wdq_ref[...], wdk_ref[...], wdv_ref[...]
    rdq, rdk, rdv = rdq_ref[...], rdk_ref[...], rdv_ref[...]
    put(keep_ref, send_ref, 0, stride, every, nn(wt_ref[...], wdq) + nn(rt_ref[...], rdq))
    put(keep_ref, send_ref, block, stride, every, nn(rt_ref[...], wdk) + nn(wt_ref[...], rdk))
    put(keep_ref, send_ref, 2 * block, stride, every, nn(rt_ref[...], wdv) + nn(wt_ref[...], rdv))
    dvec_ref[CROSS : CROSS + 1, :] = column_sum(wdq) + column_sum(rdq)
    dvec_ref[CROSS + 1 : CROSS + 2, :] = column_sum(wdv) + column_sum(rdv)
    vt_ref[...] = jnp.zeros_like(vt_ref)
    for s in range(SLOTS):
        slot = slot_of(s, me) if swaps else s
        vt_ref[pl.ds(pl.multiple_of(slot * VECTOR_ROWS, 16), VECTOR_ROWS), 0:block] = dvec_ref[:, s * block : (s + 1) * block].astype(bf16)
    for j in range(SLOTS):
        dest = keep_ref if j < SLOTS // 2 else send_ref
        start = (j % (SLOTS // 2)) * stride + 4 * block
        dest[start : start + VECTOR_ROWS, :] = vt_ref[j * VECTOR_ROWS : (j + 1) * VECTOR_ROWS, :]
    moves.leave(keep_ref, send_ref)
    wout_ref[...] = (dw_ref[...] + nt(wdq, w_ref[0]) + wpart_ref[...]).astype(bf16)
    rout_ref[...] = (rpart_ref[...] + nt(wdk, w_ref[1]) + nt(wdv, w_ref[2])).astype(bf16)


MIB = 1024 * 1024


SCALE = 20


class Moves:
    def __init__(self, ins, outs, sems):
        self.ins = [pltpu.make_async_copy(source, dest, sems.at[i]) for i, (source, dest) in enumerate(ins)]
        self.outs = [(ref, pltpu.make_async_copy(ref, dest, sems.at[len(ins) + i])) for i, (ref, dest) in enumerate(outs)]
        self.left = set()
        for copy in self.ins:
            copy.start()

    def arrive(self):
        for copy in self.ins:
            copy.wait()

    def leave(self, *refs):
        for i, (ref, copy) in enumerate(self.outs):
            if any(ref is r for r in refs):
                copy.start()
                self.left.add(i)

    def finish(self):
        for i, (_, copy) in enumerate(self.outs):
            if i not in self.left:
                copy.start()
        for _, copy in self.outs:
            copy.wait()


class Far:
    def __init__(self, array):
        self.array = array


class Scalar:
    def __init__(self, array):
        self.array = array


class Sequence:
    def __init__(self):
        self.token = self.more = ()
        self.free = False
        self.between = True

    def after(self, *arrays):
        self.more += arrays

    def __call__(self, kernel, name, outs, scratch, us, args, far_outs=(), small=False, manual=False, grid=None, in_specs=None, out_specs=None):
        here, far = pl.BlockSpec(memory_space=pltpu.VMEM), pl.BlockSpec(memory_space=pl.ANY)
        moved_in = [i for i, a in enumerate(args) if manual and not isinstance(a, (Far, Scalar))]
        moved_out = [i for i in range(len(outs)) if manual and i not in far_outs]
        if in_specs is None:
            kinds = {Far: far, Scalar: pl.BlockSpec(memory_space=pltpu.SMEM)}
            in_specs = [kinds.get(type(a), here) for a in args]
            out_specs = [far if manual or i in far_outs else here for i in range(len(outs))]
            in_specs = [far if i in moved_in else spec for i, spec in enumerate(in_specs)]
        arrays = [a.array if isinstance(a, (Far, Scalar)) else a for a in args]
        out_shape = tuple(jax.ShapeDtypeStruct(s, d) for s, d in outs)
        moved = sum(a.size * a.dtype.itemsize for a in arrays) + sum(o.size * o.dtype.itemsize for o in out_shape)
        small = small and self.between
        if grid is None:
            held = [a for a in args if not isinstance(a, (Far, Scalar))] + [jax.ShapeDtypeStruct(*o) for i, o in enumerate(outs) if i not in far_outs]
            held += [jax.ShapeDtypeStruct(*s) for s in scratch if isinstance(s, tuple)]
            held = sum(math.prod(h.shape) * jnp.dtype(h.dtype).itemsize for h in held)
            limit = int(1.15 * held) + 2 * MIB if small else 60 * MIB
        else:
            limit = 16 * MIB if small else 60 * MIB
        token = self.token + self.more
        self.more = ()

        scratch = list(scratch)
        own = len(scratch)
        if manual:
            scratch += [(arrays[i].shape, arrays[i].dtype) for i in moved_in] + [outs[i] for i in moved_out]
            scratch.append(pltpu.SemaphoreType.DMA((len(moved_in) + len(moved_out),)))

        def body(*refs):
            taken, rest = list(refs[: len(arrays)]), refs[len(arrays) + len(token) :]
            given, rest = list(rest[: len(outs)]), rest[len(outs) :]
            if not manual:
                kernel(*taken, *given, *rest)
                return
            buffers = rest[own:]
            ins = [(taken[i], buffers[j]) for j, i in enumerate(moved_in)]
            leaving = [(buffers[len(moved_in) + j], given[i]) for j, i in enumerate(moved_out)]
            for j, i in enumerate(moved_in):
                taken[i] = buffers[j]
            for j, i in enumerate(moved_out):
                given[i] = buffers[len(moved_in) + j]
            moves = Moves(ins, leaving, buffers[-1])
            kernel(moves, *taken, *given, *rest[:own])
            moves.finish()

        extra = {} if grid is None else {"grid": grid}
        got = pl.pallas_call(
            body,
            out_shape=out_shape,
            in_specs=list(in_specs) + [far] * len(token),
            out_specs=tuple(out_specs),
            scratch_shapes=[pltpu.VMEM(*s) if isinstance(s, tuple) else s for s in scratch],
            compiler_params=pltpu.CompilerParams(vmem_limit_bytes=limit),
            cost_estimate=pl.CostEstimate(flops=int(us * SCALE * 1.15e9), bytes_accessed=0, transcendentals=0),
            name=name,
            **extra,
        )(*arrays, *token)
        self.token = () if self.free else (min(got, key=lambda o: o.size * o.dtype.itemsize),)
        return got


def fetch(parts, me, w_ref, sems, vector_parts=(), vt_ref=None):
    copies = []

    def start(source, dest):
        copies.append(pltpu.make_async_copy(source, dest, sems.at[len(copies)]))
        copies[-1].start()

    if len(parts) == 1:
        for m in range(4):
            start(parts[0].at[m], w_ref.at[m])
        return copies
    block = w_ref.shape[1] // SLOTS
    for other in range(2):
        odd = ((me & 1) ^ other) == 1
        for i in range(4):
            k = jnp.where(odd, (i & 1) * 4 + (i >> 1) * 2, (i & 1) * 2 + (i >> 1) * 4) + other
            rows = pl.ds(pl.multiple_of((k ^ me) * block, 16), block)
            for m in range(4):
                start(parts[other].at[i, pl.ds(m * block, block)], w_ref.at[m, rows, :])
            if vt_ref is not None:
                start(vector_parts[other].at[i], vt_ref.at[k])
    return copies


def settle(copies):
    for copy in copies:
        copy.wait()


def kept_shapes(nq, nk, width, bias):
    blocks, qb, kb = bias.shape
    return [((nq, width), bf16), ((nk, width), bf16), ((nk, width), bf16), ((blocks * HEADS, qb, kb), bf16), ((nq, width), bf16)]


def attention_scratch(width):
    return [((4, width, width), bf16), pltpu.SemaphoreType.DMA((40,))]


def fars(parts):
    return [Far(p) for p in parts]


def cross_forward(run, me, words, regions, parts, vectors, vector_parts, wr, rw):
    nw, nr, width = words.shape[0], regions.shape[0], words.shape[1]
    outs = [((nw, width), f32), ((nr, width), f32)] + kept_shapes(nw, nr, width, wr) + kept_shapes(nr, nw, width, rw)
    outs += [((VECTOR_ROWS, width), f32)]
    scratch = attention_scratch(width)
    scratch.insert(1, ((SLOTS, VECTOR_ROWS, 128), bf16))
    args = (Scalar(me), words, regions, vectors, wr, rw, *fars(vector_parts), *fars(parts))
    got = run(partial(cross_forward_kernel, len(parts)), "cross_forward", outs, scratch, 0.05, args, manual=True)
    return got[0], got[1], got[2:7], got[7:12], got[12]


def self_forward(run, row, me, total, parts, vectors, bias):
    n, width = total.shape
    outs = [((n, width), f32)] + kept_shapes(n, n, width, bias)
    args = (Scalar(me), total, vectors, bias, *fars(parts))
    kernel = partial(self_forward_kernel, row, len(parts))
    got = run(kernel, "self_forward", outs, attention_scratch(width), 0.05, args, manual=True)
    return got[0], got[1:]


def feed_both(run, self_row, row, swaps, me, total, cot, m, vectors):
    n, width = total.shape
    hidden = m.shape[2]
    chunk = 1536
    half = (width, hidden)
    outs = [((n, width), bf16), ((n, width), f32), (half, bf16), (half, bf16), ((VECTOR_ROWS, width), f32)]
    scratch = [
        ((n, width), bf16), ((n, width), f32), ((n, hidden), bf16), ((n, hidden), f32), ((n, hidden), bf16),
        ((n, width), bf16), ((width, n), bf16), ((width, n), bf16), ((n, width), f32), ((1, hidden), f32), ((1, hidden), f32),
        ((2, width, hidden), bf16), (half, bf16), (half, bf16),
        pltpu.SemaphoreType.DMA((2,)), pltpu.SemaphoreType.DMA((hidden // chunk, 2)),
    ]
    args = (Scalar(me), total, cot, Far(m), vectors)
    return run(partial(feed_kernel, self_row, row, chunk, swaps), "feed", outs, scratch, 10 + n / 24, args, far_outs=(2, 3), manual=True)


def self_backward(run, row, blocks, swaps, me, dtot, total, parts, vectors, kept):
    n, width = total.shape
    half = (2 * width, width)
    outs = [((n, width), f32), (half, bf16), (half, bf16), ((VECTOR_ROWS, width), f32)]
    scratch = [((n, width), bf16)] * 4 + [((width, n), bf16)] * 2 + attention_scratch(width)
    args = (Scalar(me), dtot, total, vectors, *kept, *fars(parts))
    kernel = partial(self_backward_kernel, row, blocks, swaps, len(parts))
    return run(kernel, "self_backward", outs, scratch, 8 + n / 40, args, manual=True)


def region_side(run, blocks, me, dr, parts, kept):
    nr, width = dr.shape
    nw = kept[1].shape[0]
    outs = [((nr, width), bf16), ((nw, width), bf16), ((nw, width), bf16), ((nr, width), f32), ((nw, width), f32)]
    scratch = [((nr, width), bf16)] + attention_scratch(width)
    args = (Scalar(me), dr, *kept[:4], *fars(parts))
    return run(partial(region_side_kernel, blocks, len(parts)), "region_side", outs, scratch, 14, args, manual=True)


def cross_backward(run, blocks, swaps, me, dw, dr, words, regions, parts, dvecs, word_kept, region_ctx, region_grads):
    nw, nr, width = words.shape[0], regions.shape[0], words.shape[1]
    half = (2 * width + VECTOR_ROWS * (SLOTS // 2), width)
    outs = [((nw, width), bf16), ((nr, width), bf16), (half, bf16), (half, bf16)]
    scratch = [((nw, width), bf16), ((nr, width), bf16), ((nr, width), bf16), ((nw, width), bf16)]
    scratch += [((width, nw), bf16), ((width, nr), bf16)] * 2
    scratch += [((VECTOR_ROWS, width), f32), ((VECTOR_ROWS * SLOTS, width), bf16)] + attention_scratch(width)
    args = (Scalar(me), dw, dr, words, regions, *dvecs, *word_kept, region_ctx, *region_grads, *fars(parts))
    return run(partial(cross_backward_kernel, blocks, swaps, len(parts)), "cross_backward", outs, scratch, 20, args, manual=True)


def join_pieces(run, pairs, along=()):
    outs = [((2 * p.shape[0], *p.shape[1:]), p.dtype) for p, _ in pairs] + [(a.shape, a.dtype) for a in along]
    arrays = [a for pair in pairs for a in pair] + list(along)

    def kernel(*refs):
        taken, given = refs[: len(arrays)], refs[len(arrays) :]
        for i, (p, _) in enumerate(pairs):
            n = p.shape[0]
            given[i][:n] = taken[2 * i][...]
            given[i][n:] = taken[2 * i + 1][...]
        for i in range(len(along)):
            given[len(pairs) + i][...] = taken[2 * len(pairs) + i][...]

    return run(kernel, "join_pieces", outs, [], 2, arrays, small=True)


def plus(left, right):
    return (left.astype(f32) + right.astype(f32)).astype(bf16)


def columns_of(width):
    return width // 4 if width % 512 == 0 else width // 3


def add_halves(run, keep, got):
    rows, width = keep.shape
    c = columns_of(width)
    half = rows // 2

    def kernel(keep_ref, got_ref, held_ref, sent_ref):
        held_ref[...] = plus(keep_ref[:half, :], got_ref[:half, :])
        sent_ref[...] = plus(keep_ref[half:, :], got_ref[half:, :])

    def block(n):
        return pl.BlockSpec((n, c), lambda i: (0, i))

    outs = [((half, width), bf16)] * 2
    return run(kernel, "add_halves", outs, [], 6, (keep, got), small=keep.size < MIB, grid=(width // c,), in_specs=[block(rows)] * 2, out_specs=[block(half)] * 2)


def padded(rows):
    return -(-rows // 64) * 64


def add_last(run, z, held, back):
    n, width = held.shape
    rows = padded(n)

    def fill(held_ref, back_ref, ref):
        ref[:n, :] = plus(held_ref[...], back_ref[...])
        if rows > n:
            ref[n:, :] = jnp.zeros((rows - n, width), bf16)

    if z is None:
        return run(fill, "add_last", [((rows, width), bf16)], [], 2.5, (held, back), small=True)[0]

    def kernel(z_ref, held_ref, back_ref, keep_ref, send_ref, all_ref):
        fill(held_ref, back_ref, all_ref)
        split_rows(all_ref, z_ref[0] & 1, keep_ref, send_ref)

    outs = [((rows // 2, width), bf16)] * 2
    return run(kernel, "add_last", outs, [((rows, width), bf16)], 2.5, (Scalar(z), held, back), small=True)


def add_three(run, z, first, last, halve):
    def kernel(moves, z_ref, keep_ref, got_ref, held_ref, back_ref, own_ref, other_ref, *refs):
        fh_ref, fs_ref, lk_ref, ls_ref, hk_ref, hs_ref, last_ref, halve_ref = refs
        moves.arrive()
        half = keep_ref.shape[0] // 2
        fs_ref[...] = plus(keep_ref[half:, :], got_ref[half:, :])
        moves.leave(fs_ref)
        last_ref[...] = plus(held_ref[...], back_ref[...])
        split_rows(last_ref, z_ref[0] & 1, lk_ref, ls_ref)
        moves.leave(ls_ref, lk_ref)
        halve_ref[...] = plus(own_ref[...], other_ref[...])
        split_rows(halve_ref, (z_ref[0] >> 1) & 1, hk_ref, hs_ref)
        moves.leave(hs_ref, hk_ref)
        fh_ref[...] = plus(keep_ref[:half, :], got_ref[:half, :])

    args = (Scalar(z), *first, *last, *halve)
    outs = [((pair[0].shape[0] // 2, pair[0].shape[1]), bf16) for pair in (first, first, last, last, halve, halve)]
    scratch = [(last[0].shape, bf16), (halve[0].shape, bf16)]
    got = run(kernel, "add_three", outs, scratch, 8, args, manual=True)
    return got[0:2], got[2:4], got[4:6]


def split_rows(all_ref, bit, keep_ref, send_ref):
    half = all_ref.shape[0] // 2
    keep_ref[...] = all_ref[pl.ds(pl.multiple_of(bit * half, 16), half), :]
    send_ref[...] = all_ref[pl.ds(pl.multiple_of((1 - bit) * half, 16), half), :]


def join_rows(own, other, bit, all_ref):
    half = own.shape[0]
    all_ref[pl.ds(pl.multiple_of(bit * half, 16), half), :] = own[...]
    all_ref[pl.ds(pl.multiple_of((1 - bit) * half, 16), half), :] = other[...]


def replicas_halve(run, z, held, back):
    rows, width = held.shape

    def kernel(z_ref, held_ref, back_ref, keep_ref, send_ref, all_ref):
        all_ref[...] = plus(held_ref[...], back_ref[...])
        split_rows(all_ref, (z_ref[0] >> 1) & 1, keep_ref, send_ref)

    outs = [((rows // 2, width), bf16)] * 2
    return run(kernel, "replicas_halve", outs, [((rows, width), bf16)], 2, (Scalar(z), held, back), small=True)


def replicas_sum(run, held, back):
    def kernel(held_ref, back_ref, out_ref):
        out_ref[...] = plus(held_ref[...], back_ref[...])

    return run(kernel, "replicas_sum", [(held.shape, bf16)], [], 1.7, (held, back), small=True)[0]


def replicas_join(run, z, own, other):
    rows, width = own.shape

    def kernel(z_ref, own_ref, other_ref, out_ref):
        join_rows(own_ref, other_ref, (z_ref[0] >> 1) & 1, out_ref)

    return run(kernel, "replicas_join", [((2 * rows, width), bf16)], [], 1.7, (Scalar(z), own, other), small=True)[0]


VECTOR_PARTS = ((CROSS, 5), (WORD_SELF, 5), (REGION_SELF, 5), (WORD_FEED, 7), (REGION_FEED, 7))


def shard_out(all_ref, share, refs):
    count = refs[0].shape[0]
    for m in range(count):
        refs[0][m] = all_ref[m * share : (m + 1) * share, :].astype(f32)
    if len(refs) > 1:
        vectors = all_ref[count * share : count * share + VECTOR_ROWS, :share].astype(f32)
        for ref, (start, number) in zip(refs[1:], VECTOR_PARTS):
            ref[...] = vectors[start : start + number]


def shard_shapes(kind, share, width):
    if kind == "feed":
        return [((2, share, width), f32)]
    outs = [((4, share, width), f32)]
    return outs + [((number, share), f32) for _, number in VECTOR_PARTS] if kind == "cross" else outs


def shard_of_sum(run, kind, share, summed):
    def kernel(all_ref, *refs):
        shard_out(all_ref, share, refs)

    return run(kernel, "shard", shard_shapes(kind, share, summed.shape[1]), [], 2.5, (summed,), small=True)


def shard_of_halves(run, kind, share, z, own, other):
    rows, width = own.shape

    def kernel(z_ref, own_ref, other_ref, *refs):
        all_ref = refs[-1]
        join_rows(own_ref, other_ref, z_ref[0] & 1, all_ref)
        shard_out(all_ref, share, refs[:-1])

    return run(kernel, "shard", shard_shapes(kind, share, width), [((2 * rows, width), bf16)], 2.5, (Scalar(z), own, other), small=True)


def block_bias(query_slots, key_slots, key_bias, blocks):
    items = key_bias.shape[0] // blocks
    rows = jnp.arange(items * query_slots) // query_slots
    cols = jnp.arange(items * key_slots) // key_slots
    same = rows[:, None] == cols[None, :]
    return jnp.where(same[None], key_bias.reshape(blocks, 1, items * key_slots), -1e30).astype(f32)


def exchange(value, step):
    def partner(i):
        if step == 0:
            return i ^ 1
        return i ^ (2 if (step == 1) == (i % 2 == 0) else 4)

    return lax.ppermute(value, "fsdp", [(i, partner(i)) for i in range(SLOTS)])


def replica_exchange(value, bit):
    return lax.ppermute(value, "dp", [(i, i ^ (1 << bit)) for i in range(4)])


class Gather:
    def __init__(self, run, *shards):
        self.run = run
        self.pieces = [shard.reshape(1, -1, shard.shape[-1]) for shard in shards]
        self.got = [exchange(p, 1) for p in self.pieces]

    def join(self, along):
        joined = join_pieces(self.run, list(zip(self.pieces, self.got)), along)
        self.pieces = joined[: len(self.pieces)]
        return joined[len(self.pieces) :]

    def step(self, *along):
        later = self.join(along)
        self.got = [exchange(p, 2) for p in self.pieces]
        return later

    def finish(self, *along):
        later = self.join(along)
        return [(p, exchange(p, 0)) for p in self.pieces], later


class Reduction:
    def __init__(self, run, kind, share, z, keep, send, by_exchange):
        self.run, self.kind, self.share, self.z, self.by_exchange = run, kind, share, z, by_exchange
        self.state = (keep, exchange(send, 0))

    def first(self):
        held, sent = add_halves(self.run, *self.state)
        self.state = (held, exchange(sent, 1))

    def second(self):
        held, sent = add_halves(self.run, *self.state)
        self.state = (held, exchange(sent, 2))

    def last(self):
        if not self.by_exchange:
            self.state = lax.psum(add_last(self.run, None, *self.state), "dp")
            return
        held, sent = add_last(self.run, self.z, *self.state)
        self.state = (held, replica_exchange(sent, 0))

    def halve(self):
        held, sent = replicas_halve(self.run, self.z, *self.state)
        self.state = (held, replica_exchange(sent, 1))

    def sum(self):
        own = replicas_sum(self.run, *self.state)
        self.state = (own, replica_exchange(own, 1))

    def join(self):
        own = replicas_join(self.run, self.z, *self.state)
        self.state = (own, replica_exchange(own, 0))

    def out(self):
        if self.by_exchange:
            return shard_of_halves(self.run, self.kind, self.share, self.z, *self.state)
        return shard_of_sum(self.run, self.kind, self.share, self.state)


def unswapped(keep, send, block, count):
    width, wide = block * SLOTS, keep.shape[1]
    rows = jnp.concatenate([keep, send]).reshape(SLOTS, -1, wide)
    matrices = rows[:, : count * block].reshape(SLOTS, count, block, wide).transpose(1, 0, 2, 3).reshape(count, width, wide)
    pieces = [lax.psum_scatter(matrices, "fsdp", scatter_dimension=1, tiled=True)]
    if rows.shape[1] > count * block:
        vectors = rows[:, count * block :, :block].transpose(1, 0, 2).reshape(VECTOR_ROWS, width)
        pieces.append(lax.psum_scatter(vectors, "fsdp", scatter_dimension=1, tiled=True))
    return [piece.astype(f32) for piece in lax.psum(pieces, "dp")]


def local(
    words_in, regions_in, word_mask, region_count,
    cross_matrices, cross_vectors, word_self_matrices, word_self_vectors,
    region_self_matrices, region_self_vectors, word_feed_matrices, word_feed_vectors,
    region_feed_matrices, region_feed_vectors, words_cotangent, regions_cotangent,
):
    items, words, width = words_in.shape
    regions = regions_in.shape[1]
    share = cross_matrices.shape[1]
    count = width // share
    blocks = 3 if items % 12 == 0 else 1
    swaps = count == SLOTS
    me = lax.axis_index("fsdp").astype(jnp.int32).reshape(1)
    z = lax.axis_index("dp").astype(jnp.int32).reshape(1)

    own = jnp.concatenate([cross_vectors, word_self_vectors, region_self_vectors, word_feed_vectors, region_feed_vectors], axis=0)
    def whole(shard):
        return lax.all_gather(shard, "fsdp", axis=1, tiled=True)

    run = Sequence()

    word_bias = (word_mask.astype(f32) - 1.0) * 10000.0
    region_bias = jnp.where(jnp.arange(regions)[None, :] < region_count[:, None], 0.0, negative).astype(f32)
    word_rows = words_in.reshape(-1, width)
    region_rows = regions_in.reshape(-1, width)
    wr = block_bias(words, regions, region_bias, blocks)
    rw = block_bias(regions, words, word_bias, blocks)
    ww = block_bias(words, words, word_bias, blocks)
    rr = block_bias(regions, regions, region_bias, blocks)

    block = width // SLOTS
    word_cot = words_cotangent.reshape(-1, width)
    region_cot = regions_cotangent.reshape(-1, width)
    if swaps:
        own = jnp.pad(own, ((0, VECTOR_ROWS - own.shape[0]), (0, 128 - share)))
        cross_gather = Gather(run, cross_matrices, own)
        region_gather = Gather(run, region_self_matrices)
        cross_gather.step()
        region_gather.step()
        run.after(wr, rw, ww, rr, word_rows, region_rows, word_cot, region_cot)
        (cross, vector_parts), (region_feed_shard,) = cross_gather.finish(region_feed_matrices)
        region_feed = whole(region_feed_shard)
        vectors = jnp.zeros((8, 128), bf16)
    else:
        own = jnp.pad(own, ((0, VECTOR_ROWS - own.shape[0]), (0, 0)))
        vectors, vector_parts = lax.all_gather(own, "fsdp", axis=1, tiled=True), ()
        cross, region_self, word_self = ((whole(w),) for w in (cross_matrices, region_self_matrices, word_self_matrices))
        region_feed, word_feed = whole(region_feed_matrices), whole(word_feed_matrices)

    def reduction(kind, keep, send, by_exchange):
        return Reduction(run, kind, share, z, keep, send, by_exchange and lax.axis_size("dp") == 4) if swaps else None

    def step(group, name):
        return getattr(group, name)() if swaps else None

    word_one, region_one, word_kept, region_kept, vectors = cross_forward(run, me, word_rows, region_rows, cross, vectors, vector_parts, wr, rw)
    if swaps:
        ((region_self,), (word_shard, word_feed_shard)) = region_gather.finish(word_self_matrices, word_feed_matrices)
        word_feed = whole(word_feed_shard)
        word_gather = Gather(run, word_shard)
    region_two, region_self_kept = self_forward(run, REGION_SELF, me, region_one, region_self, vectors, rr)

    if swaps:
        word_gather.step()
    run.between = False
    regions_out, region_dtwo, keep_rf, send_rf, dvec_a = feed_both(
        run, REGION_SELF, REGION_FEED, swaps, me, region_two, region_cot, region_feed, vectors
    )
    if swaps:
        ((word_self,), _) = word_gather.finish()
    rf = reduction("feed", keep_rf, send_rf, False)
    region_done, keep_rs, send_rs, dvec_b = self_backward(
        run, REGION_SELF, blocks, swaps, me, region_dtwo, region_one, region_self, vectors, region_self_kept
    )
    rs = reduction("self", keep_rs, send_rs, True)
    step(rf, "first")
    word_two, word_self_kept = self_forward(run, WORD_SELF, me, word_one, word_self, vectors, ww)
    words_out, word_dtwo, keep_wf, send_wf, dvec_c = feed_both(
        run, WORD_SELF, WORD_FEED, swaps, me, word_two, word_cot, word_feed, vectors
    )
    wf = reduction("feed", keep_wf, send_wf, True)
    step(rs, "first")
    step(rf, "second")
    step(wf, "first")
    region_grads = region_side(run, blocks, me, region_done, cross, region_kept)
    step(rf, "last")
    step(rs, "second")
    word_done, keep_ws, send_ws, dvec_d = self_backward(
        run, WORD_SELF, blocks, swaps, me, word_dtwo, word_one, word_self, vectors, word_self_kept
    )
    ws = reduction("self", keep_ws, send_ws, True)
    step(wf, "second")
    step(rs, "last")
    words_grad, regions_grad, keep_cr, send_cr = cross_backward(
        run, blocks, swaps, me, word_done, region_done, word_rows, region_rows, cross,
        (dvec_a, dvec_b, dvec_c, dvec_d), word_kept, region_kept[4], region_grads,
    )
    run.between = True
    cr = reduction("cross", keep_cr, send_cr, True)

    if swaps:
        (held, sent), (own, other), (kept, far) = add_three(run, z, ws.state, wf.state, rs.state)
        ws.state = (held, exchange(sent, 1))
        wf.state = (own, replica_exchange(other, 0))
        rs.state = (kept, replica_exchange(far, 1))
        cr.first()
        ws.second()
        wf.halve()
        rs.sum()
        (grad_rf,) = rf.out()
        cr.second()
        words_grad, regions_grad, _ = lax.optimization_barrier((words_grad, regions_grad, run.token))
        ws.last()
        wf.sum()
        rs.join()
        cr.last()
        ws.halve()
        wf.join()
        (grad_rs,) = rs.out()
        cr.halve()
        ws.sum()
        (grad_wf,) = wf.out()
        cr.sum()
        ws.join()
        cr.join()
        (grad_ws,) = ws.out()
        grad_cr, *vector_grads = cr.out()
    else:
        (grad_rf,), (grad_wf,) = unswapped(keep_rf, send_rf, block, 2), unswapped(keep_wf, send_wf, block, 2)
        (grad_rs,), (grad_ws,) = unswapped(keep_rs, send_rs, block, 4), unswapped(keep_ws, send_ws, block, 4)
        grad_cr, vector_sum = unswapped(keep_cr, send_cr, block, 4)
        vector_grads = [vector_sum[start : start + number] for start, number in VECTOR_PARTS]

    return (
        words_out.reshape(items, words, width),
        regions_out.reshape(items, regions, width),
        words_grad.reshape(items, words, width),
        regions_grad.reshape(items, regions, width),
        grad_cr,
        vector_grads[0],
        grad_ws,
        vector_grads[1],
        grad_rs,
        vector_grads[2],
        grad_wf,
        vector_grads[3],
        grad_rf,
        vector_grads[4],
    )


def solution(mesh):
    items = P(("dp", "fsdp"), None, None)
    matrix = P(None, "fsdp", None)
    vector = P(None, "fsdp")
    weights = (matrix, vector) * 5
    return jax.shard_map(
        local,
        mesh=mesh,
        in_specs=(items, items, P(("dp", "fsdp"), None), P(("dp", "fsdp")), *weights, items, items),
        out_specs=(items,) * 4 + weights,
        check_vma=False,
    )
```

```python
from functools import partial
import math

import jax
import jax.numpy as jnp
from jax import lax
from jax.sharding import PartitionSpec as P
from jax.experimental import pallas as pl
from jax.experimental.pallas import tpu as pltpu

HEADS = 12
epsilon = 1e-12
negative = -10000.0
bf16 = jnp.bfloat16
f32 = jnp.float32

CROSS, WORD_SELF, REGION_SELF, WORD_FEED, REGION_FEED = 0, 5, 10, 15, 22
VECTOR_ROWS = 32


def nn(left, right):
    return jnp.dot(left, right, preferred_element_type=f32)


def nt(left, right):
    return lax.dot_general(left, right, (((1,), (1,)), ((), ())), preferred_element_type=f32)


def tn(left, right):
    return lax.dot_general(left, right, (((0,), (0,)), ((), ())), preferred_element_type=f32)


def norm_parts(total):
    centred = total - jnp.mean(total, axis=-1, keepdims=True)
    spread = jnp.mean(centred * centred, axis=-1, keepdims=True)
    rate = lax.rsqrt(spread + epsilon)
    return centred * rate, rate


def norm_back(grad, unit, rate, gain):
    scaled = grad * gain
    mean_one = jnp.mean(scaled, axis=-1, keepdims=True)
    mean_two = jnp.mean(scaled * unit, axis=-1, keepdims=True)
    return (
        rate * (scaled - mean_one - unit * mean_two),
        jnp.sum(grad * unit, axis=0, keepdims=True),
        jnp.sum(grad, axis=0, keepdims=True),
    )


def half_masks(rows):
    lane = lax.broadcasted_iota(jnp.int32, (rows, 128), 1)
    return (lane < 64, lane >= 64)


def heads_forward(q_ref, k_ref, v_ref, bias_ref, probs_ref, ctx_ref):
    blocks, qb, kb = bias_ref.shape
    pairs = q_ref.shape[1] // 128
    masks = half_masks(kb)
    zero = jnp.zeros((kb, 128), bf16)

    def block(b, carry):
        rq = pl.ds(pl.multiple_of(b * qb, 16), qb)
        rk = pl.ds(pl.multiple_of(b * kb, 16), kb)
        bias = bias_ref[b]
        for p in range(pairs):
            cols = pl.ds(p * 128, 128)
            qp = q_ref[rq, cols]
            kp = k_ref[rk, cols]
            vp = v_ref[rk, cols]
            mixed = None
            for half in range(2):
                s = nt(qp, jnp.where(masks[half], kp, zero)) * 0.125 + bias
                e = jnp.exp(s - jnp.max(s, axis=-1, keepdims=True))
                low = (e / jnp.sum(e, axis=-1, keepdims=True)).astype(bf16)
                probs_ref[b * (2 * pairs) + 2 * p + half] = low
                part = nn(low, jnp.where(masks[half], vp, zero))
                mixed = part if mixed is None else mixed + part
            ctx_ref[rq, cols] = mixed.astype(bf16)
        return carry

    lax.fori_loop(0, blocks, block, 0, unroll=True)


def heads_backward(q_ref, k_ref, v_ref, probs_ref, dctx_ref, dq_ref, dk_ref, dv_ref, blocks):
    qb = q_ref.shape[0] // blocks
    kb = k_ref.shape[0] // blocks
    pairs = q_ref.shape[1] // 128
    kmasks, qmasks = half_masks(kb), half_masks(qb)
    kzero, qzero = jnp.zeros((kb, 128), bf16), jnp.zeros((qb, 128), bf16)

    def block(b, carry):
        rq = pl.ds(pl.multiple_of(b * qb, 16), qb)
        rk = pl.ds(pl.multiple_of(b * kb, 16), kb)
        for p in range(pairs):
            cols = pl.ds(p * 128, 128)
            qp = q_ref[rq, cols]
            kp = k_ref[rk, cols]
            vp = v_ref[rk, cols]
            dc = dctx_ref[rq, cols]
            dq = dk = dv = 0.0
            for half in range(2):
                low = probs_ref[b * (2 * pairs) + 2 * p + half]
                probs = low.astype(f32)
                dp = nt(dc, jnp.where(kmasks[half], vp, kzero))
                dv = dv + tn(low, jnp.where(qmasks[half], dc, qzero))
                t = probs * dp
                ds = (t - probs * jnp.sum(t, axis=-1, keepdims=True)).astype(bf16)
                dq = dq + nn(ds, jnp.where(kmasks[half], kp, kzero))
                dk = dk + tn(ds, jnp.where(qmasks[half], qp, qzero))
            dq_ref[rq, cols] = (dq * 0.125).astype(bf16)
            dk_ref[rk, cols] = (dk * 0.125).astype(bf16)
            dv_ref[rk, cols] = dv.astype(bf16)
        return carry

    lax.fori_loop(0, blocks, block, 0, unroll=True)


def vec(vec_ref, row):
    return vec_ref[row : row + 1, :]


def attend(moves, x_low, c_low, base, w_ref, vec_ref, row, bias_ref, q_ref, k_ref, v_ref, probs_ref, ctx_ref):
    q_ref[...] = (nn(x_low, w_ref[0]) + vec(vec_ref, row)).astype(bf16)
    k_ref[...] = nn(c_low, w_ref[1]).astype(bf16)
    v_ref[...] = (nn(c_low, w_ref[2]) + vec(vec_ref, row + 1)).astype(bf16)
    moves.leave(q_ref, k_ref, v_ref)
    heads_forward(q_ref, k_ref, v_ref, bias_ref, probs_ref, ctx_ref)
    moves.leave(probs_ref, ctx_ref)
    return base + nn(ctx_ref[...], w_ref[3]) + vec(vec_ref, row + 2)


def cross_forward_kernel(count, moves, me_ref, words_ref, regions_ref, known_ref, wr_ref, rw_ref, *refs):
    vector_parts, refs = (refs[:2], refs[2:]) if count == 2 else ((), refs)
    parts, refs = refs[:count], refs[count:]
    wtot_ref, rtot_ref, wq_ref, wk_ref, wv_ref, wp_ref, wc_ref, rq_ref, rk_ref, rv_ref, rp_ref, rc_ref = refs[:12]
    vec_ref, w_ref, vt_ref, sems = refs[12:]
    copies = fetch(parts, me_ref[0], w_ref, sems, vector_parts, vt_ref)
    moves.arrive()
    settle(copies)
    if count == 1:
        vec_ref[...] = known_ref[...].astype(f32)
    else:
        block = w_ref.shape[1] // SLOTS
        for s in range(SLOTS):
            vec_ref[:, s * block : (s + 1) * block] = vt_ref[s ^ me_ref[0]][:, :block].astype(f32)
    words, regions = words_ref[...], regions_ref[...]
    wtot_ref[...] = attend(moves, words, regions, words.astype(f32), w_ref, vec_ref, CROSS, wr_ref, wq_ref, wk_ref, wv_ref, wp_ref, wc_ref)
    moves.leave(wtot_ref)
    rtot_ref[...] = attend(moves, regions, words, regions.astype(f32), w_ref, vec_ref, CROSS, rw_ref, rq_ref, rk_ref, rv_ref, rp_ref, rc_ref)


def self_forward_kernel(row, count, moves, me_ref, tot_ref, vec_ref, bias_ref, *refs):
    parts = refs[:count]
    out_ref, q_ref, k_ref, v_ref, p_ref, c_ref, w_ref, sems = refs[count:]
    copies = fetch(parts, me_ref[0], w_ref, sems)
    moves.arrive()
    unit, _ = norm_parts(tot_ref[...])
    y = unit * vec(vec_ref, CROSS + 3) + vec(vec_ref, CROSS + 4)
    low = y.astype(bf16)
    settle(copies)
    out_ref[...] = attend(moves, low, low, y, w_ref, vec_ref, row, bias_ref, q_ref, k_ref, v_ref, p_ref, c_ref)


def gelu_parts(x):
    size = jnp.abs(x)
    e = jnp.exp(x * x * -0.5)
    t = 1.0 / (1.0 + (0.3275911 * 0.7071067811865476) * size)
    poly = t * (0.127414796 + t * (-0.142248368 + t * (0.7107068705 + t * (-0.7265760135 + t * 0.5307027145))))
    tail = poly * e
    phi = jnp.where(x >= 0, 1.0 - tail, tail)
    return x * phi, phi + x * e * 0.3989422804014327


def slot_of(s, me):
    k = s ^ me
    core, x, y = k & 1, (k >> 1) & 1, (k >> 2) & 1
    flip = (me & 1) ^ core
    return core * 4 + jnp.where(flip == 0, x * 2 + y, y * 2 + x)


def place(dest_ref, value, me):
    if me is None:
        dest_ref[...] = value
        return
    rows = value.shape[0] // SLOTS
    for s in range(SLOTS):
        dest_ref[pl.ds(pl.multiple_of(slot_of(s, me) * rows, 16), rows), :] = value[s * rows : (s + 1) * rows, :]


SLOTS = 8


def put(keep_ref, send_ref, base, stride, cols, value):
    rows = value.shape[0] // SLOTS
    low = value.astype(bf16)
    for j in range(SLOTS):
        dest = keep_ref if j < SLOTS // 2 else send_ref
        start = base + (j % (SLOTS // 2)) * stride
        dest[start : start + rows, cols] = low[j * rows : (j + 1) * rows]


def feed_kernel(
    self_row, row, chunk, swaps,
    moves, me_ref, tot_ref, cot_ref, far_ref, vec_ref,
    out_ref, dtot_ref, far_keep_ref, far_send_ref, dvec_ref,
    x_ref, y_ref, h_ref, gp_ref, dpre_ref, dy_ref, xt_ref, dyt_ref, acc_ref, bup_ref, dbup_ref,
    m_ref, keep_ref, send_ref, in_sems, out_sems,
):
    me = me_ref[0] if swaps else None
    copies = [pltpu.make_async_copy(far_ref.at[m], m_ref.at[m], in_sems.at[m]) for m in range(2)]
    for copy in copies:
        copy.start()
    moves.arrive()
    width = tot_ref.shape[1]
    hidden = m_ref.shape[2]
    parts = hidden // width
    block = width // SLOTS
    for i in range(parts):
        bup_ref[:, i * width : (i + 1) * width] = vec(vec_ref, row + i)
    unit2, rate2 = norm_parts(tot_ref[...])
    y = unit2 * vec(vec_ref, self_row + 3) + vec(vec_ref, self_row + 4)
    y_ref[...] = y
    x_ref[...] = y.astype(bf16)
    copies[0].wait()

    def up(i, carry):
        cols = pl.ds(pl.multiple_of(i * chunk, 128), chunk)
        pre = nn(x_ref[...], m_ref[0, :, cols]) + bup_ref[:, cols]
        value, slope = gelu_parts(pre)
        h_ref[:, cols] = value.astype(bf16)
        gp_ref[:, cols] = slope
        return carry

    lax.fori_loop(0, hidden // chunk, up, 0)
    copies[1].wait()

    def down(i, carry):
        cols = pl.ds(0, width)
        acc_ref[:, cols] = nt(h_ref[...], m_ref[1, pl.ds(0, width), :])
        return carry

    lax.fori_loop(0, 1, down, 0, unroll=True)
    gain = vec(vec_ref, row + 5)
    unit, rate = norm_parts(y_ref[...] + acc_ref[...] + vec(vec_ref, row + 4))
    out_ref[...] = (unit * gain + vec(vec_ref, row + 6)).astype(bf16)
    moves.leave(out_ref)
    dtot, dgain, dshift = norm_back(cot_ref[...].astype(f32), unit, rate, gain)
    dy = dtot.astype(bf16)
    dy_ref[...] = dy
    dvec_ref[...] = jnp.zeros_like(dvec_ref)
    dvec_ref[row + 4 : row + 5, :] = jnp.sum(dy.astype(f32), axis=0, keepdims=True)
    dvec_ref[row + 5 : row + 6, :] = dgain
    dvec_ref[row + 6 : row + 7, :] = dshift
    y_ref[...] = dtot
    place(xt_ref, x_ref[...].T, me)
    place(dyt_ref, dy.T, me)

    def leaving(i):
        cols = pl.ds(pl.multiple_of(i * chunk, 128), chunk)
        return (
            pltpu.make_async_copy(keep_ref.at[:, cols], far_keep_ref.at[:, cols], out_sems.at[i, 0]),
            pltpu.make_async_copy(send_ref.at[:, cols], far_send_ref.at[:, cols], out_sems.at[i, 1]),
        )

    def back(i, carry):
        cols = pl.ds(pl.multiple_of(i * chunk, 128), chunk)
        dpre = (nn(dy_ref[...], m_ref[1, :, cols]) * gp_ref[:, cols]).astype(bf16)
        dpre_ref[:, cols] = dpre
        dbup_ref[:, cols] = jnp.sum(dpre.astype(f32), axis=0, keepdims=True)
        put(keep_ref, send_ref, 0, 2 * block, cols, nn(xt_ref[...], dpre))
        put(keep_ref, send_ref, block, 2 * block, cols, nn(dyt_ref[...], h_ref[:, cols]))
        for copy in leaving(i):
            copy.start()
        return carry

    lax.fori_loop(0, hidden // chunk, back, 0)
    for i in range(parts):
        dvec_ref[row + i : row + i + 1, :] = dbup_ref[:, i * width : (i + 1) * width]

    def rows(i, carry):
        cols = pl.ds(0, width)
        acc_ref[:, cols] = nt(dpre_ref[...], m_ref[0, pl.ds(0, width), :])
        return carry

    lax.fori_loop(0, 1, rows, 0, unroll=True)
    unit2, rate2 = norm_parts(tot_ref[...])
    dtot2, dgain2, dshift2 = norm_back(acc_ref[...] + y_ref[...], unit2, rate2, vec(vec_ref, self_row + 3))
    dtot_ref[...] = dtot2
    dvec_ref[self_row + 3 : self_row + 4, :] = dgain2
    dvec_ref[self_row + 4 : self_row + 5, :] = dshift2
    for i in range(hidden // chunk):
        settle(leaving(i))


def column_sum(low):
    return jnp.sum(low.astype(f32), axis=0, keepdims=True)


def self_backward_kernel(
    row, blocks, swaps, count,
    moves, me_ref, dtot_ref, tot_ref, vec_ref, q_ref, k_ref, v_ref, p_ref, c_ref, *refs,
):
    parts = refs[:count]
    out_ref, keep_ref, send_ref, dvec_ref, dq_ref, dk_ref, dv_ref, dc_ref, xt_ref, ct_ref, w_ref, sems = refs[count:]
    me = me_ref[0] if swaps else None
    copies = fetch(parts, me, w_ref, sems)
    moves.arrive()
    da = dtot_ref[...].astype(bf16)
    dvec_ref[...] = jnp.zeros_like(dvec_ref)
    dvec_ref[row + 2 : row + 3, :] = column_sum(da)
    place(ct_ref, c_ref[...].T, me)
    width = w_ref.shape[2]
    every = pl.ds(0, width)
    block = width // SLOTS
    put(keep_ref, send_ref, 3 * block, 4 * block, every, nn(ct_ref[...], da))
    settle(copies)
    dc_ref[...] = nt(da, w_ref[3]).astype(bf16)
    heads_backward(q_ref, k_ref, v_ref, p_ref, dc_ref, dq_ref, dk_ref, dv_ref, blocks)
    unit, rate = norm_parts(tot_ref[...])
    gain = vec(vec_ref, CROSS + 3)
    low = (unit * gain + vec(vec_ref, CROSS + 4)).astype(bf16)
    place(xt_ref, low.T, me)
    dq, dk, dv = dq_ref[...], dk_ref[...], dv_ref[...]
    put(keep_ref, send_ref, 0, 4 * block, every, nn(xt_ref[...], dq))
    put(keep_ref, send_ref, block, 4 * block, every, nn(xt_ref[...], dk))
    put(keep_ref, send_ref, 2 * block, 4 * block, every, nn(xt_ref[...], dv))
    moves.leave(keep_ref, send_ref)
    dvec_ref[row : row + 1, :] = column_sum(dq)
    dvec_ref[row + 1 : row + 2, :] = column_sum(dv)
    dx = dtot_ref[...] + nt(dq, w_ref[0]) + nt(dk, w_ref[1]) + nt(dv, w_ref[2])
    dtot, dgain, dshift = norm_back(dx, unit, rate, gain)
    out_ref[...] = dtot
    dvec_ref[CROSS + 3 : CROSS + 4, :] = dgain
    dvec_ref[CROSS + 4 : CROSS + 5, :] = dshift


def region_side_kernel(
    blocks, count,
    moves, me_ref, dr_ref, rq_ref, rk_ref, rv_ref, rp_ref, *refs,
):
    rdq_ref, rdk_ref, rdv_ref, rpart_ref, wpart_ref, rdc_ref, w_ref, sems = refs[count:]
    copies = fetch(refs[:count], me_ref[0], w_ref, sems)
    moves.arrive()
    settle(copies)
    rdc_ref[...] = nt(dr_ref[...].astype(bf16), w_ref[3]).astype(bf16)
    heads_backward(rq_ref, rk_ref, rv_ref, rp_ref, rdc_ref, rdq_ref, rdk_ref, rdv_ref, blocks)
    moves.leave(rdq_ref, rdk_ref, rdv_ref)
    rpart_ref[...] = dr_ref[...] + nt(rdq_ref[...], w_ref[0])
    wpart_ref[...] = nt(rdk_ref[...], w_ref[1]) + nt(rdv_ref[...], w_ref[2])


def cross_backward_kernel(
    blocks, swaps, count,
    moves, me_ref, dw_ref, dr_ref, words_ref, regions_ref, va_ref, vb_ref, vc_ref, vd_ref,
    wq_ref, wk_ref, wv_ref, wp_ref, wc_ref, rc_ref, rdq_ref, rdk_ref, rdv_ref, rpart_ref, wpart_ref, *refs,
):
    parts, refs = refs[:count], refs[count:]
    wout_ref, rout_ref, keep_ref, send_ref, wdq_ref, wdk_ref, wdv_ref, wdc_ref, wct_ref, rct_ref = refs[:10]
    wt_ref, rt_ref, dvec_ref, vt_ref, w_ref, sems = refs[10:]
    me = me_ref[0] if swaps else None
    copies = fetch(parts, me, w_ref, sems)
    moves.arrive()
    width = w_ref.shape[2]
    every = pl.ds(0, width)
    block = width // SLOTS
    stride = 4 * block + VECTOR_ROWS
    wda, rda = dw_ref[...].astype(bf16), dr_ref[...].astype(bf16)
    dvec_ref[...] = va_ref[...] + vb_ref[...] + vc_ref[...] + vd_ref[...]
    dvec_ref[CROSS + 2 : CROSS + 3, :] = column_sum(wda) + column_sum(rda)
    place(wct_ref, wc_ref[...].T, me)
    place(rct_ref, rc_ref[...].T, me)
    put(keep_ref, send_ref, 3 * block, stride, every, nn(wct_ref[...], wda) + nn(rct_ref[...], rda))
    settle(copies)
    wdc_ref[...] = nt(wda, w_ref[3]).astype(bf16)
    heads_backward(wq_ref, wk_ref, wv_ref, wp_ref, wdc_ref, wdq_ref, wdk_ref, wdv_ref, blocks)
    place(wt_ref, words_ref[...].T, me)
    place(rt_ref, regions_ref[...].T, me)
    wdq, wdk, wdv = wdq_ref[...], wdk_ref[...], wdv_ref[...]
    rdq, rdk, rdv = rdq_ref[...], rdk_ref[...], rdv_ref[...]
    put(keep_ref, send_ref, 0, stride, every, nn(wt_ref[...], wdq) + nn(rt_ref[...], rdq))
    put(keep_ref, send_ref, block, stride, every, nn(rt_ref[...], wdk) + nn(wt_ref[...], rdk))
    put(keep_ref, send_ref, 2 * block, stride, every, nn(rt_ref[...], wdv) + nn(wt_ref[...], rdv))
    dvec_ref[CROSS : CROSS + 1, :] = column_sum(wdq) + column_sum(rdq)
    dvec_ref[CROSS + 1 : CROSS + 2, :] = column_sum(wdv) + column_sum(rdv)
    vt_ref[...] = jnp.zeros_like(vt_ref)
    for s in range(SLOTS):
        slot = slot_of(s, me) if swaps else s
        vt_ref[pl.ds(pl.multiple_of(slot * VECTOR_ROWS, 16), VECTOR_ROWS), 0:block] = dvec_ref[:, s * block : (s + 1) * block].astype(bf16)
    for j in range(SLOTS):
        dest = keep_ref if j < SLOTS // 2 else send_ref
        start = (j % (SLOTS // 2)) * stride + 4 * block
        dest[start : start + VECTOR_ROWS, :] = vt_ref[j * VECTOR_ROWS : (j + 1) * VECTOR_ROWS, :]
    moves.leave(keep_ref, send_ref)
    wout_ref[...] = (dw_ref[...] + nt(wdq, w_ref[0]) + wpart_ref[...]).astype(bf16)
    rout_ref[...] = (rpart_ref[...] + nt(wdk, w_ref[1]) + nt(wdv, w_ref[2])).astype(bf16)


MIB = 1024 * 1024


SCALE = 20


class Moves:
    def __init__(self, ins, outs, sems):
        self.ins = [pltpu.make_async_copy(source, dest, sems.at[i]) for i, (source, dest) in enumerate(ins)]
        self.outs = [(ref, pltpu.make_async_copy(ref, dest, sems.at[len(ins) + i])) for i, (ref, dest) in enumerate(outs)]
        self.left = set()
        for copy in self.ins:
            copy.start()

    def arrive(self):
        for copy in self.ins:
            copy.wait()

    def leave(self, *refs):
        for i, (ref, copy) in enumerate(self.outs):
            if any(ref is r for r in refs):
                copy.start()
                self.left.add(i)

    def finish(self):
        for i, (_, copy) in enumerate(self.outs):
            if i not in self.left:
                copy.start()
        for _, copy in self.outs:
            copy.wait()


class Far:
    def __init__(self, array):
        self.array = array


class Scalar:
    def __init__(self, array):
        self.array = array


class Sequence:
    def __init__(self):
        self.token = self.more = ()
        self.free = False
        self.between = True

    def after(self, *arrays):
        self.more += arrays

    def __call__(self, kernel, name, outs, scratch, us, args, far_outs=(), small=False, manual=False, grid=None, in_specs=None, out_specs=None):
        here, far = pl.BlockSpec(memory_space=pltpu.VMEM), pl.BlockSpec(memory_space=pl.ANY)
        moved_in = [i for i, a in enumerate(args) if manual and not isinstance(a, (Far, Scalar))]
        moved_out = [i for i in range(len(outs)) if manual and i not in far_outs]
        if in_specs is None:
            kinds = {Far: far, Scalar: pl.BlockSpec(memory_space=pltpu.SMEM)}
            in_specs = [kinds.get(type(a), here) for a in args]
            out_specs = [far if manual or i in far_outs else here for i in range(len(outs))]
            in_specs = [far if i in moved_in else spec for i, spec in enumerate(in_specs)]
        arrays = [a.array if isinstance(a, (Far, Scalar)) else a for a in args]
        out_shape = tuple(jax.ShapeDtypeStruct(s, d) for s, d in outs)
        moved = sum(a.size * a.dtype.itemsize for a in arrays) + sum(o.size * o.dtype.itemsize for o in out_shape)
        small = small and self.between
        if grid is None:
            held = [a for a in args if not isinstance(a, (Far, Scalar))] + [jax.ShapeDtypeStruct(*o) for i, o in enumerate(outs) if i not in far_outs]
            held += [jax.ShapeDtypeStruct(*s) for s in scratch if isinstance(s, tuple)]
            held = sum(math.prod(h.shape) * jnp.dtype(h.dtype).itemsize for h in held)
            limit = int(1.15 * held) + 2 * MIB if small else 60 * MIB
        else:
            limit = 16 * MIB if small else 60 * MIB
        token = self.token + self.more
        self.more = ()

        scratch = list(scratch)
        own = len(scratch)
        if manual:
            scratch += [(arrays[i].shape, arrays[i].dtype) for i in moved_in] + [outs[i] for i in moved_out]
            scratch.append(pltpu.SemaphoreType.DMA((len(moved_in) + len(moved_out),)))

        def body(*refs):
            taken, rest = list(refs[: len(arrays)]), refs[len(arrays) + len(token) :]
            given, rest = list(rest[: len(outs)]), rest[len(outs) :]
            if not manual:
                kernel(*taken, *given, *rest)
                return
            buffers = rest[own:]
            ins = [(taken[i], buffers[j]) for j, i in enumerate(moved_in)]
            leaving = [(buffers[len(moved_in) + j], given[i]) for j, i in enumerate(moved_out)]
            for j, i in enumerate(moved_in):
                taken[i] = buffers[j]
            for j, i in enumerate(moved_out):
                given[i] = buffers[len(moved_in) + j]
            moves = Moves(ins, leaving, buffers[-1])
            kernel(moves, *taken, *given, *rest[:own])
            moves.finish()

        extra = {} if grid is None else {"grid": grid}
        got = pl.pallas_call(
            body,
            out_shape=out_shape,
            in_specs=list(in_specs) + [far] * len(token),
            out_specs=tuple(out_specs),
            scratch_shapes=[pltpu.VMEM(*s) if isinstance(s, tuple) else s for s in scratch],
            compiler_params=pltpu.CompilerParams(vmem_limit_bytes=limit),
            cost_estimate=pl.CostEstimate(flops=int(us * SCALE * 1.15e9), bytes_accessed=0, transcendentals=0),
            name=name,
            **extra,
        )(*arrays, *token)
        self.token = () if self.free else (min(got, key=lambda o: o.size * o.dtype.itemsize),)
        return got


def fetch(parts, me, w_ref, sems, vector_parts=(), vt_ref=None):
    copies = []

    def start(source, dest):
        copies.append(pltpu.make_async_copy(source, dest, sems.at[len(copies)]))
        copies[-1].start()

    if len(parts) == 1:
        for m in range(4):
            start(parts[0].at[m], w_ref.at[m])
        return copies
    block = w_ref.shape[1] // SLOTS
    for other in range(2):
        odd = ((me & 1) ^ other) == 1
        for i in range(4):
            k = jnp.where(odd, (i & 1) * 4 + (i >> 1) * 2, (i & 1) * 2 + (i >> 1) * 4) + other
            rows = pl.ds(pl.multiple_of((k ^ me) * block, 16), block)
            for m in range(4):
                start(parts[other].at[i, pl.ds(m * block, block)], w_ref.at[m, rows, :])
            if vt_ref is not None:
                start(vector_parts[other].at[i], vt_ref.at[k])
    return copies


def settle(copies):
    for copy in copies:
        copy.wait()


def kept_shapes(nq, nk, width, bias):
    blocks, qb, kb = bias.shape
    return [((nq, width), bf16), ((nk, width), bf16), ((nk, width), bf16), ((blocks * HEADS, qb, kb), bf16), ((nq, width), bf16)]


def attention_scratch(width):
    return [((4, width, width), bf16), pltpu.SemaphoreType.DMA((40,))]


def fars(parts):
    return [Far(p) for p in parts]


def cross_forward(run, me, words, regions, parts, vectors, vector_parts, wr, rw):
    nw, nr, width = words.shape[0], regions.shape[0], words.shape[1]
    outs = [((nw, width), f32), ((nr, width), f32)] + kept_shapes(nw, nr, width, wr) + kept_shapes(nr, nw, width, rw)
    outs += [((VECTOR_ROWS, width), f32)]
    scratch = attention_scratch(width)
    scratch.insert(1, ((SLOTS, VECTOR_ROWS, 128), bf16))
    args = (Scalar(me), words, regions, vectors, wr, rw, *fars(vector_parts), *fars(parts))
    got = run(partial(cross_forward_kernel, len(parts)), "cross_forward", outs, scratch, 0.05, args, manual=True)
    return got[0], got[1], got[2:7], got[7:12], got[12]


def self_forward(run, row, me, total, parts, vectors, bias):
    n, width = total.shape
    outs = [((n, width), f32)] + kept_shapes(n, n, width, bias)
    args = (Scalar(me), total, vectors, bias, *fars(parts))
    kernel = partial(self_forward_kernel, row, len(parts))
    got = run(kernel, "self_forward", outs, attention_scratch(width), 0.05, args, manual=True)
    return got[0], got[1:]


def feed_both(run, self_row, row, swaps, me, total, cot, m, vectors):
    n, width = total.shape
    hidden = m.shape[2]
    chunk = 1536
    half = (width, hidden)
    outs = [((n, width), bf16), ((n, width), f32), (half, bf16), (half, bf16), ((VECTOR_ROWS, width), f32)]
    scratch = [
        ((n, width), bf16), ((n, width), f32), ((n, hidden), bf16), ((n, hidden), f32), ((n, hidden), bf16),
        ((n, width), bf16), ((width, n), bf16), ((width, n), bf16), ((n, width), f32), ((1, hidden), f32), ((1, hidden), f32),
        ((2, width, hidden), bf16), (half, bf16), (half, bf16),
        pltpu.SemaphoreType.DMA((2,)), pltpu.SemaphoreType.DMA((hidden // chunk, 2)),
    ]
    args = (Scalar(me), total, cot, Far(m), vectors)
    return run(partial(feed_kernel, self_row, row, chunk, swaps), "feed", outs, scratch, 10 + n / 24, args, far_outs=(2, 3), manual=True)


def self_backward(run, row, blocks, swaps, me, dtot, total, parts, vectors, kept):
    n, width = total.shape
    half = (2 * width, width)
    outs = [((n, width), f32), (half, bf16), (half, bf16), ((VECTOR_ROWS, width), f32)]
    scratch = [((n, width), bf16)] * 4 + [((width, n), bf16)] * 2 + attention_scratch(width)
    args = (Scalar(me), dtot, total, vectors, *kept, *fars(parts))
    kernel = partial(self_backward_kernel, row, blocks, swaps, len(parts))
    return run(kernel, "self_backward", outs, scratch, 8 + n / 40, args, manual=True)


def region_side(run, blocks, me, dr, parts, kept):
    nr, width = dr.shape
    nw = kept[1].shape[0]
    outs = [((nr, width), bf16), ((nw, width), bf16), ((nw, width), bf16), ((nr, width), f32), ((nw, width), f32)]
    scratch = [((nr, width), bf16)] + attention_scratch(width)
    args = (Scalar(me), dr, *kept[:4], *fars(parts))
    return run(partial(region_side_kernel, blocks, len(parts)), "region_side", outs, scratch, 14, args, manual=True)


def cross_backward(run, blocks, swaps, me, dw, dr, words, regions, parts, dvecs, word_kept, region_ctx, region_grads):
    nw, nr, width = words.shape[0], regions.shape[0], words.shape[1]
    half = (2 * width + VECTOR_ROWS * (SLOTS // 2), width)
    outs = [((nw, width), bf16), ((nr, width), bf16), (half, bf16), (half, bf16)]
    scratch = [((nw, width), bf16), ((nr, width), bf16), ((nr, width), bf16), ((nw, width), bf16)]
    scratch += [((width, nw), bf16), ((width, nr), bf16)] * 2
    scratch += [((VECTOR_ROWS, width), f32), ((VECTOR_ROWS * SLOTS, width), bf16)] + attention_scratch(width)
    args = (Scalar(me), dw, dr, words, regions, *dvecs, *word_kept, region_ctx, *region_grads, *fars(parts))
    return run(partial(cross_backward_kernel, blocks, swaps, len(parts)), "cross_backward", outs, scratch, 20, args, manual=True)


def join_pieces(run, pairs, along=()):
    outs = [((2 * p.shape[0], *p.shape[1:]), p.dtype) for p, _ in pairs] + [(a.shape, a.dtype) for a in along]
    arrays = [a for pair in pairs for a in pair] + list(along)

    def kernel(*refs):
        taken, given = refs[: len(arrays)], refs[len(arrays) :]
        for i, (p, _) in enumerate(pairs):
            n = p.shape[0]
            given[i][:n] = taken[2 * i][...]
            given[i][n:] = taken[2 * i + 1][...]
        for i in range(len(along)):
            given[len(pairs) + i][...] = taken[2 * len(pairs) + i][...]

    return run(kernel, "join_pieces", outs, [], 2, arrays, small=True)


def plus(left, right):
    return (left.astype(f32) + right.astype(f32)).astype(bf16)


def columns_of(width):
    return width // 2 if width % 256 == 0 else width


def add_halves(run, keep, got):
    rows, width = keep.shape
    c = columns_of(width)
    half = rows // 2

    def kernel(keep_ref, got_ref, held_ref, sent_ref):
        held_ref[...] = plus(keep_ref[:half, :], got_ref[:half, :])
        sent_ref[...] = plus(keep_ref[half:, :], got_ref[half:, :])

    def block(n):
        return pl.BlockSpec((n, c), lambda i: (0, i))

    outs = [((half, width), bf16)] * 2
    return run(kernel, "add_halves", outs, [], 6, (keep, got), small=keep.size < MIB, grid=(width // c,), in_specs=[block(rows)] * 2, out_specs=[block(half)] * 2)


def padded(rows):
    return -(-rows // 64) * 64


def add_last(run, z, held, back):
    n, width = held.shape
    rows = padded(n)

    def fill(held_ref, back_ref, ref):
        ref[:n, :] = plus(held_ref[...], back_ref[...])
        if rows > n:
            ref[n:, :] = jnp.zeros((rows - n, width), bf16)

    if z is None:
        return run(fill, "add_last", [((rows, width), bf16)], [], 2.5, (held, back), small=True)[0]

    def kernel(z_ref, held_ref, back_ref, keep_ref, send_ref, all_ref):
        fill(held_ref, back_ref, all_ref)
        split_rows(all_ref, z_ref[0] & 1, keep_ref, send_ref)

    outs = [((rows // 2, width), bf16)] * 2
    return run(kernel, "add_last", outs, [((rows, width), bf16)], 2.5, (Scalar(z), held, back), small=True)


def add_three(run, z, first, last, halve):
    def kernel(moves, z_ref, keep_ref, got_ref, held_ref, back_ref, own_ref, other_ref, *refs):
        fh_ref, fs_ref, lk_ref, ls_ref, hk_ref, hs_ref, last_ref, halve_ref = refs
        moves.arrive()
        half = keep_ref.shape[0] // 2
        fs_ref[...] = plus(keep_ref[half:, :], got_ref[half:, :])
        moves.leave(fs_ref)
        last_ref[...] = plus(held_ref[...], back_ref[...])
        split_rows(last_ref, z_ref[0] & 1, lk_ref, ls_ref)
        moves.leave(ls_ref, lk_ref)
        halve_ref[...] = plus(own_ref[...], other_ref[...])
        split_rows(halve_ref, (z_ref[0] >> 1) & 1, hk_ref, hs_ref)
        moves.leave(hs_ref, hk_ref)
        fh_ref[...] = plus(keep_ref[:half, :], got_ref[:half, :])

    args = (Scalar(z), *first, *last, *halve)
    outs = [((pair[0].shape[0] // 2, pair[0].shape[1]), bf16) for pair in (first, first, last, last, halve, halve)]
    scratch = [(last[0].shape, bf16), (halve[0].shape, bf16)]
    got = run(kernel, "add_three", outs, scratch, 8, args, manual=True)
    return got[0:2], got[2:4], got[4:6]


def split_rows(all_ref, bit, keep_ref, send_ref):
    half = all_ref.shape[0] // 2
    keep_ref[...] = all_ref[pl.ds(pl.multiple_of(bit * half, 16), half), :]
    send_ref[...] = all_ref[pl.ds(pl.multiple_of((1 - bit) * half, 16), half), :]


def join_rows(own, other, bit, all_ref):
    half = own.shape[0]
    all_ref[pl.ds(pl.multiple_of(bit * half, 16), half), :] = own[...]
    all_ref[pl.ds(pl.multiple_of((1 - bit) * half, 16), half), :] = other[...]


def replicas_halve(run, z, held, back):
    rows, width = held.shape

    def kernel(z_ref, held_ref, back_ref, keep_ref, send_ref, all_ref):
        all_ref[...] = plus(held_ref[...], back_ref[...])
        split_rows(all_ref, (z_ref[0] >> 1) & 1, keep_ref, send_ref)

    outs = [((rows // 2, width), bf16)] * 2
    return run(kernel, "replicas_halve", outs, [((rows, width), bf16)], 2, (Scalar(z), held, back), small=True)


def replicas_sum(run, held, back):
    def kernel(held_ref, back_ref, out_ref):
        out_ref[...] = plus(held_ref[...], back_ref[...])

    return run(kernel, "replicas_sum", [(held.shape, bf16)], [], 1.7, (held, back), small=True)[0]


def replicas_join(run, z, own, other):
    rows, width = own.shape

    def kernel(z_ref, own_ref, other_ref, out_ref):
        join_rows(own_ref, other_ref, (z_ref[0] >> 1) & 1, out_ref)

    return run(kernel, "replicas_join", [((2 * rows, width), bf16)], [], 1.7, (Scalar(z), own, other), small=True)[0]


VECTOR_PARTS = ((CROSS, 5), (WORD_SELF, 5), (REGION_SELF, 5), (WORD_FEED, 7), (REGION_FEED, 7))


def shard_out(all_ref, share, refs):
    count = refs[0].shape[0]
    for m in range(count):
        refs[0][m] = all_ref[m * share : (m + 1) * share, :].astype(f32)
    if len(refs) > 1:
        vectors = all_ref[count * share : count * share + VECTOR_ROWS, :share].astype(f32)
        for ref, (start, number) in zip(refs[1:], VECTOR_PARTS):
            ref[...] = vectors[start : start + number]


def shard_shapes(kind, share, width):
    if kind == "feed":
        return [((2, share, width), f32)]
    outs = [((4, share, width), f32)]
    return outs + [((number, share), f32) for _, number in VECTOR_PARTS] if kind == "cross" else outs


def shard_of_sum(run, kind, share, summed):
    def kernel(all_ref, *refs):
        shard_out(all_ref, share, refs)

    return run(kernel, "shard", shard_shapes(kind, share, summed.shape[1]), [], 2.5, (summed,), small=True)


def shard_of_halves(run, kind, share, z, own, other):
    rows, width = own.shape

    def kernel(z_ref, own_ref, other_ref, *refs):
        all_ref = refs[-1]
        join_rows(own_ref, other_ref, z_ref[0] & 1, all_ref)
        shard_out(all_ref, share, refs[:-1])

    return run(kernel, "shard", shard_shapes(kind, share, width), [((2 * rows, width), bf16)], 2.5, (Scalar(z), own, other), small=True)


def block_bias(query_slots, key_slots, key_bias, blocks):
    items = key_bias.shape[0] // blocks
    rows = jnp.arange(items * query_slots) // query_slots
    cols = jnp.arange(items * key_slots) // key_slots
    same = rows[:, None] == cols[None, :]
    return jnp.where(same[None], key_bias.reshape(blocks, 1, items * key_slots), -1e30).astype(f32)


def exchange(value, step):
    def partner(i):
        if step == 0:
            return i ^ 1
        return i ^ (2 if (step == 1) == (i % 2 == 0) else 4)

    return lax.ppermute(value, "fsdp", [(i, partner(i)) for i in range(SLOTS)])


def replica_exchange(value, bit):
    return lax.ppermute(value, "dp", [(i, i ^ (1 << bit)) for i in range(4)])


class Gather:
    def __init__(self, run, *shards):
        self.run = run
        self.pieces = [shard.reshape(1, -1, shard.shape[-1]) for shard in shards]
        self.got = [exchange(p, 1) for p in self.pieces]

    def join(self, along):
        joined = join_pieces(self.run, list(zip(self.pieces, self.got)), along)
        self.pieces = joined[: len(self.pieces)]
        return joined[len(self.pieces) :]

    def step(self, *along):
        later = self.join(along)
        self.got = [exchange(p, 2) for p in self.pieces]
        return later

    def finish(self, *along):
        later = self.join(along)
        return [(p, exchange(p, 0)) for p in self.pieces], later


class Reduction:
    def __init__(self, run, kind, share, z, keep, send, by_exchange):
        self.run, self.kind, self.share, self.z, self.by_exchange = run, kind, share, z, by_exchange
        self.state = (keep, exchange(send, 0))

    def first(self):
        held, sent = add_halves(self.run, *self.state)
        self.state = (held, exchange(sent, 1))

    def second(self):
        held, sent = add_halves(self.run, *self.state)
        self.state = (held, exchange(sent, 2))

    def last(self):
        if not self.by_exchange:
            self.state = lax.psum(add_last(self.run, None, *self.state), "dp")
            return
        held, sent = add_last(self.run, self.z, *self.state)
        self.state = (held, replica_exchange(sent, 0))

    def halve(self):
        held, sent = replicas_halve(self.run, self.z, *self.state)
        self.state = (held, replica_exchange(sent, 1))

    def sum(self):
        own = replicas_sum(self.run, *self.state)
        self.state = (own, replica_exchange(own, 1))

    def join(self):
        own = replicas_join(self.run, self.z, *self.state)
        self.state = (own, replica_exchange(own, 0))

    def out(self):
        if self.by_exchange:
            return shard_of_halves(self.run, self.kind, self.share, self.z, *self.state)
        return shard_of_sum(self.run, self.kind, self.share, self.state)


def unswapped(keep, send, block, count):
    width, wide = block * SLOTS, keep.shape[1]
    rows = jnp.concatenate([keep, send]).reshape(SLOTS, -1, wide)
    matrices = rows[:, : count * block].reshape(SLOTS, count, block, wide).transpose(1, 0, 2, 3).reshape(count, width, wide)
    pieces = [lax.psum_scatter(matrices, "fsdp", scatter_dimension=1, tiled=True)]
    if rows.shape[1] > count * block:
        vectors = rows[:, count * block :, :block].transpose(1, 0, 2).reshape(VECTOR_ROWS, width)
        pieces.append(lax.psum_scatter(vectors, "fsdp", scatter_dimension=1, tiled=True))
    return [piece.astype(f32) for piece in lax.psum(pieces, "dp")]


def local(
    words_in, regions_in, word_mask, region_count,
    cross_matrices, cross_vectors, word_self_matrices, word_self_vectors,
    region_self_matrices, region_self_vectors, word_feed_matrices, word_feed_vectors,
    region_feed_matrices, region_feed_vectors, words_cotangent, regions_cotangent,
):
    items, words, width = words_in.shape
    regions = regions_in.shape[1]
    share = cross_matrices.shape[1]
    count = width // share
    blocks = 3 if items % 12 == 0 else 1
    swaps = count == SLOTS
    me = lax.axis_index("fsdp").astype(jnp.int32).reshape(1)
    z = lax.axis_index("dp").astype(jnp.int32).reshape(1)

    own = jnp.concatenate([cross_vectors, word_self_vectors, region_self_vectors, word_feed_vectors, region_feed_vectors], axis=0)
    def whole(shard):
        return lax.all_gather(shard, "fsdp", axis=1, tiled=True)

    run = Sequence()

    word_bias = (word_mask.astype(f32) - 1.0) * 10000.0
    region_bias = jnp.where(jnp.arange(regions)[None, :] < region_count[:, None], 0.0, negative).astype(f32)
    word_rows = words_in.reshape(-1, width)
    region_rows = regions_in.reshape(-1, width)
    wr = block_bias(words, regions, region_bias, blocks)
    rw = block_bias(regions, words, word_bias, blocks)
    ww = block_bias(words, words, word_bias, blocks)
    rr = block_bias(regions, regions, region_bias, blocks)

    block = width // SLOTS
    word_cot = words_cotangent.reshape(-1, width)
    region_cot = regions_cotangent.reshape(-1, width)
    if swaps:
        own = jnp.pad(own, ((0, VECTOR_ROWS - own.shape[0]), (0, 128 - share)))
        cross_gather = Gather(run, cross_matrices, own)
        region_gather = Gather(run, region_self_matrices)
        cross_gather.step()
        region_gather.step()
        run.after(wr, rw, ww, rr, word_rows, region_rows, word_cot, region_cot)
        (cross, vector_parts), (region_feed_shard,) = cross_gather.finish(region_feed_matrices)
        region_feed = whole(region_feed_shard)
        vectors = own
    else:
        own = jnp.pad(own, ((0, VECTOR_ROWS - own.shape[0]), (0, 0)))
        vectors, vector_parts = lax.all_gather(own, "fsdp", axis=1, tiled=True), ()
        cross, region_self, word_self = ((whole(w),) for w in (cross_matrices, region_self_matrices, word_self_matrices))
        region_feed, word_feed = whole(region_feed_matrices), whole(word_feed_matrices)

    def reduction(kind, keep, send, by_exchange):
        return Reduction(run, kind, share, z, keep, send, by_exchange and lax.axis_size("dp") == 4) if swaps else None

    def step(group, name):
        return getattr(group, name)() if swaps else None

    word_one, region_one, word_kept, region_kept, vectors = cross_forward(run, me, word_rows, region_rows, cross, vectors, vector_parts, wr, rw)
    if swaps:
        ((region_self,), (word_shard, word_feed_shard)) = region_gather.finish(word_self_matrices, word_feed_matrices)
        word_feed = whole(word_feed_shard)
        word_gather = Gather(run, word_shard)
    region_two, region_self_kept = self_forward(run, REGION_SELF, me, region_one, region_self, vectors, rr)

    if swaps:
        word_gather.step()
    run.between = False
    regions_out, region_dtwo, keep_rf, send_rf, dvec_a = feed_both(
        run, REGION_SELF, REGION_FEED, swaps, me, region_two, region_cot, region_feed, vectors
    )
    if swaps:
        ((word_self,), _) = word_gather.finish()
    rf = reduction("feed", keep_rf, send_rf, False)
    region_done, keep_rs, send_rs, dvec_b = self_backward(
        run, REGION_SELF, blocks, swaps, me, region_dtwo, region_one, region_self, vectors, region_self_kept
    )
    rs = reduction("self", keep_rs, send_rs, True)
    step(rf, "first")
    word_two, word_self_kept = self_forward(run, WORD_SELF, me, word_one, word_self, vectors, ww)
    words_out, word_dtwo, keep_wf, send_wf, dvec_c = feed_both(
        run, WORD_SELF, WORD_FEED, swaps, me, word_two, word_cot, word_feed, vectors
    )
    wf = reduction("feed", keep_wf, send_wf, True)
    step(rs, "first")
    step(rf, "second")
    step(wf, "first")
    region_grads = region_side(run, blocks, me, region_done, cross, region_kept)
    step(rf, "last")
    step(rs, "second")
    word_done, keep_ws, send_ws, dvec_d = self_backward(
        run, WORD_SELF, blocks, swaps, me, word_dtwo, word_one, word_self, vectors, word_self_kept
    )
    ws = reduction("self", keep_ws, send_ws, True)
    step(wf, "second")
    step(rs, "last")
    words_grad, regions_grad, keep_cr, send_cr = cross_backward(
        run, blocks, swaps, me, word_done, region_done, word_rows, region_rows, cross,
        (dvec_a, dvec_b, dvec_c, dvec_d), word_kept, region_kept[4], region_grads,
    )
    run.between = True
    cr = reduction("cross", keep_cr, send_cr, True)

    if swaps:
        (held, sent), (own, other), (kept, far) = add_three(run, z, ws.state, wf.state, rs.state)
        ws.state = (held, exchange(sent, 1))
        wf.state = (own, replica_exchange(other, 0))
        rs.state = (kept, replica_exchange(far, 1))
        cr.first()
        ws.second()
        wf.halve()
        rs.sum()
        (grad_rf,) = rf.out()
        cr.second()
        words_grad, regions_grad, _ = lax.optimization_barrier((words_grad, regions_grad, run.token))
        ws.last()
        wf.sum()
        rs.join()
        cr.last()
        ws.halve()
        wf.join()
        (grad_rs,) = rs.out()
        cr.halve()
        ws.sum()
        (grad_wf,) = wf.out()
        cr.sum()
        ws.join()
        cr.join()
        (grad_ws,) = ws.out()
        grad_cr, *vector_grads = cr.out()
    else:
        (grad_rf,), (grad_wf,) = unswapped(keep_rf, send_rf, block, 2), unswapped(keep_wf, send_wf, block, 2)
        (grad_rs,), (grad_ws,) = unswapped(keep_rs, send_rs, block, 4), unswapped(keep_ws, send_ws, block, 4)
        grad_cr, vector_sum = unswapped(keep_cr, send_cr, block, 4)
        vector_grads = [vector_sum[start : start + number] for start, number in VECTOR_PARTS]

    return (
        words_out.reshape(items, words, width),
        regions_out.reshape(items, regions, width),
        words_grad.reshape(items, words, width),
        regions_grad.reshape(items, regions, width),
        grad_cr,
        vector_grads[0],
        grad_ws,
        vector_grads[1],
        grad_rs,
        vector_grads[2],
        grad_wf,
        vector_grads[3],
        grad_rf,
        vector_grads[4],
    )


def solution(mesh):
    items = P(("dp", "fsdp"), None, None)
    matrix = P(None, "fsdp", None)
    vector = P(None, "fsdp")
    weights = (matrix, vector) * 5
    return jax.shard_map(
        local,
        mesh=mesh,
        in_specs=(items, items, P(("dp", "fsdp"), None), P(("dp", "fsdp")), *weights, items, items),
        out_specs=(items,) * 4 + weights,
        check_vma=False,
    )
```
